32 devices in a mesh: dp: 8 (over y, x, core), hid: 4 (over z).
Axes of the slice: x: 2, y: 2, z: 4, core: 2. Of those that a mesh axis runs over, the one named last changes fastest.
Arguments:
- tokens: bfloat16 [32, 1024, 512], P('dp', None, 'hid'), may hold values from -6 to 6
- seq_count: int32 [8], P('dp'), may hold values from 1 to 4, as said below
- out_grad: bfloat16 [32, 1024, 512], P('dp', None, 'hid'), may hold values from -6 to 6
- norm_params: float32 [4, 512], P(None, 'hid'), may hold values from -1.2 to 1.7
- norm_first: float32 [4, 512], P(None, 'hid'), may hold values from -0.0014648438 to 0.0014648438
- norm_second: float32 [4, 512], P(None, 'hid'), may hold values from 4.7218652e-08 to 1.8898677e-07
- controller_weight: float32 [512, 8], P('hid'), may hold values from -0.125 to 0.125
- router_first: float32 [512, 8], P('hid'), may hold values from -0.0029296875 to 0.0029296875
- router_second: float32 [512, 8], P('hid'), may hold values from 1.7108836e-07 to 6.8271623e-07
- attn_in: float32 [512, 3, 512], P('dp', None, 'hid'), may hold values from -0.25 to 0.25
- attn_in_first: float32 [512, 3, 512], P('dp', None, 'hid'), may hold values from -0.00036621094 to 0.00036621094
- attn_in_second: float32 [512, 3, 512], P('dp', None, 'hid'), may hold values from 2.9497638e-09 to 1.1776624e-08
- attn_in_average: float32 [512, 3, 512], P('dp', None, 'hid'), may hold values from -0.25 to 0.25
- attn_out: float32 [512, 512], P('dp', 'hid'), may hold values from -1 to 1
- attn_out_first: float32 [512, 512], P('dp', 'hid'), may hold values from -0.00036621094 to 0.00036621094
- attn_out_second: float32 [512, 512], P('dp', 'hid'), may hold values from 2.9497638e-09 to 1.1776624e-08
- attn_out_average: float32 [512, 512], P('dp', 'hid'), may hold values from -1 to 1
- expert_in: float32 [8, 512, 2048], P('dp', None, 'hid'), may hold values from -3.375 to 3.375
- expert_in_first: float32 [8, 512, 2048], P('dp', None, 'hid'), may hold values from -1.5258789e-05 to 1.5258789e-05
- expert_in_second: float32 [8, 512, 2048], P('dp', None, 'hid'), may hold values from 4.348837e-12 to 1.7395347e-11
- expert_in_average: float32 [8, 512, 2048], P('dp', None, 'hid'), may hold values from -1.5 to 1.5
- expert_out: float32 [8, 2048, 512], P('dp', 'hid'), may hold values from -0.125 to 0.125
- expert_out_first: float32 [8, 2048, 512], P('dp', 'hid'), may hold values from -0.00036621094 to 0.00036621094
- expert_out_second: float32 [8, 2048, 512], P('dp', 'hid'), may hold values from 2.9497638e-09 to 1.1776624e-08
- expert_out_average: float32 [8, 2048, 512], P('dp', 'hid'), may hold values from -0.125 to 0.125
Outputs:
- block_out: bfloat16 [32, 1024, 512], P('dp', None, 'hid')
- tokens_grad: float32 [32, 1024, 512], P('dp', None, 'hid')
- grad_norm: float32 [], replicated
- norm_first_new: float32 [4, 512], P(None, 'hid')
- norm_second_new: float32 [4, 512], P(None, 'hid')
- norm_params_new: float32 [4, 512], P(None, 'hid')
- router_first_new: float32 [512, 8], P('hid')
- router_second_new: float32 [512, 8], P('hid')
- router_new: float32 [512, 8], P('hid')
- attn_in_first_new: float32 [512, 3, 512], P('dp', None, 'hid')
- attn_in_second_new: float32 [512, 3, 512], P('dp', None, 'hid')
- attn_in_new: float32 [512, 3, 512], P('dp', None, 'hid')
- attn_in_average_new: float32 [512, 3, 512], P('dp', None, 'hid')
- attn_out_first_new: float32 [512, 512], P('dp', 'hid')
- attn_out_second_new: float32 [512, 512], P('dp', 'hid')
- attn_out_new: float32 [512, 512], P('dp', 'hid')
- attn_out_average_new: float32 [512, 512], P('dp', 'hid')
- expert_in_first_new: float32 [8, 512, 2048], P('dp', None, 'hid')
- expert_in_second_new: float32 [8, 512, 2048], P('dp', None, 'hid')
- expert_in_new: float32 [8, 512, 2048], P('dp', None, 'hid')
- expert_in_average_new: float32 [8, 512, 2048], P('dp', None, 'hid')
- expert_out_first_new: float32 [8, 2048, 512], P('dp', 'hid')
- expert_out_second_new: float32 [8, 2048, 512], P('dp', 'hid')
- expert_out_new: float32 [8, 2048, 512], P('dp', 'hid')
- expert_out_average_new: float32 [8, 2048, 512], P('dp', 'hid')
The draws below stay inside these ranges and needn't reach their ends.
Inputs may be any that keep to these rules, and one draw needn't show every extreme that they name: `seq_count`: each dp index's live sequences fill its first slots; some index has all 4 slots live and some index only one.
All inputs are finite; a program needn't handle non-finite values.
Results may differ from the reference program's by a relative error of at most 0.023.
The reference program's roundings to bfloat16 on the way count: a program that leaves them out, or rounds other values in their place, can miss the bound.
Values may be sent and summed in bfloat16 or wider, within the bound.
A program may use at most 256 MiB of HBM per device.

```python
import math
from functools import partial
import jax
import jax.numpy as jnp
from jax import lax

D = 512
HEADS = 8
HS = 64
H = 2048
GROUP = 32
L = 1024
SLOTS = 4
STEP = 10
EXPERTS = 8
SEQS = 32
PARAMS = 17831936
N_DP = 8


def draw_tokens(key, part):
    key = jax.random.fold_in(key, 5)
    value_key = jax.random.fold_in(key, 0)
    values = jnp.clip(jax.random.normal(value_key, (SEQS, L, D), jnp.float32), -6.0, 6.0)
    return values.astype(jnp.bfloat16)


def draw_seq_count(key, part):
    key = jax.random.fold_in(key, 11)
    count_key, order_key = jax.random.split(key)
    counts = jax.random.randint(count_key, (N_DP,), 1, SLOTS + 1)
    order = jax.random.permutation(order_key, N_DP)
    counts = counts.at[order[0]].set(SLOTS)
    counts = counts.at[order[1]].set(1)
    return counts.astype(jnp.int32)


def ramp_gains(key, low_end, rise):
    ramp = jnp.arange(D, dtype=jnp.float32) / (D - 1)
    jitter = jax.random.uniform(key, (2, D), jnp.float32, 0.9, 1.1)
    return (low_end + rise * ramp)[None, :] * jitter


def draw_norm_params(key, part):
    key = jax.random.fold_in(key, 23)
    gain_key, bias_key = jax.random.split(key)
    gains = ramp_gains(gain_key, 0.6, 0.8)
    biases = jnp.clip(0.2 * jax.random.normal(bias_key, (2, D), jnp.float32), -1.2, 1.2)
    return jnp.stack([gains[0], biases[0], gains[1], biases[1]], 0).astype(jnp.float32)


def rising_entries(key, rise):
    entries = jnp.clip(jax.random.normal(key, (EXPERTS, D, H), jnp.float32), -6.0, 6.0) * (D // GROUP) ** (-0.5)
    by_expert = jnp.sqrt(1.0 + rise * jnp.arange(EXPERTS, dtype=jnp.float32) / max(EXPERTS - 1, 1))
    by_unit = jnp.sqrt(1.0 + rise * jnp.arange(H, dtype=jnp.float32) / (H - 1))
    values = entries * by_expert[:, None, None] * by_unit[None, None, :]
    limit = 13.5 * (D // GROUP) ** (-0.5)
    return jnp.clip(values, -limit, limit)


def draw_expert_in(key, part):
    key = jax.random.fold_in(key, 37)
    values = rising_entries(key, 2.0)
    return values.astype(jnp.float32)


def levels(rng, extent, cuts, smallest, largest):
    level, own = 1.0, jax.random.fold_in(rng, 6)
    for dim, parts in cuts:
        draws = jnp.exp(jax.random.uniform(jax.random.fold_in(own, dim), (parts,), jnp.float32, smallest / len(cuts), largest / len(cuts)))
        level = level * jnp.repeat(draws, extent[dim] // parts).reshape([-1 if axis == dim else 1 for axis in range(len(extent))])
    return level


def scatter_about(rng, shape, scale, most, cuts=(), held_as=jnp.bfloat16):
    values = jax.random.normal(rng, shape, jnp.float32) * scale
    if len(cuts) > 0:
        values = levels(rng, shape, cuts, -0.22, 0.18) * values
    return jnp.clip(values, min=-most, max=most).astype(held_as)


def setup_inputs(seed: int = 0) -> dict:
    key_of = jax.random.split(jax.random.key(seed), 26)
    return {
        "tokens": draw_tokens(jax.random.fold_in(key_of[25], 71), 0),
        "seq_count": draw_seq_count(jax.random.fold_in(key_of[25], 71), 0),
        "out_grad": scatter_about(key_of[2], (SEQS, L, D), 1.0, 6.0, ((0, 8), (2, 4))),
        "norm_params": draw_norm_params(jax.random.fold_in(key_of[25], 71), 0),
        "norm_first": scatter_about(key_of[4], (4, D), (0.444 * PARAMS ** -0.5), 0.0014648438, ((1, 4),), jnp.float32),
        "norm_second": jnp.clip(jnp.exp(math.log(1.8898677467404923e-07) - 1.386888 * jax.random.uniform(key_of[5], (4, D), jnp.float32) ** levels(key_of[5], (4, D), ((1, 4),), -0.2, 0.2)), 4.7218652099445535e-08, 1.8898677467404923e-07),
        "controller_weight": scatter_about(key_of[6], (D, EXPERTS), (4 * D) ** -0.5, 0.125, ((0, 4),), jnp.float32),
        "router_first": scatter_about(key_of[7], (D, EXPERTS), (0.07 * (0.216 * D * HEADS * HS + EXPERTS * D * H // (4 * GROUP)) ** -0.5), 0.0029296875, ((0, 4),), jnp.float32),
        "router_second": jnp.clip(jnp.exp(math.log(6.827162337685877e-07) - 1.3838992 * jax.random.uniform(key_of[8], (D, EXPERTS), jnp.float32) ** levels(key_of[8], (D, EXPERTS), ((0, 4),), -0.2, 0.2)), 1.7108835947965417e-07, 6.827162337685877e-07),
        "attn_in": scatter_about(key_of[9], (D, 3, HEADS * HS), D ** -0.5, 0.25, ((0, 8), (2, 4)), jnp.float32),
        "attn_in_first": scatter_about(key_of[10], (D, 3, HEADS * HS), (0.111 * PARAMS ** -0.5), 0.00036621094, ((0, 8), (2, 4)), jnp.float32),
        "attn_in_second": jnp.clip(jnp.exp(math.log(1.177662412032987e-08) - 1.38439147 * jax.random.uniform(key_of[11], (D, 3, HEADS * HS), jnp.float32) ** levels(key_of[11], (D, 3, HEADS * HS), ((0, 8), (2, 4)), -0.2, 0.2)), 2.9497637665798493e-09, 1.177662412032987e-08),
        "attn_in_average": scatter_about(key_of[12], (D, 3, HEADS * HS), D ** -0.5, 0.25, ((0, 8), (2, 4)), jnp.float32),
        "attn_out": scatter_about(key_of[13], (D, HEADS * HS), (HEADS * HS // 16) ** -0.5, 1.0, ((0, 8), (1, 4)), jnp.float32),
        "attn_out_first": scatter_about(key_of[14], (D, HEADS * HS), (0.111 * PARAMS ** -0.5), 0.00036621094, ((0, 8), (1, 4)), jnp.float32),
        "attn_out_second": jnp.clip(jnp.exp(math.log(1.177662412032987e-08) - 1.38439147 * jax.random.uniform(key_of[15], (D, HEADS * HS), jnp.float32) ** levels(key_of[15], (D, HEADS * HS), ((0, 8), (1, 4)), -0.2, 0.2)), 2.9497637665798493e-09, 1.177662412032987e-08),
        "attn_out_average": scatter_about(key_of[16], (D, HEADS * HS), (HEADS * HS // 16) ** -0.5, 1.0, ((0, 8), (1, 4)), jnp.float32),
        "expert_in": draw_expert_in(jax.random.fold_in(key_of[25], 71), 0),
        "expert_in_first": scatter_about(key_of[18], (EXPERTS, D, H), (0.002 * GROUP ** -0.5 * (0.216 * D * HEADS * HS + EXPERTS * D * H // (4 * GROUP)) ** -0.5), 1.52587890625e-05, ((0, 8), (2, 4)), jnp.float32),
        "expert_in_second": jnp.clip(jnp.exp(math.log(1.7395347315374288e-11) - 1.3862944 * jax.random.uniform(key_of[19], (EXPERTS, D, H), jnp.float32) ** levels(key_of[19], (EXPERTS, D, H), ((0, 8), (2, 4)), -0.2, 0.2)), 4.348836828843572e-12, 1.7395347315374288e-11),
        "expert_in_average": scatter_about(key_of[20], (EXPERTS, D, H), (D // GROUP) ** -0.5, 1.5, ((0, 8), (2, 4)), jnp.float32),
        "expert_out": scatter_about(key_of[21], (EXPERTS, H, D), H ** -0.5, 0.125, ((0, 8), (1, 4)), jnp.float32),
        "expert_out_first": scatter_about(key_of[22], (EXPERTS, H, D), (0.111 * PARAMS ** -0.5), 0.00036621094, ((0, 8), (1, 4)), jnp.float32),
        "expert_out_second": jnp.clip(jnp.exp(math.log(1.177662412032987e-08) - 1.38439147 * jax.random.uniform(key_of[23], (EXPERTS, H, D), jnp.float32) ** levels(key_of[23], (EXPERTS, H, D), ((0, 8), (1, 4)), -0.2, 0.2)), 2.9497637665798493e-09, 1.177662412032987e-08),
        "expert_out_average": scatter_about(key_of[24], (EXPERTS, H, D), H ** -0.5, 0.125, ((0, 8), (1, 4)), jnp.float32),
    }


precise_setting = lax.Precision.HIGHEST
norm_epsilon = 1e-05
fill_value = -1e+30
clip_limit = 1.0
beta_first = 0.9
beta_second = 0.95
adam_epsilon = 1e-08
weight_decay = 0.1

@jax.custom_vjp
def low(v):
    return lax.optimization_barrier(v.astype(jnp.bfloat16)).astype(jnp.float32)

@jax.custom_vjp
def low_back(v):
    return v

def low_keep(v):
    return (low(v), None)

def low_pass(kept, grad):
    return (grad,)

def back_keep(v):
    return (v, None)

def back_low(kept, grad):
    return (low(grad),)
low.defvjp(low_keep, low_pass)
low_back.defvjp(back_keep, back_low)

def norm_rows(values, gain, bias):
    center = lax.optimization_barrier(jnp.mean(values, axis=-1, keepdims=True))
    deviation = values - center
    spread = lax.optimization_barrier(jnp.mean(deviation * deviation, axis=-1, keepdims=True))
    return deviation * lax.rsqrt(spread + norm_epsilon) * gain + bias

def attend_sequence(a_seq, qkv_low, out_low):
    seq_len = a_seq.shape[0]
    proj = jnp.einsum('ld,dcf->lcf', a_seq, qkv_low, precision=precise_setting)
    proj = low(low_back(proj))
    query = proj[:, 0].reshape(seq_len, HEADS, HS)
    key_rows = proj[:, 1].reshape(seq_len, HEADS, HS)
    value_rows = proj[:, 2].reshape(seq_len, HEADS, HS)
    scores = jnp.einsum('qhe,khe->hqk', query, key_rows, precision=precise_setting) * HS ** (-0.5)
    scores = low_back(scores)
    positions = jnp.arange(seq_len)
    causal = positions[None, :] <= positions[:, None]
    probs = jax.nn.softmax(jnp.where(causal[None], scores, fill_value), axis=-1)
    probs = low(probs)
    heads_out = jnp.einsum('hqk,khe->qhe', probs, value_rows, precision=precise_setting).reshape(seq_len, HEADS * HS)
    heads_out = low(low_back(heads_out))
    return low_back(jnp.einsum('lf,df->ld', heads_out, out_low, precision=precise_setting))

def expert_apply(packed):
    rows_in, weight_in, weight_out = packed
    pre_act = low_back(jnp.dot(rows_in, weight_in, precision=precise_setting))
    act_low = low(jax.nn.gelu(pre_act))
    return low_back(jnp.dot(act_low, weight_out, precision=precise_setting))

def forward(inputs, norm_params, controller_weight, attn_in, attn_out, expert_in, expert_out, live_slot):
    group_len = GROUP // SLOTS
    groups = L // group_len
    normed_in = low(norm_rows(inputs, norm_params[0], norm_params[1]))
    attend = jax.checkpoint(partial(attend_sequence, qkv_low=low(attn_in), out_low=low(attn_out)))
    attn = lax.map(attend, normed_in)
    hidden_one = inputs + attn
    dispatched_input = norm_rows(hidden_one, norm_params[2], norm_params[3])
    router_scores = jnp.einsum('nbc,cx->nbx', dispatched_input, controller_weight, precision=precise_setting)
    live_five = live_slot.reshape(N_DP, SLOTS, 1, 1, 1)
    masked = jnp.where(live_five, router_scores.reshape(N_DP, SLOTS, groups, group_len, EXPERTS), fill_value)
    group_peak = lax.optimization_barrier(jnp.max(masked, axis=(1, 3), keepdims=True))
    exp_logits = jnp.exp(masked - group_peak)
    gates = exp_logits / lax.optimization_barrier(jnp.sum(exp_logits, axis=(1, 3), keepdims=True))
    routed_five = dispatched_input.reshape(N_DP, SLOTS, groups, group_len, D)
    mixed = low(jnp.einsum('nsgpe,nsgpd->nged', gates, routed_five, precision=precise_setting))
    rows_all = jnp.transpose(mixed, (2, 0, 1, 3)).reshape(EXPERTS, N_DP * groups, D)
    expert_rows = lax.map(jax.checkpoint(expert_apply), (rows_all, low(expert_in), low(expert_out)))
    expert_rows = jnp.transpose(expert_rows.reshape(EXPERTS, N_DP, groups, D), (1, 2, 0, 3))
    spread_back = jnp.einsum('nsgpe,nged->nsgpd', gates, expert_rows, precision=precise_setting).reshape(SEQS, L, D)
    return jnp.where(live_slot.reshape(SEQS, 1, 1), hidden_one + spread_back, 0.0)

def adam_update(weight, grad, first, second, rate, factor):
    clipped = grad * factor
    first_new = beta_first * first + (1.0 - beta_first) * clipped
    second_new = beta_second * second + (1.0 - beta_second) * clipped * clipped
    first_hat = first_new / (1.0 - beta_first ** STEP)
    second_hat = second_new / (1.0 - beta_second ** STEP)
    weight_new = weight - rate * (first_hat / (jnp.sqrt(second_hat) + adam_epsilon) + weight_decay * weight)
    return (first_new, second_new, weight_new)

def reference(tokens, seq_count, out_grad, norm_params, norm_first, norm_second, controller_weight, router_first, router_second, attn_in, attn_in_first, attn_in_second, attn_in_average, attn_out, attn_out_first, attn_out_second, attn_out_average, expert_in, expert_in_first, expert_in_second, expert_in_average, expert_out, expert_out_first, expert_out_second, expert_out_average):
    ema_keep = (1.0 + STEP) / (10.0 + STEP)
    live_slot = jnp.arange(SLOTS, dtype=jnp.int32)[None, :] < seq_count[:, None]
    inputs = tokens.astype(jnp.float32)
    result, pull = jax.vjp(partial(forward, live_slot=live_slot), inputs, norm_params, controller_weight, attn_in, attn_out, expert_in, expert_out)
    grads = pull(out_grad.astype(jnp.float32))
    squares = jnp.sum(grads[1] * grads[1])
    for grad in grads[2:]:
        squares = squares + jnp.sum(grad * grad)
    grad_norm = jnp.sqrt(squares)
    factor = jnp.minimum(1.0, clip_limit / grad_norm)
    norm_up = adam_update(norm_params, grads[1], norm_first, norm_second, 0.6, factor)
    router_up = adam_update(controller_weight, grads[2], router_first, router_second, (4 * D) ** (-0.5), factor)
    attn_in_up = adam_update(attn_in, grads[3], attn_in_first, attn_in_second, 0.5 * D ** (-0.5), factor)
    attn_out_up = adam_update(attn_out, grads[4], attn_out_first, attn_out_second, 0.5 * (HEADS * HS // 16) ** (-0.5), factor)
    expert_in_up = adam_update(expert_in, grads[5], expert_in_first, expert_in_second, 2.5 * (D // GROUP) ** (-0.5), factor)
    expert_out_up = adam_update(expert_out, grads[6], expert_out_first, expert_out_second, 0.5 * H ** (-0.5), factor)
    return (result.astype(jnp.bfloat16), grads[0], grad_norm, norm_up[0], norm_up[1], norm_up[2], router_up[0], router_up[1], router_up[2], attn_in_up[0], attn_in_up[1], attn_in_up[2], ema_keep * attn_in_average + (1.0 - ema_keep) * attn_in_up[2], attn_out_up[0], attn_out_up[1], attn_out_up[2], ema_keep * attn_out_average + (1.0 - ema_keep) * attn_out_up[2], expert_in_up[0], expert_in_up[1], expert_in_up[2], ema_keep * expert_in_average + (1.0 - ema_keep) * expert_in_up[2], expert_out_up[0], expert_out_up[1], expert_out_up[2], ema_keep * expert_out_average + (1.0 - ema_keep) * expert_out_up[2])
```

```python
import functools

import jax
import jax.numpy as jnp
from jax import lax
from jax.experimental import pallas as pl
from jax.experimental.pallas import tpu as pltpu
from jax.sharding import PartitionSpec as P

D = 512
HEADS = 8
HS = 64
H = 2048
GROUP = 32
STEP = 10
BLK = 256
FS = 128
GB = 16

norm_epsilon = 1e-05
fill_value = -1e30
clip_limit = 1.0
beta_first = 0.9
beta_second = 0.95
adam_epsilon = 1e-08
weight_decay = 0.1

f32 = jnp.float32
bf16 = jnp.bfloat16
MESH = pl.DeviceIdType.MESH
EXACT = lax.Precision.HIGHEST
VM = pl.BlockSpec(memory_space=pltpu.VMEM)
HB = pl.BlockSpec(memory_space=pl.ANY)
SM = pl.BlockSpec(memory_space=pltpu.SMEM)
DMA = pltpu.SemaphoreType.DMA


def dot(a, b, precision=None):
    return lax.dot_general(
        a, b, (((1,), (0,)), ((), ())), precision=precision, preferred_element_type=f32
    )


def dot_last(a, b, precision=None):
    return lax.dot_general(
        a, b, (((1,), (1,)), ((), ())), precision=precision, preferred_element_type=f32
    )


def dot_first(a, b, precision=None):
    return lax.dot_general(
        a, b, (((0,), (0,)), ((), ())), precision=precision, preferred_element_type=f32
    )


def greet(peers):
    barrier = pltpu.get_barrier_semaphore()
    for peer in peers:
        pl.semaphore_signal(barrier, inc=1, device_id=peer, device_id_type=MESH)
    pl.semaphore_wait(barrier, len(peers))


def remote(src, dst, send, recv, peer):
    return pltpu.make_async_remote_copy(
        src_ref=src, dst_ref=dst, send_sem=send, recv_sem=recv, device_id=peer, device_id_type=MESH
    )


def lanes(ref_like, index):
    return pl.ds(pl.multiple_of(index * ref_like, ref_like), ref_like)


def features(ref, rows):
    return jnp.concatenate([ref[f, rows, :] for f in range(ref.shape[0])], axis=1)


def row_of(ref, row):
    return jnp.concatenate([ref[f, row : row + 1, :] for f in range(ref.shape[0])], axis=1)


def standardize(v):
    center = jnp.sum(v, -1, keepdims=True) / v.shape[-1]
    dev = v - center
    inv = lax.rsqrt(jnp.sum(dev * dev, -1, keepdims=True) / v.shape[-1] + norm_epsilon)
    return dev * inv, center, inv


def head_masks(rows):
    lane = lax.broadcasted_iota(jnp.int32, (rows, FS), 1)
    return lane < HS


def project_kernel(
    nd, nh, tok, wblk, pblk, x, w, p, a1, qkv, tss, tsr, wss, wsr, dss, dsr, css, csr, pss, psr, loc
):
    n = lax.axis_index("dp")
    h = lax.axis_index("hid")
    core = lax.rem(n, 2)
    chip = lax.div(n, 2)
    chips = nd // 2
    seq = tok.shape[1]
    zpeer = [{"hid": lax.rem(h + k, nh)} for k in range(1, nh)]
    cpeer = [{"dp": lax.rem(chip + k, chips) * 2 + core} for k in range(1, chips)]
    partner = {"dp": chip * 2 + 1 - core}
    greet(zpeer + cpeer + [partner])
    locals_ = [
        pltpu.make_async_copy(wblk, w.at[h, chip, core], loc.at[0]),
        pltpu.make_async_copy(pblk, p.at[h], loc.at[1]),
        pltpu.make_async_copy(tok.at[h], x.at[h], loc.at[2]),
    ]
    for c in locals_:
        c.start()
    wz = [
        remote(wblk, w.at[h, chip, core], wss.at[k], wsr.at[k], zpeer[k]) for k in range(nh - 1)
    ]
    pz = [remote(pblk, p.at[h], pss.at[k], psr.at[k], zpeer[k]) for k in range(nh - 1)]
    for c in wz + pz:
        c.start()
    tz = []
    for b in range(seq // BLK):
        rows = pl.ds(b * BLK, BLK)
        for k in range(nh - 1):
            c = remote(
                tok.at[lax.rem(h + k + 1, nh), rows],
                x.at[h, rows],
                tss.at[b, k],
                tsr.at[b, k],
                zpeer[k],
            )
            c.start()
            tz.append(c)
    for c in locals_:
        c.wait()
    for c in wz:
        c.wait_recv()
    wc = [
        remote(w.at[:, chip, core], w.at[:, chip, core], dss.at[k], dsr.at[k], cpeer[k])
        for k in range(chips - 1)
    ]
    for c in wc:
        c.start()
    for c in pz + wc:
        c.wait_recv()
    for c in wz + wc:
        c.wait_send()
    wp = remote(w.at[:, :, core], w.at[:, :, core], css.at[0], csr.at[0], partner)
    wp.start()
    gain = row_of(p, 0)
    bias = row_of(p, 1)
    for b in range(seq // BLK):
        rows = pl.ds(b * BLK, BLK)
        for k in range(nh - 1):
            tz[b * (nh - 1) + k].wait_recv()
        normed, _, _ = standardize(features(x, rows).astype(f32))
        a1[rows, :] = (normed * gain + bias).astype(bf16)
        if b == 0:
            wp.wait_recv()
    lane = lax.broadcasted_iota(jnp.int32, (BLK, 3 * FS), 1)
    scale = jnp.where(lane < FS, HS**-0.5, 1.0).astype(bf16)

    def heads(hp, carry):
        wq = w[hp].reshape(D, D)[:, : 3 * FS]
        for b in range(seq // BLK):
            rows = pl.ds(b * BLK, BLK)
            qkv[hp, rows, :] = dot(a1[rows, :], wq).astype(bf16) * scale
        return carry

    lax.fori_loop(0, nh, heads, 0)
    for c in pz + tz + [wp]:
        c.wait_send()


def controller_rows(p, pad, experts):
    pad[...] = jnp.zeros_like(pad)
    for f in range(p.shape[0]):
        pad[0:experts, f * FS : (f + 1) * FS] = p[f, 8 : 8 + experts, :]


def attend_kernel(
    nh, experts, x, w, p, qkv, heads, lse, h1, h1f, stf, h1b, st, pad, hss, hsr, sss, ssr, loc
):
    h = lax.axis_index("hid")
    seq = x.shape[1]
    zpeer = [{"hid": lax.rem(h + k, nh)} for k in range(1, nh)]
    greet(zpeer)
    controller_rows(p, pad, experts)
    gain = row_of(p, 2)
    bias = row_of(p, 3)
    low_half = head_masks(BLK)
    lane = lax.broadcasted_iota(jnp.int32, (BLK, FS), 1)
    causal = lax.broadcasted_iota(jnp.int32, (BLK, BLK), 1) <= lax.broadcasted_iota(
        jnp.int32, (BLK, BLK), 0
    )
    lse[...] = jnp.zeros_like(lse)
    sends = []
    for b in range(seq // BLK):
        rows = pl.ds(b * BLK, BLK)
        past = b * BLK

        def pair(hp, carry):
            q = qkv[hp, rows, 0:FS]
            outs = []
            lses = lse[rows, :]
            for half in range(2):
                mine = low_half if half == 0 else jnp.logical_not(low_half)
                qm = jnp.where(mine, q, jnp.zeros_like(q))
                s_now = dot_last(qm, qkv[hp, rows, FS : 2 * FS])
                s_now = jnp.where(causal, s_now, fill_value)
                peak = jnp.max(s_now, -1, keepdims=True)
                if b > 0:
                    s_past = dot_last(qm, qkv[hp, 0:past, FS : 2 * FS])
                    peak = jnp.maximum(peak, jnp.max(s_past, -1, keepdims=True))
                e_now = jnp.exp(s_now - peak)
                total = jnp.sum(e_now, -1, keepdims=True)
                if b > 0:
                    e_past = jnp.exp(s_past - peak)
                    total = total + jnp.sum(e_past, -1, keepdims=True)
                inv = 1.0 / total
                out = dot((e_now * inv).astype(bf16), qkv[hp, rows, 2 * FS :])
                if b > 0:
                    out = out + dot((e_past * inv).astype(bf16), qkv[hp, 0:past, 2 * FS :])
                outs.append(out)
                lses = jnp.where(lane == 2 * hp + half, peak + jnp.log(total), lses)
            lse[rows, :] = lses
            heads[hp, rows, :] = jnp.where(low_half, outs[0], outs[1]).astype(bf16)
            return carry

        lax.fori_loop(0, nh, pair, 0)
        attn = jnp.zeros((BLK, D), f32)
        for hp in range(nh):
            attn = attn + dot_last(heads[hp, rows, :], w[hp].reshape(D, D)[:, 3 * FS :])
        hidden = features(x, rows).astype(f32) + attn
        h1[rows, :] = hidden
        normed, center, inv = standardize(hidden)
        u = normed * gain + bias
        cols = dot_last(u, pad[...], EXACT)
        cols = jnp.where(lane == experts, center, jnp.where(lane == experts + 1, inv, cols))
        st[:, rows] = cols.T[0 : experts + 8, :]
        for f in range(nh):
            h1b[f, rows, :] = hidden[:, f * FS : (f + 1) * FS].astype(bf16)
        mine = [
            pltpu.make_async_copy(h1b.at[h, rows], h1f.at[h, rows], loc.at[b, 0]),
            pltpu.make_async_copy(st.at[:, rows], stf.at[h, :, rows], loc.at[b, 1]),
        ]
        for c in mine:
            c.start()
        for k in range(nh - 1):
            c = remote(
                h1b.at[lax.rem(h + k + 1, nh), rows],
                h1f.at[h, rows],
                hss.at[b, k],
                hsr.at[b, k],
                zpeer[k],
            )
            s = remote(
                st.at[:, rows], stf.at[h, :, rows], sss.at[b, k], ssr.at[b, k], zpeer[k]
            )
            c.start()
            s.start()
            sends += [c, s]
        sends += mine
    for c in sends:
        c.wait()


def expand(stb, experts, el):
    rows = lax.broadcasted_iota(jnp.int32, (experts + 8, el + 2 * FS), 0)
    cols = lax.broadcasted_iota(jnp.int32, (experts + 8, el + 2 * FS), 1)
    target = jnp.where(
        cols < el, lax.shift_right_logical(cols, 4), jnp.where(cols < el + FS, experts, experts + 1)
    )
    pick = (rows == target).astype(f32)
    return [dot_first(stb[s], pick, EXACT) for s in range(stb.shape[0])]


def own_group(tokens, el):
    token = lax.broadcasted_iota(jnp.int32, (tokens, el), 0)
    lane = lax.broadcasted_iota(jnp.int32, (tokens, el), 1)
    group = lax.shift_right_logical(token, 3) & (GB - 1)
    return (lane & (GB - 1)) == group


def block_values(h1f, og, p_gain, p_bias, live, rows, mean, inv):
    slots = h1f.shape[0]
    nhat, u, dy, hid = [], [], [], []
    for s in range(slots):
        hidden = h1f[s, rows, :].astype(f32)
        hat = (hidden - mean[s]) * inv[s]
        nhat.append(hat)
        u.append(hat * p_gain + p_bias)
        hid.append(hidden)
        dy.append(jnp.where(s < live, og[s, rows, :].astype(f32), 0.0))
    return nhat, u, dy, hid


def expert_kernel(
    nd, nh, experts, count, h1f, stf, og, npar, win, wout, gates, yin, g_in, g_out, sq,
    mout, xz, act, dpre, prs, rin, wi, wo,
    dss, dsr, zss, zsr, rss, rsr, yss, ysr, loc
):
    n = lax.axis_index("dp")
    h = lax.axis_index("hid")
    seq = h1f.shape[1]
    slots = h1f.shape[0]
    el = experts * GB
    span = GB * GROUP // slots
    zpeer = [{"hid": lax.rem(h + k, nh)} for k in range(1, nh)]
    dpeer = [{"dp": lax.rem(n + k, nd)} for k in range(1, nd)]
    greet(zpeer + dpeer)
    live = count[0]
    gain = npar[2:3, :]
    bias = npar[3:4, :]
    mask = own_group(slots * span, el)

    def gate_block(b, carry):
        rows = pl.ds(pl.multiple_of(b * span, span), span)
        grows = pl.ds(pl.multiple_of(b * GB, GB), GB)
        spread = expand(stf[:, :, rows], experts, el)
        logits = jnp.stack(
            [jnp.where(s < live, spread[s][:, :el], fill_value) for s in range(slots)]
        ).reshape(slots, GB, span // GB, el)
        peak = jnp.max(logits, axis=(0, 2), keepdims=True)
        e = jnp.exp(logits - peak)
        gate = e / jnp.sum(e, axis=(0, 2), keepdims=True)
        gate = jnp.where(mask, gate.reshape(slots * span, el), 0.0)
        gates[b] = gate
        mean = [v[:, el : el + FS] for v in spread]
        inv = [v[:, el + FS :] for v in spread]
        _, u, dy, _ = block_values(h1f, og, gain, bias, live, rows, mean, inv)
        both = jnp.concatenate([jnp.concatenate(u, 0), jnp.concatenate(dy, 0)], 1)
        mixed = dot_first(gate, both, EXACT).astype(bf16)
        mout[:, 0, grows, :] = mixed[:, :FS].reshape(experts, GB, FS)
        mout[:, 1, grows, :] = mixed[:, FS:].reshape(experts, GB, FS)
        return carry

    lax.fori_loop(0, seq // span, gate_block, 0)

    def to_expert(k):
        e = lax.rem(n + k, nd)
        return remote(mout.at[e], xz.at[h, n], dss.at[k], dsr.at[k], {"dp": e})

    def to_feature(k, j):
        src = lax.rem(n - k + nd, nd)
        return remote(
            xz.at[h, src], xz.at[h, src], zss.at[k, j], zsr.at[k, j], {"hid": lax.rem(h + j + 1, nh)}
        )

    def to_sum(k, j):
        src = lax.rem(n - k + nd, nd)
        peer = lax.rem(h + j + 1, nh)
        return remote(
            prs.at[peer, src], rin.at[j, src], rss.at[k, j], rsr.at[k, j], {"hid": peer}
        )

    def to_home(k):
        src = lax.rem(n - k + nd, nd)
        return remote(prs.at[h, src], yin.at[n], yss.at[k], ysr.at[k], {"dp": src})

    own = pltpu.make_async_copy(mout.at[n], xz.at[h, n], loc.at[0])
    own.start()

    def start_expert(k, carry):
        to_expert(k).start()
        return carry

    lax.fori_loop(1, nd, start_expert, 0)
    wi[...] = win[...].astype(bf16)
    wo[...] = wout[...].astype(bf16)
    own.wait()
    for j in range(nh - 1):
        to_feature(0, j).start()

    def forward(k, carry):
        to_expert(k).wait_recv()
        for j in range(nh - 1):
            to_feature(k, j).start()
        return carry

    lax.fori_loop(1, nd, forward, 0)

    def expert(k, carry):
        src = lax.rem(n - k + nd, nd)
        for j in range(nh - 1):
            to_feature(k, j).wait_recv()
        mixed = jnp.concatenate([xz[f, src, 0] for f in range(nh)], axis=1)
        drows = jnp.concatenate([xz[f, src, 1] for f in range(nh)], axis=1)
        pre = dot(mixed, wi[...])
        cube = 0.7978845608028654
        t = jnp.tanh(cube * (pre + 0.044715 * (pre * pre * pre)))
        a = (0.5 * pre * (1.0 + t)).astype(bf16)
        slope = 0.5 * (1.0 + t) + 0.5 * pre * (1.0 - t * t) * (
            cube * (1.0 + 3.0 * 0.044715 * (pre * pre))
        )
        rows = dot(a, wo[...])
        d = (dot_last(drows, wo[...]) * slope).astype(bf16)
        dmix = dot_last(d, wi[...])
        act[src] = a
        dpre[src] = d
        for f in range(nh):
            prs[f, src, 0] = rows[:, f * FS : (f + 1) * FS].astype(bf16)
            prs[f, src, 1] = dmix[:, f * FS : (f + 1) * FS].astype(bf16)
        for j in range(nh - 1):
            to_sum(k, j).start()
        return carry

    lax.fori_loop(0, nd, expert, 0)
    total = nd * act.shape[1]
    squares = jnp.zeros((8, FS), f32)
    a_all = act[...].reshape(total, act.shape[2])
    d_all = dpre[...].reshape(total, dpre.shape[2])
    for f in range(nh):
        cols = pl.ds(f * FS, FS)
        gi = dot_first(xz[f, :, 0].reshape(total, FS), d_all)
        go = dot_first(a_all, xz[f, :, 1].reshape(total, FS))
        g_in[cols, :] = gi
        g_out[:, cols] = go
        for m in range(nh):
            part = gi[:, m * FS : (m + 1) * FS]
            squares = squares + jnp.sum((part * part).reshape(FS // 8, 8, FS), 0)
        squares = squares + jnp.sum((go * go).reshape(D // 8, 8, FS), 0)
    sq[...] = squares

    def summed(k, carry):
        src = lax.rem(n - k + nd, nd)
        for j in range(nh - 1):
            to_sum(k, j).wait_recv()
        value = prs[h, src].astype(f32)
        for j in range(nh - 1):
            value = value + rin[j, src].astype(f32)
        prs[h, src] = value.astype(bf16)

        @pl.when(k > 0)
        def _():
            to_home(k).start()

        return carry

    lax.fori_loop(0, nd, summed, 0)
    mine = pltpu.make_async_copy(prs.at[h, n], yin.at[n], loc.at[1])
    mine.start()

    def finish(k, carry):
        to_expert(k).wait_send()
        to_home(k).wait()
        return carry

    lax.fori_loop(1, nd, finish, 0)

    def finish_z(k, carry):
        for j in range(nh - 1):
            to_feature(k, j).wait_send()
            to_sum(k, j).wait_send()
        return carry

    lax.fori_loop(0, nd, finish_z, 0)
    mine.wait()


def return_kernel(
    nh, experts, count, h1f, stf, og, npar, gates, yin, block_out, p1s, pay, fg,
    p1, py, hss, hsr, sss, ssr, loc
):
    h = lax.axis_index("hid")
    seq = h1f.shape[1]
    slots = h1f.shape[0]
    el = experts * GB
    span = GB * GROUP // slots
    per = BLK // span
    zpeer = [{"hid": lax.rem(h + k, nh)} for k in range(1, nh)]
    greet(zpeer)
    live = count[0]
    gain = npar[2:3, :]
    bias = npar[3:4, :]
    mask = own_group(slots * span, el)
    fold = (
        lax.broadcasted_iota(jnp.int32, (experts, el), 0)
        == lax.shift_right_logical(lax.broadcasted_iota(jnp.int32, (experts, el), 1), 4)
    ).astype(f32)
    ones = jnp.ones((8, FS), f32)
    row8 = lax.broadcasted_iota(jnp.int32, (8, span), 0)
    fg[...] = jnp.zeros_like(fg)

    def back_block(b, carry):
        rows = pl.ds(pl.multiple_of(b * span, span), span)
        grows = pl.ds(pl.multiple_of(b * GB, GB), GB)
        spread = expand(stf[:, :, rows], experts, el)
        mean = [v[:, el : el + FS] for v in spread]
        inv = [v[:, el + FS :] for v in spread]
        nhat, u, dy, hid = block_values(h1f, og, gain, bias, live, rows, mean, inv)
        er = yin[:, 0, grows, :].reshape(el, FS)
        dm = yin[:, 1, grows, :].reshape(el, FS)
        y = jnp.concatenate([er, dm], 1).astype(f32)
        gate = gates[b]
        bd = dot(gate, y, EXACT)
        dyu = jnp.concatenate([jnp.concatenate(dy, 0), jnp.concatenate(u, 0)], 1)
        dgates = dot_last(dyu, y, EXACT)
        gd = gate * dgates
        inner = jnp.sum(gd.reshape(slots, GB, span // GB, el), axis=(0, 2), keepdims=True)
        dlog = (gd.reshape(slots, GB, span // GB, el) - gate.reshape(slots, GB, span // GB, el) * inner)
        dlog = dlog.reshape(slots, span, el)
        acc_gain = jnp.zeros((1, FS), f32)
        acc_bias = jnp.zeros((1, FS), f32)
        for s in range(slots):
            part = slice(s * span, (s + 1) * span)
            back = bd[part, :FS]
            du = bd[part, FS:]
            block_out[s, rows, :] = jnp.where(s < live, hid[s] + back, 0.0).astype(bf16)
            q = du * gain
            p1[s, rows, :] = (dy[s] + inv[s] * q).astype(bf16)
            acc_gain = acc_gain + jnp.sum(du * nhat[s], 0, keepdims=True)
            acc_bias = acc_bias + jnp.sum(du, 0, keepdims=True)
            py[s, 0:experts, rows] = dot_last(fold, dlog[s], EXACT)
            s1 = dot_last(ones, q, EXACT)
            s2 = dot_last(ones, q * nhat[s], EXACT)
            py[s, experts : experts + 8, rows] = jnp.where(row8 == 0, s1, s2)
        fg[2:3, :] += acc_gain
        fg[3:4, :] += acc_bias
        return carry

    sends = []
    for c in reversed(range(seq // BLK)):
        lax.fori_loop(c * per, (c + 1) * per, back_block, 0)
        rows = pl.ds(c * BLK, BLK)
        mine = [
            pltpu.make_async_copy(p1.at[h, rows], p1s.at[h, rows], loc.at[c, 0]),
            pltpu.make_async_copy(py.at[h, :, rows], pay.at[h, :, rows], loc.at[c, 1]),
        ]
        for m in mine:
            m.start()
        for k in range(nh - 1):
            peer = lax.rem(h + k + 1, nh)
            a = remote(p1.at[peer, rows], p1s.at[h, rows], hss.at[c, k], hsr.at[c, k], zpeer[k])
            s = remote(
                py.at[peer, :, rows], pay.at[h, :, rows], sss.at[c, k], ssr.at[c, k], zpeer[k]
            )
            a.start()
            s.start()
            sends += [a, s]
        sends += mine
    for c in sends:
        c.wait()


def backward_kernel(
    nh, experts, x, w, p, a1, qkv, heads, lse, h1, p1s, pay, tgf, gw, sg,
    dk, dv, dqkv, dattn, dheads, tgb, pad, small, hss, hsr, loc
):
    h = lax.axis_index("hid")
    seq = x.shape[1]
    zpeer = [{"hid": lax.rem(h + k, nh)} for k in range(1, nh)]
    greet(zpeer)
    controller_rows(p, pad, experts)
    gain1 = row_of(p, 0)
    gain2 = row_of(p, 2)
    bias2 = row_of(p, 3)
    low_half = head_masks(BLK)
    lane = lax.broadcasted_iota(jnp.int32, (BLK, FS), 1)
    causal = lax.broadcasted_iota(jnp.int32, (BLK, BLK), 1) <= lax.broadcasted_iota(
        jnp.int32, (BLK, BLK), 0
    )
    eye = (
        lax.broadcasted_iota(jnp.int32, (experts + 8, FS), 0)
        == lax.broadcasted_iota(jnp.int32, (experts + 8, FS), 1)
    ).astype(f32)
    small[...] = jnp.zeros_like(small)
    sends = []
    for b in reversed(range(seq // BLK)):
        rows = pl.ds(b * BLK, BLK)
        past = b * BLK
        last = b == seq // BLK - 1
        total = pay[0, :, rows]
        for f in range(1, nh):
            total = total + pay[f, :, rows]
        cols = dot_first(total, eye, EXACT)
        s1 = cols[:, experts : experts + 1]
        s2 = cols[:, experts + 1 : experts + 2]
        hidden = h1[rows, :]
        nhat, _, inv = standardize(hidden)
        du = dot(jnp.where(lane < experts, cols, 0.0), pad[...], EXACT)
        q = du * gain2
        mq = (s1 + jnp.sum(q, -1, keepdims=True)) / D
        mqn = (s2 + jnp.sum(q * nhat, -1, keepdims=True)) / D
        dh1 = features(p1s, rows).astype(f32) + inv * (q - mq - nhat * mqn)
        small[2:3, :] += jnp.sum(du * nhat, 0, keepdims=True)
        small[3:4, :] += jnp.sum(du, 0, keepdims=True)
        small[8 : 8 + experts, :] += dot_first(cols, nhat * gain2 + bias2, EXACT)[0:experts]
        da = dh1.astype(bf16)
        dattn[rows, :] = da

        def pair(hp, carry):
            dh = dot(da, w[hp].reshape(D, D)[:, 3 * FS :]).astype(bf16)
            qb = qkv[hp, rows, 0:FS]
            dq = jnp.zeros((BLK, FS), f32)
            zero = jnp.zeros_like(qb)
            spans = [(rows, True)]
            if b > 0:
                spans.append((pl.ds(0, past), False))
            dks = [jnp.zeros((BLK, FS), f32), jnp.zeros((past, FS), f32)]
            dvs = [jnp.zeros((BLK, FS), f32), jnp.zeros((past, FS), f32)]
            for half in range(2):
                mine = low_half if half == 0 else jnp.logical_not(low_half)
                qm = jnp.where(mine, qb, zero)
                dm = jnp.where(mine, dh, zero)
                base = jnp.sum(
                    jnp.where(lane == 2 * hp + half, lse[rows, :], 0.0), -1, keepdims=True
                )
                probs, dprobs = [], []
                inner = jnp.zeros((BLK, 1), f32)
                for keys, now in spans:
                    s = dot_last(qm, qkv[hp, keys, FS : 2 * FS])
                    if now:
                        s = jnp.where(causal, s, fill_value)
                    pr = jnp.exp(s - base)
                    dp = dot_last(dm, qkv[hp, keys, 2 * FS :])
                    inner = inner + jnp.sum(pr * dp, -1, keepdims=True)
                    probs.append(pr)
                    dprobs.append(dp)
                for i, (keys, now) in enumerate(spans):
                    ds = (probs[i] * (dprobs[i] - inner)).astype(bf16)
                    kk = qkv[hp, keys, FS : 2 * FS]
                    part = dot(ds, kk)
                    dq = dq + jnp.where(mine, part, 0.0)
                    dks[i] = dks[i] + dot_first(ds, qm)
                    dvs[i] = dvs[i] + dot_first(probs[i].astype(bf16), dm)
            if last:
                dk[hp, rows, :] = dks[0]
                dv[hp, rows, :] = dvs[0]
                if b > 0:
                    dk[hp, 0:past, :] = dks[1]
                    dv[hp, 0:past, :] = dvs[1]
            else:
                dk[hp, rows, :] += dks[0]
                dv[hp, rows, :] += dvs[0]
                if b > 0:
                    dk[hp, 0:past, :] += dks[1]
                    dv[hp, 0:past, :] += dvs[1]
            dqkv[hp, rows, 0:FS] = (dq * HS**-0.5).astype(bf16)
            dqkv[hp, rows, FS : 2 * FS] = dk[hp, rows, :].astype(bf16)
            dqkv[hp, rows, 2 * FS :] = dv[hp, rows, :].astype(bf16)
            return carry

        lax.fori_loop(0, nh, pair, 0)
        da1 = jnp.zeros((BLK, D), f32)
        for hp in range(nh):
            da1 = da1 + dot_last(dqkv[hp, rows, :], w[hp].reshape(D, D)[:, : 3 * FS])
        hat, _, inv1 = standardize(features(x, rows).astype(f32))
        q1 = da1 * gain1
        m1 = jnp.sum(q1, -1, keepdims=True) / D
        m2 = jnp.sum(q1 * hat, -1, keepdims=True) / D
        tg = dh1 + inv1 * (q1 - m1 - hat * m2)
        small[0:1, :] += jnp.sum(da1 * hat, 0, keepdims=True)
        small[1:2, :] += jnp.sum(da1, 0, keepdims=True)
        for f in range(nh):
            tgb[f, rows, :] = tg[:, f * FS : (f + 1) * FS].astype(bf16)
        mine = pltpu.make_async_copy(tgb.at[h, rows], tgf.at[h, rows], loc.at[b])
        mine.start()
        sends.append(mine)
        for k in range(nh - 1):
            peer = lax.rem(h + k + 1, nh)
            c = remote(tgb.at[peer, rows], tgf.at[h, rows], hss.at[b, k], hsr.at[b, k], zpeer[k])
            c.start()
            sends.append(c)

    def weight_grads(hp, carry):
        gi = dot_first(a1[...], dqkv[hp]).astype(bf16)
        go = dot_first(dattn[...], heads[hp]).astype(bf16)
        gw[hp] = jnp.concatenate([gi, go], 1).reshape(gw.shape[1:])
        return carry

    lax.fori_loop(0, nh, weight_grads, 0)
    for f in range(nh):
        sg[f] = small[:, f * FS : (f + 1) * FS]
    for c in sends:
        c.wait()


def reduce_kernel(
    nd, nh, experts, gw, sg, fg, sqe, gsum, ssum, norm,
    wc, ch, own, wr, zr, zs, szr, sdr, sqd, sqz, sdb, sqb,
    css, csr, dss, dsr, zss, zsr, ass, asr, bss, bsr, qss, qsr, rss, rsr
):
    n = lax.axis_index("dp")
    h = lax.axis_index("hid")
    core = lax.rem(n, 2)
    chip = lax.div(n, 2)
    chips = nd // 2
    zid = [lax.rem(h + k, nh) for k in range(1, nh)]
    zpeer = [{"hid": z} for z in zid]
    did = [lax.rem(n + k, nd) for k in range(1, nd)]
    dpeer = [{"dp": d} for d in did]
    greet(zpeer + dpeer)
    partner = {"dp": chip * 2 + 1 - core}
    first = remote(gw.at[:, :, 1 - core], wc, css.at[0], csr.at[0], partner)
    first.start()
    sz = [remote(sg.at[zid[k]], szr.at[k], ass.at[k], asr.at[k], zpeer[k]) for k in range(nh - 1)]
    for c in sz:
        c.start()
    for c in sz:
        c.wait_recv()
    small = sg[h]
    for k in range(nh - 1):
        small = small + szr[k]
    small = jnp.concatenate([small[0:8] + fg[...], small[8:]], 0)
    sdb[...] = small
    sd = [remote(sdb, sdr.at[k], bss.at[k], bsr.at[k], dpeer[k]) for k in range(nd - 1)]
    for c in sd:
        c.start()
    first.wait_recv()
    for hp in range(nh):
        ch[hp] = (gw[hp, :, core].astype(f32) + wc[hp].astype(f32)).astype(bf16)
    cid = [lax.rem(chip + k, chips) for k in range(1, chips)]
    second = [
        remote(ch.at[:, cid[k]], wr.at[k], dss.at[k], dsr.at[k], {"dp": cid[k] * 2 + core})
        for k in range(chips - 1)
    ]
    for c in second:
        c.start()
    for c in sd:
        c.wait_recv()
    for k in range(nd - 1):
        small = small + sdr[k]
    ssum[...] = small
    for c in second:
        c.wait_recv()
    total = ch[:, chip].astype(f32)
    for k in range(chips - 1):
        total = total + wr[k].astype(f32)
    zs[...] = total.astype(bf16)
    third = [
        remote(zs.at[zid[k]], zr.at[k], zss.at[k], zsr.at[k], zpeer[k]) for k in range(nh - 1)
    ]
    for c in third:
        c.start()
    for c in third:
        c.wait_recv()
    block = zs[h].astype(f32)
    for k in range(nh - 1):
        block = block + zr[k].astype(f32)
    gsum[...] = block
    squares = sqe[...]
    for f in range(nh):
        part = block[:, f * FS : (f + 1) * FS]
        squares = squares + jnp.sum((part * part).reshape(part.shape[0] // 8, 8, FS), 0)
    both = jnp.sum((small * small).reshape(small.shape[0] // 8, 8, FS), 0)
    squares = squares + jnp.where(n == 0, both, 0.0)
    sqb[0] = squares
    qd = [remote(sqb.at[0], sqd.at[k], qss.at[k], qsr.at[k], dpeer[k]) for k in range(nd - 1)]
    for c in qd:
        c.start()
    for c in qd:
        c.wait_recv()
    for k in range(nd - 1):
        squares = squares + sqd[k]
    sqb[1] = squares
    qz = [remote(sqb.at[1], sqz.at[k], rss.at[k], rsr.at[k], zpeer[k]) for k in range(nh - 1)]
    for c in qz:
        c.start()
    for c in qz:
        c.wait_recv()
    for k in range(nh - 1):
        squares = squares + sqz[k]
    everything = jnp.sum(jnp.sum(squares, 1, keepdims=True), 0, keepdims=True)
    norm[...] = jnp.broadcast_to(jnp.sqrt(everything), norm.shape)
    for c in [first] + sz + sd + second + third + qd + qz:
        c.wait_send()


def call(kernel, cid, outs, scratch, ins, limit=60):
    return pl.pallas_call(
        kernel,
        out_shape=[jax.ShapeDtypeStruct(s, t) for s, t in outs],
        in_specs=[spec for spec, _ in ins],
        out_specs=[VM] * len(outs),
        scratch_shapes=scratch,
        compiler_params=pltpu.CompilerParams(
            collective_id=cid, has_side_effects=True, vmem_limit_bytes=limit * 2**20
        ),

    )(*[value for _, value in ins])


def adam_update(weight, grad, first, second, rate, factor):
    clipped = grad * factor
    first_new = beta_first * first + (1.0 - beta_first) * clipped
    second_new = beta_second * second + (1.0 - beta_second) * clipped * clipped
    first_hat = first_new / (1.0 - beta_first**STEP)
    second_hat = second_new / (1.0 - beta_second**STEP)
    weight_new = weight - rate * (
        first_hat / (jnp.sqrt(second_hat) + adam_epsilon) + weight_decay * weight
    )
    return (first_new, second_new, weight_new)


def shards(
    tokens,
    seq_count,
    out_grad,
    norm_params,
    norm_first,
    norm_second,
    controller_weight,
    router_first,
    router_second,
    attn_in,
    attn_in_first,
    attn_in_second,
    attn_in_average,
    attn_out,
    attn_out_first,
    attn_out_second,
    attn_out_average,
    expert_in,
    expert_in_first,
    expert_in_second,
    expert_in_average,
    expert_out,
    expert_out_first,
    expert_out_second,
    expert_out_average,
):
    ema_keep = (1.0 + STEP) / (10.0 + STEP)
    nd = lax.axis_size("dp")
    nh = lax.axis_size("hid")
    chips = nd // 2
    slots, seq, _ = tokens.shape
    experts = controller_weight.shape[1]
    r = attn_in.shape[0]
    el = experts * GB
    groups = seq * slots // GROUP
    blocks = seq // BLK
    hidden = expert_in.shape[2]
    er = 8 + experts
    wblk = jnp.concatenate([attn_in.reshape(r, 3 * FS), attn_out], 1).astype(bf16)
    pblk = jnp.concatenate([norm_params, jnp.zeros((4, FS), f32), controller_weight.T], 0)
    z3 = nh - 1

    x, w, p, a1, qkv = call(
        functools.partial(project_kernel, nd, nh),
        1,
        [
            ((nh, seq, FS), bf16),
            ((nh, chips, 2, r, D), bf16),
            ((nh, er, FS), f32),
            ((seq, D), bf16),
            ((nh, seq, 3 * FS), bf16),
        ],
        [DMA((blocks, z3))] * 2
        + [DMA((z3,))] * 2
        + [DMA((chips - 1,))] * 2
        + [DMA((1,))] * 2
        + [DMA((z3,))] * 2
        + [DMA((3,))],
        [(VM, tokens), (VM, wblk), (VM, pblk)],
    )
    heads, lse, h1, h1f, stf = call(
        functools.partial(attend_kernel, nh, experts),
        2,
        [
            ((nh, seq, FS), bf16),
            ((seq, FS), f32),
            ((seq, D), f32),
            ((nh, seq, FS), bf16),
            ((nh, er, seq), f32),
        ],
        [
            pltpu.VMEM((nh, seq, FS), bf16),
            pltpu.VMEM((er, seq), f32),
            pltpu.VMEM((FS, D), f32),
        ]
        + [DMA((blocks, z3))] * 4
        + [DMA((blocks, 2))],
        [(VM, x), (VM, w), (VM, p), (VM, qkv)],
    )
    gates, yin, g_in, g_out, sqe = call(
        functools.partial(expert_kernel, nd, nh, experts),
        3,
        [
            ((groups // GB, GB * GROUP, el), f32),
            ((nd, 2, groups, FS), bf16),
            ((D, hidden), f32),
            ((hidden, D), f32),
            ((8, FS), f32),
        ],
        [
            pltpu.VMEM((experts, 2, groups, FS), bf16),
            pltpu.VMEM((nh, nd, 2, groups, FS), bf16),
            pltpu.VMEM((nd, groups, hidden), bf16),
            pltpu.VMEM((nd, groups, hidden), bf16),
            pltpu.VMEM((nh, nd, 2, groups, FS), bf16),
            pltpu.VMEM((z3, nd, 2, groups, FS), bf16),
            pltpu.VMEM((D, hidden), bf16),
            pltpu.VMEM((hidden, D), bf16),
        ]
        + [DMA((nd,))] * 2
        + [DMA((nd, z3))] * 4
        + [DMA((nd,))] * 2
        + [DMA((2,))],
        [
            (SM, seq_count),
            (VM, h1f),
            (VM, stf),
            (VM, out_grad),
            (VM, norm_params),
            (VM, expert_in[0]),
            (VM, expert_out[0]),
        ],
    )
    block_out, p1s, pay, fg = call(
        functools.partial(return_kernel, nh, experts),
        4,
        [
            ((slots, seq, FS), bf16),
            ((nh, seq, FS), bf16),
            ((nh, er, seq), f32),
            ((8, FS), f32),
        ],
        [pltpu.VMEM((nh, seq, FS), bf16), pltpu.VMEM((nh, er, seq), f32)]
        + [DMA((blocks, z3))] * 4
        + [DMA((blocks, 2))],
        [
            (SM, seq_count),
            (VM, h1f),
            (VM, stf),
            (VM, out_grad),
            (VM, norm_params),
            (VM, gates),
            (VM, yin),
        ],
    )
    tgf, gw, sg = call(
        functools.partial(backward_kernel, nh, experts),
        5,
        [
            ((slots, seq, FS), bf16),
            ((nh, chips, 2, r, D), bf16),
            ((nh, er, FS), f32),
        ],
        [
            pltpu.VMEM((nh, seq, FS), f32),
            pltpu.VMEM((nh, seq, FS), f32),
            pltpu.VMEM((nh, seq, 3 * FS), bf16),
            pltpu.VMEM((seq, D), bf16),
            pltpu.VMEM((seq, FS), bf16),
            pltpu.VMEM((nh, seq, FS), bf16),
            pltpu.VMEM((FS, D), f32),
            pltpu.VMEM((er, D), f32),
        ]
        + [DMA((blocks, z3))] * 2
        + [DMA((blocks,))],
        [
            (VM, v)
            for v in (x, w, p, a1, qkv, heads, lse, h1, p1s, pay)
        ],
    )
    gsum, ssum, norm = call(
        functools.partial(reduce_kernel, nd, nh, experts),
        6,
        [((r, D), f32), ((er, FS), f32), ((8, FS), f32)],
        [
            pltpu.VMEM((nh, chips, r, D), bf16),
            pltpu.VMEM((nh, chips, r, D), bf16),
            pltpu.VMEM((8, FS), f32),
            pltpu.VMEM((chips - 1, nh, r, D), bf16),
            pltpu.VMEM((z3, r, D), bf16),
            pltpu.VMEM((nh, r, D), bf16),
            pltpu.VMEM((z3, er, FS), f32),
            pltpu.VMEM((nd - 1, er, FS), f32),
            pltpu.VMEM((nd - 1, 8, FS), f32),
            pltpu.VMEM((z3, 8, FS), f32),
            pltpu.VMEM((er, FS), f32),
            pltpu.VMEM((2, 8, FS), f32),
        ]
        + [DMA((1,))] * 2
        + [DMA((chips - 1,))] * 2
        + [DMA((z3,))] * 4
        + [DMA((nd - 1,))] * 4
        + [DMA((z3,))] * 2,
        [(VM, gw), (VM, sg), (VM, fg), (VM, sqe)],
    )
    grad_norm = norm[0, 0]
    tokens_grad = tgf.astype(f32)
    attn_in_sum = gsum[:, : 3 * FS].reshape(attn_in.shape)
    attn_out_sum = gsum[:, 3 * FS :]
    norm_sum = ssum[0:4]
    router_sum = ssum[8:].T
    expert_in_sum = g_in[None]
    expert_out_sum = g_out[None]
    factor = jnp.minimum(1.0, clip_limit / grad_norm)
    norm_up = adam_update(norm_params, norm_sum, norm_first, norm_second, 0.6, factor)
    router_up = adam_update(
        controller_weight, router_sum, router_first, router_second, (4 * D) ** (-0.5), factor
    )
    attn_in_up = adam_update(
        attn_in, attn_in_sum, attn_in_first, attn_in_second, 0.5 * D ** (-0.5), factor
    )
    attn_out_up = adam_update(
        attn_out,
        attn_out_sum,
        attn_out_first,
        attn_out_second,
        0.5 * (HEADS * HS // 16) ** (-0.5),
        factor,
    )
    expert_in_up = adam_update(
        expert_in,
        expert_in_sum,
        expert_in_first,
        expert_in_second,
        2.5 * (D // GROUP) ** (-0.5),
        factor,
    )
    expert_out_up = adam_update(
        expert_out, expert_out_sum, expert_out_first, expert_out_second, 0.5 * H ** (-0.5), factor
    )
    return (
        block_out,
        tokens_grad,
        grad_norm,
        norm_up[0],
        norm_up[1],
        norm_up[2],
        router_up[0],
        router_up[1],
        router_up[2],
        attn_in_up[0],
        attn_in_up[1],
        attn_in_up[2],
        ema_keep * attn_in_average + (1.0 - ema_keep) * attn_in_up[2],
        attn_out_up[0],
        attn_out_up[1],
        attn_out_up[2],
        ema_keep * attn_out_average + (1.0 - ema_keep) * attn_out_up[2],
        expert_in_up[0],
        expert_in_up[1],
        expert_in_up[2],
        ema_keep * expert_in_average + (1.0 - ema_keep) * expert_in_up[2],
        expert_out_up[0],
        expert_out_up[1],
        expert_out_up[2],
        ema_keep * expert_out_average + (1.0 - ema_keep) * expert_out_up[2],
    )


def solution(mesh):
    return jax.shard_map(
        shards,
        mesh=mesh,
        in_specs=(
            P("dp", None, "hid"),
            P("dp"),
            P("dp", None, "hid"),
            P(None, "hid"),
            P(None, "hid"),
            P(None, "hid"),
            P("hid", None),
            P("hid", None),
            P("hid", None),
            P("dp", None, "hid"),
            P("dp", None, "hid"),
            P("dp", None, "hid"),
            P("dp", None, "hid"),
            P("dp", "hid"),
            P("dp", "hid"),
            P("dp", "hid"),
            P("dp", "hid"),
            P("dp", None, "hid"),
            P("dp", None, "hid"),
            P("dp", None, "hid"),
            P("dp", None, "hid"),
            P("dp", "hid", None),
            P("dp", "hid", None),
            P("dp", "hid", None),
            P("dp", "hid", None),
        ),
        out_specs=(
            P("dp", None, "hid"),
            P("dp", None, "hid"),
            P(),
            P(None, "hid"),
            P(None, "hid"),
            P(None, "hid"),
            P("hid", None),
            P("hid", None),
            P("hid", None),
            P("dp", None, "hid"),
            P("dp", None, "hid"),
            P("dp", None, "hid"),
            P("dp", None, "hid"),
            P("dp", "hid"),
            P("dp", "hid"),
            P("dp", "hid"),
            P("dp", "hid"),
            P("dp", None, "hid"),
            P("dp", None, "hid"),
            P("dp", None, "hid"),
            P("dp", None, "hid"),
            P("dp", "hid", None),
            P("dp", "hid", None),
            P("dp", "hid", None),
            P("dp", "hid", None),
        ),
        check_vma=False,
    )
```

```python
import functools

import jax
import jax.numpy as jnp
from jax import lax
from jax.experimental import pallas as pl
from jax.experimental.pallas import tpu as pltpu
from jax.sharding import PartitionSpec as P

D = 512
HEADS = 8
HS = 64
H = 2048
GROUP = 32
STEP = 10
BLK = 256
FS = 128
GB = 16

norm_epsilon = 1e-05
fill_value = -1e30
clip_limit = 1.0
beta_first = 0.9
beta_second = 0.95
adam_epsilon = 1e-08
weight_decay = 0.1

f32 = jnp.float32
bf16 = jnp.bfloat16
MESH = pl.DeviceIdType.MESH
EXACT = lax.Precision.HIGHEST
VM = pl.BlockSpec(memory_space=pltpu.VMEM)
HB = pl.BlockSpec(memory_space=pl.ANY)
SM = pl.BlockSpec(memory_space=pltpu.SMEM)
DMA = pltpu.SemaphoreType.DMA


def dot(a, b, precision=None):
    return lax.dot_general(
        a, b, (((1,), (0,)), ((), ())), precision=precision, preferred_element_type=f32
    )


def dot_last(a, b, precision=None):
    return lax.dot_general(
        a, b, (((1,), (1,)), ((), ())), precision=precision, preferred_element_type=f32
    )


def dot_first(a, b, precision=None):
    return lax.dot_general(
        a, b, (((0,), (0,)), ((), ())), precision=precision, preferred_element_type=f32
    )


def greet(peers):
    barrier = pltpu.get_barrier_semaphore()
    for peer in peers:
        pl.semaphore_signal(barrier, inc=1, device_id=peer, device_id_type=MESH)
    pl.semaphore_wait(barrier, len(peers))


def remote(src, dst, send, recv, peer):
    return pltpu.make_async_remote_copy(
        src_ref=src, dst_ref=dst, send_sem=send, recv_sem=recv, device_id=peer, device_id_type=MESH
    )


def lanes(ref_like, index):
    return pl.ds(pl.multiple_of(index * ref_like, ref_like), ref_like)


def features(ref, rows):
    return jnp.concatenate([ref[f, rows, :] for f in range(ref.shape[0])], axis=1)


def row_of(ref, row):
    return jnp.concatenate([ref[f, row : row + 1, :] for f in range(ref.shape[0])], axis=1)


def split(v):
    high = v.astype(bf16)
    return high, (v - high.astype(f32)).astype(bf16)


def split3(v):
    high, _ = split(v)
    rest = v - high.astype(f32)
    mid, low = split(rest)
    return high, mid, low


def iota(shape, dim):
    return lax.broadcasted_iota(jnp.int32, shape, dim)


def standardize(v):
    center = jnp.sum(v, -1, keepdims=True) / v.shape[-1]
    dev = v - center
    inv = lax.rsqrt(jnp.sum(dev * dev, -1, keepdims=True) / v.shape[-1] + norm_epsilon)
    return dev * inv, center, inv


def controller_rows(p, pad, experts):
    pad[...] = jnp.zeros_like(pad)
    for f in range(p.shape[0]):
        high, low = split(p[f, 8 : 8 + experts, :])
        pad[0, 0:experts, f * FS : (f + 1) * FS] = high.astype(f32)
        pad[1, 0:experts, f * FS : (f + 1) * FS] = low.astype(f32)


def both_heads(v):
    low = iota(v.shape, 1) < HS
    zero = jnp.zeros_like(v)
    return jnp.concatenate([jnp.where(low, v, zero), jnp.where(low, zero, v)], 0)


def forward_kernel(
    nd, nh, experts, tok, wblk, pblk,
    xo, wout, p, qkvo, kto, headso, recipo, h1o, h1f, stf, eouts,
    x, w, qkv, kt, heads, recip, h1, a1, vt, es, h1b, st, pad,
    tss, tsr, wss, wsr, dss, dsr, css, csr, pss, psr, hss, hsr, sss, ssr, loc, esem, mine_sem, save
):
    n = lax.axis_index("dp")
    h = lax.axis_index("hid")
    core = lax.rem(n, 2)
    chip = lax.div(n, 2)
    chips = nd // 2
    seq = tok.shape[1]
    blocks = seq // BLK
    zpeer = [{"hid": lax.rem(h + k, nh)} for k in range(1, nh)]
    cpeer = [{"dp": lax.rem(chip + k, chips) * 2 + core} for k in range(1, chips)]
    partner = {"dp": chip * 2 + 1 - core}
    greet(zpeer + cpeer + [partner])
    locals_ = [
        pltpu.make_async_copy(wblk, w.at[h, chip, core], loc.at[0]),
        pltpu.make_async_copy(pblk, p.at[h], loc.at[1]),
        pltpu.make_async_copy(tok.at[h], x.at[h], loc.at[2]),
    ]
    for c in locals_:
        c.start()
    wz = [
        remote(wblk, w.at[h, chip, core], wss.at[k], wsr.at[k], zpeer[k]) for k in range(nh - 1)
    ]
    pz = [remote(pblk, p.at[h], pss.at[k], psr.at[k], zpeer[k]) for k in range(nh - 1)]
    for c in wz + pz:
        c.start()
    tz = []
    for b in range(blocks):
        rows = pl.ds(b * BLK, BLK)
        for k in range(nh - 1):
            c = remote(
                tok.at[lax.rem(h + k + 1, nh), rows],
                x.at[h, rows],
                tss.at[b, k],
                tsr.at[b, k],
                zpeer[k],
            )
            c.start()
            tz.append(c)
    locals_[0].wait()
    wc = []
    for j in range(nh):
        piece = lax.rem(h - j + nh, nh)
        if j > 0:
            wz[j - 1].wait_recv()
        for k in range(chips - 1):
            c = remote(
                w.at[piece, chip, core], w.at[piece, chip, core],
                dss.at[j, k], dsr.at[j, k], cpeer[k]
            )
            c.start()
            wc.append(c)
    for c in pz + wc:
        c.wait_recv()
    wp = remote(w.at[:, :, core], w.at[:, :, core], css.at[0], csr.at[0], partner)
    wp.start()
    for c in locals_[1:]:
        c.wait()
    controller_rows(p, pad, experts)
    gain1 = row_of(p, 0)
    bias1 = row_of(p, 1)
    gain2 = row_of(p, 2)
    bias2 = row_of(p, 3)
    scale = jnp.where(iota((BLK, 3 * FS), 1) < FS, HS**-0.5, 1.0).astype(bf16)
    lane = iota((BLK, FS), 1)
    low_half = lane < HS
    causal = iota((BLK, 2 * BLK), 0) <= (iota((BLK, 2 * BLK), 1) & (BLK - 1))
    one = jnp.ones((FS, BLK), bf16)
    low_rows = iota((FS, BLK), 0) < HS
    sends = []
    for b in range(blocks):
        rows = pl.ds(b * BLK, BLK)
        past = b * BLK
        e_ref = es[b]
        for k in range(nh - 1):
            tz[b * (nh - 1) + k].wait_recv()
        normed, _, _ = standardize(features(x, rows).astype(f32))
        a1[...] = (normed * gain1 + bias1).astype(bf16)
        if b == 0:
            wp.wait_recv()
            c = pltpu.make_async_copy(w, wout, loc.at[3])
            c.start()
            sends.append(c)

        def pair(hp, carry):
            proj = dot(a1[...], w[hp].reshape(D, D)[:, : 3 * FS])
            low = proj.astype(bf16) * scale
            qkv[hp, rows, :] = low
            kt[hp, :, rows] = proj[:, FS : 2 * FS].T.astype(bf16)
            vt[hp, :, rows] = proj[:, 2 * FS :].T.astype(bf16)
            q = both_heads(low[:, :FS])
            s_now = dot_last(low[:, FS : 2 * FS], q)
            s_now = jnp.where(causal, s_now, fill_value)
            peak = jnp.max(s_now, 0, keepdims=True)
            if b > 0:
                s_past = dot_last(qkv[hp, 0:past, FS : 2 * FS], q)
                peak = jnp.maximum(peak, jnp.max(s_past, 0, keepdims=True))
                e_ref[hp, 0:past, :] = jnp.exp(s_past - peak).astype(bf16)
            e_ref[hp, past : past + BLK, :] = jnp.exp(s_now - peak).astype(bf16)
            outs = []
            for half in range(2):
                total = jnp.zeros((FS, BLK), f32)
                for j in range(b + 1):
                    keys = slice(j * BLK, (j + 1) * BLK)
                    v = vt[hp, :, keys]
                    v = jnp.where(low_rows, v, one) if half == 0 else jnp.where(low_rows, one, v)
                    total = total + dot(v, e_ref[hp, keys, half * BLK : (half + 1) * BLK])
                outs.append(total.T)
            value = jnp.where(low_half, outs[0], outs[1])
            total = jnp.where(low_half, pltpu.roll(outs[0], HS, 1), pltpu.roll(outs[1], HS, 1))
            inv = 1.0 / total
            recip[hp, rows, :] = inv
            heads[hp, rows, :] = (value * inv).astype(bf16)
            return carry

        lax.fori_loop(0, nh, pair, 0)
        saves = [
            (e_ref, eouts[b]),
            (x.at[:, rows], xo.at[:, rows]),
            (qkv.at[:, rows], qkvo.at[:, rows]),
            (kt.at[:, :, rows], kto.at[:, :, rows]),
            (heads.at[:, rows], headso.at[:, rows]),
            (recip.at[:, rows], recipo.at[:, rows]),
        ]
        for k, (src, dst) in enumerate(saves):
            c = pltpu.make_async_copy(src, dst, esem.at[b, k])
            c.start()
            sends.append(c)
        attn = jnp.zeros((BLK, D), f32)
        for hp in range(nh):
            attn = attn + dot_last(heads[hp, rows, :], w[hp].reshape(D, D)[:, 3 * FS :])
        hidden = features(x, rows).astype(f32) + attn
        h1[rows, :] = hidden
        c = pltpu.make_async_copy(h1.at[rows], h1o.at[rows], save.at[b])
        c.start()
        sends.append(c)
        normed, center, inv = standardize(hidden)
        u = normed * gain2 + bias2
        uh, ul = split(u)
        cols = dot_last(
            jnp.concatenate([uh, ul, uh], 1),
            jnp.concatenate([pad[0], pad[0], pad[1]], 1).astype(bf16),
        )
        cols = jnp.where(lane == experts, center, jnp.where(lane == experts + 1, inv, cols))
        st[:, rows] = cols.T[0 : experts + 8, :]
        for f in range(nh):
            h1b[f, rows, :] = hidden[:, f * FS : (f + 1) * FS].astype(bf16)
        mine = [
            pltpu.make_async_copy(h1b.at[h, rows], h1f.at[h, rows], mine_sem.at[b, 0]),
            pltpu.make_async_copy(st.at[:, rows], stf.at[h, :, rows], mine_sem.at[b, 1]),
        ]
        for c in mine:
            c.start()
        for k in range(nh - 1):
            c = remote(
                h1b.at[lax.rem(h + k + 1, nh), rows],
                h1f.at[h, rows],
                hss.at[b, k],
                hsr.at[b, k],
                zpeer[k],
            )
            s = remote(
                st.at[:, rows], stf.at[h, :, rows], sss.at[b, k], ssr.at[b, k], zpeer[k]
            )
            c.start()
            s.start()
            sends += [c, s]
        sends += mine
    for c in sends:
        c.wait()
    for c in wz + pz + tz + wc + [wp]:
        c.wait_send()


def expand(stb, experts, el, gates):
    height = stb.shape[1]
    width = (el if gates else 0) + 2 * FS
    rows = iota((3 * height, width), 0)
    cols = iota((3 * height, width), 1)
    rows = jnp.where(rows >= 2 * height, rows - 2 * height, rows)
    rows = jnp.where(rows >= height, rows - height, rows)
    base = el if gates else 0
    target = jnp.where(cols < base + FS, experts, experts + 1)
    if gates:
        target = jnp.where(cols < el, lax.shift_right_logical(cols, 4), target)
    pick = jnp.where(rows == target, 1.0, 0.0).astype(bf16)
    return [
        dot_first(jnp.concatenate(split3(stb[s]), 0), pick) for s in range(stb.shape[0])
    ]


def own_group(tokens, el):
    group = lax.shift_right_logical(iota((tokens, el), 0), 3) & (GB - 1)
    return (iota((tokens, el), 1) & (GB - 1)) == group


def block_values(h1f, og, gain, bias, live, rows, mean, inv):
    slots = h1f.shape[0]
    nhat, u, dy, hid = [], [], [], []
    for s in range(slots):
        hidden = h1f[s, rows, :].astype(f32)
        hat = (hidden - mean[s]) * inv[s]
        nhat.append(hat)
        u.append((hat * gain + bias).astype(bf16))
        hid.append(hidden)
        grad = og[s, rows, :]
        dy.append(jnp.where(s < live, grad, jnp.zeros_like(grad)))
    return nhat, u, dy, hid


def expert_kernel(
    nd, nh, experts, count, h1f, stf, og, npar, win, wout, gates, yin, g_in, g_out, sq,
    mout, xz, act, dpre, ps, inl, inr, yo, wf, wi, wo,
    dss, dsr, xsr, xsl, xrl, xrr, isr, isl, irl, irr, yss, ysr, loc
):
    n = lax.axis_index("dp")
    h = lax.axis_index("hid")
    seq = h1f.shape[1]
    slots = h1f.shape[0]
    el = experts * GB
    span = GB * GROUP // slots
    top = nh - 1
    right = {"hid": jnp.minimum(h + 1, top)}
    left = {"hid": jnp.maximum(h - 1, 0)}
    weights = [
        pltpu.make_async_copy(win, wf.at[0], loc.at[0]),
        pltpu.make_async_copy(wout, wf.at[1], loc.at[1]),
    ]
    for c in weights:
        c.start()
    greet([{"hid": lax.rem(h + k, nh)} for k in range(1, nh)] + [
        {"dp": lax.rem(n + k, nd)} for k in range(1, nd)
    ])
    live = count[0]
    gain = npar[2:3, :]
    bias = npar[3:4, :]
    mask = own_group(slots * span, el)

    def gate_block(b, carry):
        rows = pl.ds(pl.multiple_of(b * span, span), span)
        grows = pl.ds(pl.multiple_of(b * GB, GB), GB)
        spread = expand(stf[:, :, rows], experts, el, True)
        logits = jnp.stack(
            [jnp.where(s < live, spread[s][:, :el], fill_value) for s in range(slots)]
        ).reshape(slots, GB, span // GB, el)
        peak = jnp.max(logits, axis=(0, 2), keepdims=True)
        e = jnp.exp(logits - peak)
        gate = e / jnp.sum(e, axis=(0, 2), keepdims=True)
        gate = jnp.where(mask, gate.reshape(slots * span, el), 0.0).astype(bf16)
        gates[b] = gate
        mean = [v[:, el : el + FS] for v in spread]
        inv = [v[:, el + FS :] for v in spread]
        _, u, dy, _ = block_values(h1f, og, gain, bias, live, rows, mean, inv)
        both = jnp.concatenate([jnp.concatenate(u, 0), jnp.concatenate(dy, 0)], 1)
        mixed = dot_first(gate, both).astype(bf16)
        mout[:, 0, grows, :] = mixed[:, :FS].reshape(experts, GB, FS)
        mout[:, 1, grows, :] = mixed[:, FS:].reshape(experts, GB, FS)
        return carry

    lax.fori_loop(0, seq // span, gate_block, 0)

    def source(k):
        return lax.rem(n - k + nd, nd)

    def to_expert(k):
        e = lax.rem(n + k, nd)
        return remote(mout.at[e], xz.at[h, n], dss.at[k], dsr.at[k], {"dp": e})

    def go_right(k, j):
        piece = xz.at[jnp.maximum(h - j, 0), source(k)]
        return remote(piece, piece, xsr.at[k, j], xrl.at[k, j], right)

    def go_left(k, j):
        piece = xz.at[jnp.minimum(h + j, top), source(k)]
        return remote(piece, piece, xsl.at[k, j], xrr.at[k, j], left)

    def sum_right(k, d):
        piece = inl.at[k, jnp.minimum(h + d, top)]
        return remote(piece, piece, isr.at[k, d], irl.at[k, d - 1], right)

    def sum_left(k, d):
        piece = inr.at[k, jnp.maximum(h - d, 0)]
        return remote(piece, piece, isl.at[k, d], irr.at[k, d - 1], left)

    def from_left(k, d):
        piece = inl.at[k, jnp.minimum(h + d, top)]
        return remote(piece, piece, isr.at[k, d], irl.at[k, d], right)

    def from_right(k, d):
        piece = inr.at[k, jnp.maximum(h - d, 0)]
        return remote(piece, piece, isl.at[k, d], irr.at[k, d], left)

    def to_home(k):
        src = source(k)
        return remote(yo.at[k], yin.at[n], yss.at[k], ysr.at[k], {"dp": src})

    own = pltpu.make_async_copy(mout.at[n], xz.at[h, n], loc.at[2])
    own.start()

    def start_expert(k, carry):
        to_expert(k).start()
        return carry

    lax.fori_loop(1, nd, start_expert, 0)
    for c in weights:
        c.wait()
    wi[...] = wf[0].astype(bf16)
    wo[...] = wf[1].astype(bf16)
    own.wait()

    def expert(k):
        src = source(k)
        slot = lax.rem(k, nh)
        mixed = jnp.concatenate([xz[f, src, 0] for f in range(nh)], axis=1)
        drows = jnp.concatenate([xz[f, src, 1] for f in range(nh)], axis=1)
        pre = dot(mixed, wi[...])
        cube = 0.7978845608028654
        t = jnp.tanh(cube * (pre + 0.044715 * (pre * pre * pre)))
        a = (0.5 * pre * (1.0 + t)).astype(bf16)
        slope = 0.5 * (1.0 + t) + 0.5 * pre * (1.0 - t * t) * (
            cube * (1.0 + 3.0 * 0.044715 * (pre * pre))
        )
        rows = dot(a, wo[...])
        d = (dot_last(drows, wo[...]) * slope).astype(bf16)
        dmix = dot_last(d, wi[...])
        act[src] = a
        dpre[src] = d
        for f in range(nh):
            ps[slot, f, 0] = rows[:, f * FS : (f + 1) * FS].astype(bf16)
            ps[slot, f, 1] = dmix[:, f * FS : (f + 1) * FS].astype(bf16)

    def step(t, carry):
        @pl.when(t < nd)
        def _():
            @pl.when(t > 0)
            def _():
                to_expert(t).wait_recv()

            @pl.when(h < top)
            def _():
                go_right(t, 0).start()

            @pl.when(h > 0)
            def _():
                go_left(t, 0).start()

        for j in range(1, nh):
            k = t - j
            here = jnp.logical_and(k >= 0, k < nd)

            @pl.when(jnp.logical_and(here, h >= j))
            def _(k=k, j=j):
                go_right(k, j - 1).wait_recv()
                if j < top:

                    @pl.when(h < top)
                    def _():
                        go_right(k, j).start()

            @pl.when(jnp.logical_and(here, h + j <= top))
            def _(k=k, j=j):
                go_left(k, j - 1).wait_recv()
                if j < top:

                    @pl.when(h > 0)
                    def _():
                        go_left(k, j).start()

        ke = t - top

        @pl.when(jnp.logical_and(ke >= 0, ke < nd))
        def _():
            expert(ke)

        kr = t - top - h

        @pl.when(jnp.logical_and(kr >= 0, kr < nd))
        def _():
            slot = lax.rem(kr, nh)
            for d in range(nh):

                @pl.when(h + d <= top)
                def _(d=d):
                    dest = jnp.minimum(h + d, top)

                    @pl.when(h > 0)
                    def _():
                        from_left(kr, d).wait_recv()
                        if d > 0:
                            value = inl[kr, dest].astype(f32) + ps[slot, dest].astype(f32)
                            inl[kr, dest] = value.astype(bf16)

                    if d > 0:

                        @pl.when(h == 0)
                        def _():
                            inl[kr, dest] = ps[slot, dest]

                        sum_right(kr, d).start()

        kl = t - top - (top - h)

        @pl.when(jnp.logical_and(kl >= 0, kl < nd))
        def _():
            slot = lax.rem(kl, nh)
            for d in range(nh):

                @pl.when(h - d >= 0)
                def _(d=d):
                    dest = jnp.maximum(h - d, 0)

                    @pl.when(h < top)
                    def _():
                        from_right(kl, d).wait_recv()
                        if d > 0:
                            value = inr[kl, dest].astype(f32) + ps[slot, dest].astype(f32)
                            inr[kl, dest] = value.astype(bf16)

                    if d > 0:

                        @pl.when(h == top)
                        def _():
                            inr[kl, dest] = ps[slot, dest]

                        sum_left(kl, d).start()

        kf = t - 2 * top

        @pl.when(kf >= 0)
        def _():
            slot = lax.rem(kf, nh)

            @pl.when(h == 0)
            def _():
                yo[kf] = (ps[slot, h].astype(f32) + inr[kf, h].astype(f32)).astype(bf16)

            @pl.when(h == top)
            def _():
                yo[kf] = (ps[slot, h].astype(f32) + inl[kf, h].astype(f32)).astype(bf16)

            @pl.when(jnp.logical_and(h > 0, h < top))
            def _():
                value = ps[slot, h].astype(f32) + inl[kf, h].astype(f32)
                yo[kf] = (value + inr[kf, h].astype(f32)).astype(bf16)

            @pl.when(kf > 0)
            def _():
                to_home(kf).start()

        return carry

    lax.fori_loop(0, nd + 2 * top, step, 0)
    mine = pltpu.make_async_copy(yo.at[0], yin.at[n], loc.at[3])
    mine.start()
    total = nd * act.shape[1]
    squares = jnp.zeros((8, FS), f32)
    a_all = act[...].reshape(total, act.shape[2])
    d_all = dpre[...].reshape(total, dpre.shape[2])
    for f in range(nh):
        cols = pl.ds(f * FS, FS)
        gi = dot_first(xz[f, :, 0].reshape(total, FS), d_all)
        go = dot_first(a_all, xz[f, :, 1].reshape(total, FS))
        g_in[cols, :] = gi
        g_out[:, cols] = go
        for m in range(nh):
            part = gi[:, m * FS : (m + 1) * FS]
            squares = squares + jnp.sum((part * part).reshape(FS // 8, 8, FS), 0)
        squares = squares + jnp.sum((go * go).reshape(D // 8, 8, FS), 0)
    sq[...] = squares

    def finish(k, carry):
        @pl.when(k > 0)
        def _():
            to_expert(k).wait_send()
            to_home(k).wait()

        for j in range(top):

            @pl.when(jnp.logical_and(h < top, h >= j))
            def _(j=j):
                go_right(k, j).wait_send()

            @pl.when(jnp.logical_and(h > 0, h + j <= top))
            def _(j=j):
                go_left(k, j).wait_send()

        for d in range(1, nh):

            @pl.when(h + d <= top)
            def _(d=d):
                sum_right(k, d).wait_send()

            @pl.when(h - d >= 0)
            def _(d=d):
                sum_left(k, d).wait_send()

        return carry

    lax.fori_loop(0, nd, finish, 0)
    mine.wait()


def backward_kernel(
    nh, experts, count, h1f, stf, og, npar, gates, yin, p, xi, win, qkvi, kti, headsi, recipi, h1i,
    ein, block_out, fg, tgf, gw, sg,
    p1, py, p1s, pay, x, w, qkv, kt, heads, recip, h1, a1, dk, dv, dqkv, dattn, tgb, pad, small,
    es, pss, psr, sss, ssr, hss, hsr, loc, mloc, lsem, esem
):
    h = lax.axis_index("hid")
    seq = h1f.shape[1]
    slots = h1f.shape[0]
    blocks = seq // BLK
    el = experts * GB
    span = GB * GROUP // slots
    per = BLK // span
    zpeer = [{"hid": lax.rem(h + k, nh)} for k in range(1, nh)]
    held = [(xi, x), (win, w), (h1i, h1), (qkvi, qkv), (kti, kt), (headsi, heads), (recipi, recip)]
    held = [pltpu.make_async_copy(src, dst, lsem.at[i]) for i, (src, dst) in enumerate(held)]
    for c in held:
        c.start()
    loads = [pltpu.make_async_copy(ein[b], es[b], esem.at[b]) for b in range(blocks)]
    for c in reversed(loads):
        c.start()
    greet(zpeer)
    live = count[0]
    gain = npar[2:3, :]
    bias = npar[3:4, :]
    height = experts + 8
    srow = iota((height, el + 2 * FS), 0)
    scol = iota((height, el + 2 * FS), 1)
    target = jnp.where(scol < el, lax.shift_right_logical(scol, 4), experts)
    target = jnp.where(scol >= el + FS, experts + 1, target)
    fold = jnp.where(srow == target, 1.0, 0.0).astype(bf16)
    fold = jnp.concatenate([fold, fold], 1)
    fg[...] = jnp.zeros_like(fg)

    def back_block(b, carry):
        rows = pl.ds(pl.multiple_of(b * span, span), span)
        grows = pl.ds(pl.multiple_of(b * GB, GB), GB)
        spread = expand(stf[:, :, rows], experts, el, False)
        mean = [v[:, :FS] for v in spread]
        inv = [v[:, FS:] for v in spread]
        nhat, u, dy, hid = block_values(h1f, og, gain, bias, live, rows, mean, inv)
        y = jnp.concatenate(
            [yin[:, 0, grows, :].reshape(el, FS), yin[:, 1, grows, :].reshape(el, FS)], 1
        )
        gate = gates[b]
        bd = dot(gate, y)
        dgates = dot_last(
            jnp.concatenate([jnp.concatenate(dy, 0), jnp.concatenate(u, 0)], 1), y
        )
        gate = gate.astype(f32)
        gd = gate * dgates
        gd4 = gd.reshape(slots, GB, span // GB, el)
        inner = jnp.sum(gd4, axis=(0, 2), keepdims=True)
        dlog = gd4 - gate.reshape(slots, GB, span // GB, el) * inner
        dlog = dlog.reshape(slots * span, el)
        qs, qn = [], []
        acc_gain = jnp.zeros((1, FS), f32)
        acc_bias = jnp.zeros((1, FS), f32)
        for s in range(slots):
            part = slice(s * span, (s + 1) * span)
            back = bd[part, :FS]
            du = bd[part, FS:]
            block_out[s, rows, :] = jnp.where(s < live, hid[s] + back, 0.0).astype(bf16)
            q = du * gain
            p1[s, rows, :] = (dy[s].astype(f32) + inv[s] * q).astype(bf16)
            acc_gain = acc_gain + jnp.sum(du * nhat[s], 0, keepdims=True)
            acc_bias = acc_bias + jnp.sum(du, 0, keepdims=True)
            qs.append(q)
            qn.append(q * nhat[s])
        high, low = split(
            jnp.concatenate([dlog, jnp.concatenate(qs, 0), jnp.concatenate(qn, 0)], 1)
        )
        folded = dot_last(fold, jnp.concatenate([high, low], 1))
        for s in range(slots):
            py[s, :, rows] = folded[:, s * span : (s + 1) * span]
        fg[2:3, :] += acc_gain
        fg[3:4, :] += acc_bias
        return carry

    arrive = [None] * blocks
    sends = []
    for c in reversed(range(blocks)):
        lax.fori_loop(c * per, (c + 1) * per, back_block, 0)
        rows = pl.ds(c * BLK, BLK)
        mine = [
            pltpu.make_async_copy(p1.at[h, rows], p1s.at[h, rows], mloc.at[c, 0]),
            pltpu.make_async_copy(py.at[h, :, rows], pay.at[h, :, rows], mloc.at[c, 1]),
        ]
        for m in mine:
            m.start()
        far = []
        for k in range(nh - 1):
            peer = lax.rem(h + k + 1, nh)
            a = remote(p1.at[peer, rows], p1s.at[h, rows], pss.at[c, k], psr.at[c, k], zpeer[k])
            s = remote(
                py.at[peer, :, rows], pay.at[h, :, rows], sss.at[c, k], ssr.at[c, k], zpeer[k]
            )
            a.start()
            s.start()
            far += [a, s]
        arrive[c] = (mine, far)
    controller_rows(p, pad, experts)
    gain1 = row_of(p, 0)
    bias1 = row_of(p, 1)
    gain2 = row_of(p, 2)
    bias2 = row_of(p, 3)
    lane = iota((BLK, FS), 1)
    low_half = lane < HS
    er = iota((3 * height, FS), 0)
    er = jnp.where(er >= 2 * height, er - 2 * height, er)
    er = jnp.where(er >= height, er - height, er)
    eye = jnp.where(er == iota((3 * height, FS), 1), 1.0, 0.0).astype(bf16)
    pick = iota((8, 2 * FS), 1) & (FS - 1)
    row = iota((8, 2 * FS), 0)
    pick = ((row == 0) & (pick < HS)) | ((row == 1) & (pick >= HS))
    pick = jnp.where(pick, 1.0, 0.0).astype(bf16)
    small[...] = jnp.zeros_like(small)
    for c in held:
        c.wait()
    for b in reversed(range(blocks)):
        rows = pl.ds(b * BLK, BLK)
        last = b == blocks - 1
        e_ref = es[b]
        mine, far = arrive[b]
        for c in mine:
            c.wait()
        for c in far:
            c.wait_recv()
        total = pay[0, :, rows]
        for f in range(1, nh):
            total = total + pay[f, :, rows]
        cols = dot_first(jnp.concatenate(split3(total), 0), eye)
        s1 = cols[:, experts : experts + 1]
        s2 = cols[:, experts + 1 : experts + 2]
        hidden = h1[rows, :]
        nhat, _, inv = standardize(hidden)
        ch, cl = split(jnp.where(lane < experts, cols, 0.0))
        du = dot(
            jnp.concatenate([ch, cl, ch], 1),
            jnp.concatenate([pad[0], pad[0], pad[1]], 0).astype(bf16),
        )
        q = du * gain2
        mq = (s1 + jnp.sum(q, -1, keepdims=True)) / D
        mqn = (s2 + jnp.sum(q * nhat, -1, keepdims=True)) / D
        dh1 = features(p1s, rows).astype(f32) + inv * (q - mq - nhat * mqn)
        small[2:3, :] += jnp.sum(du * nhat, 0, keepdims=True)
        small[3:4, :] += jnp.sum(du, 0, keepdims=True)
        routed = dot_first(
            jnp.concatenate([ch, cl], 1), (nhat * gain2 + bias2).astype(bf16)
        )
        small[8 : 8 + experts, :] += routed[0:experts] + routed[FS : FS + experts]
        dattn[rows, :] = dh1.astype(bf16)
        loads[b].wait()

        def pair(hp, carry):
            dh = dot(dattn[rows, :], w[hp].reshape(D, D)[:, 3 * FS :]).astype(bf16).astype(f32)
            dh = dh * recip[hp, rows, :]
            high, rest = split(dh * heads[hp, rows, :].astype(f32))
            inner = dot_last(pick, jnp.concatenate([high, rest], 1))
            inner = jnp.concatenate([inner[0:1], inner[1:2]], 1)
            dhs = both_heads(dh.astype(bf16))
            qs = both_heads(qkv[hp, rows, 0:FS])
            dqt = jnp.zeros((FS, 2 * BLK), f32)
            for j in range(b + 1):
                keys = slice(j * BLK, (j + 1) * BLK)
                e = e_ref[hp, keys, :]
                dp = dot_last(qkv[hp, keys, 2 * FS :], dhs)
                ds = (e.astype(f32) * (dp - inner)).astype(bf16)
                dqt = dqt + dot(kt[hp, :, keys], ds)
                if last:
                    dk[hp, keys, :] = dot(ds, qs)
                    dv[hp, keys, :] = dot(e, dhs)
                else:
                    dk[hp, keys, :] += dot(ds, qs)
                    dv[hp, keys, :] += dot(e, dhs)
            dq = jnp.where(low_half, dqt[:, :BLK].T, dqt[:, BLK:].T)
            dqkv[hp, rows, 0:FS] = (dq * HS**-0.5).astype(bf16)
            dqkv[hp, rows, FS : 2 * FS] = dk[hp, rows, :].astype(bf16)
            dqkv[hp, rows, 2 * FS :] = dv[hp, rows, :].astype(bf16)
            return carry

        lax.fori_loop(0, nh, pair, 0)
        da1 = jnp.zeros((BLK, D), f32)
        for hp in range(nh):
            da1 = da1 + dot_last(dqkv[hp, rows, :], w[hp].reshape(D, D)[:, : 3 * FS])
        hat, _, inv1 = standardize(features(x, rows).astype(f32))
        a1[rows, :] = (hat * gain1 + bias1).astype(bf16)
        q1 = da1 * gain1
        m1 = jnp.sum(q1, -1, keepdims=True) / D
        m2 = jnp.sum(q1 * hat, -1, keepdims=True) / D
        tg = dh1 + inv1 * (q1 - m1 - hat * m2)
        small[0:1, :] += jnp.sum(da1 * hat, 0, keepdims=True)
        small[1:2, :] += jnp.sum(da1, 0, keepdims=True)
        for f in range(nh):
            tgb[f, rows, :] = tg[:, f * FS : (f + 1) * FS].astype(bf16)
        mine = pltpu.make_async_copy(tgb.at[h, rows], tgf.at[h, rows], loc.at[b])
        mine.start()
        sends.append(mine)
        for k in range(nh - 1):
            peer = lax.rem(h + k + 1, nh)
            c = remote(tgb.at[peer, rows], tgf.at[h, rows], hss.at[b, k], hsr.at[b, k], zpeer[k])
            c.start()
            sends.append(c)

    def weight_grads(hp, carry):
        gi = dot_first(a1[...], dqkv[hp]).astype(bf16)
        go = dot_first(dattn[...], heads[hp]).astype(bf16)
        gw[hp] = jnp.concatenate([gi, go], 1).reshape(gw.shape[1:])
        return carry

    lax.fori_loop(0, nh, weight_grads, 0)
    for f in range(nh):
        sg[f] = small[:, f * FS : (f + 1) * FS]
    for _, far in arrive:
        for c in far:
            c.wait_send()
    for c in sends:
        c.wait()


def reduce_kernel(
    nd, nh, experts, gw, sg, fg, sqe, gsum, ssum, norm,
    wc, ch, own, wr, zr, zs, szr, sdr, sqd, sqz, sdb, sqb,
    css, csr, dss, dsr, zss, zsr, ass, asr, bss, bsr, qss, qsr, rss, rsr
):
    n = lax.axis_index("dp")
    h = lax.axis_index("hid")
    core = lax.rem(n, 2)
    chip = lax.div(n, 2)
    chips = nd // 2
    zid = [lax.rem(h + k, nh) for k in range(1, nh)]
    zpeer = [{"hid": z} for z in zid]
    did = [lax.rem(n + k, nd) for k in range(1, nd)]
    dpeer = [{"dp": d} for d in did]
    greet(zpeer + dpeer)
    partner = {"dp": chip * 2 + 1 - core}
    first = remote(gw.at[:, :, 1 - core], wc, css.at[0], csr.at[0], partner)
    first.start()
    sz = [remote(sg.at[zid[k]], szr.at[k], ass.at[k], asr.at[k], zpeer[k]) for k in range(nh - 1)]
    for c in sz:
        c.start()
    for c in sz:
        c.wait_recv()
    small = sg[h]
    for k in range(nh - 1):
        small = small + szr[k]
    small = jnp.concatenate([small[0:8] + fg[...], small[8:]], 0)
    sdb[...] = small
    sd = [remote(sdb, sdr.at[k], bss.at[k], bsr.at[k], dpeer[k]) for k in range(nd - 1)]
    for c in sd:
        c.start()
    first.wait_recv()
    for hp in range(nh):
        ch[hp] = (gw[hp, :, core].astype(f32) + wc[hp].astype(f32)).astype(bf16)
    cid = [lax.rem(chip + k, chips) for k in range(1, chips)]
    second = [
        remote(ch.at[:, cid[k]], wr.at[k], dss.at[k], dsr.at[k], {"dp": cid[k] * 2 + core})
        for k in range(chips - 1)
    ]
    for c in second:
        c.start()
    for c in sd:
        c.wait_recv()
    for k in range(nd - 1):
        small = small + sdr[k]
    ssum[...] = small
    for c in second:
        c.wait_recv()
    total = ch[:, chip].astype(f32)
    for k in range(chips - 1):
        total = total + wr[k].astype(f32)
    zs[...] = total.astype(bf16)
    third = [
        remote(zs.at[zid[k]], zr.at[k], zss.at[k], zsr.at[k], zpeer[k]) for k in range(nh - 1)
    ]
    for c in third:
        c.start()
    for c in third:
        c.wait_recv()
    block = zs[h].astype(f32)
    for k in range(nh - 1):
        block = block + zr[k].astype(f32)
    gsum[...] = block
    squares = sqe[...]
    for f in range(nh):
        part = block[:, f * FS : (f + 1) * FS]
        squares = squares + jnp.sum((part * part).reshape(part.shape[0] // 8, 8, FS), 0)
    both = jnp.sum((small * small).reshape(small.shape[0] // 8, 8, FS), 0)
    squares = squares + jnp.where(n == 0, both, 0.0)
    sqb[0] = squares
    qd = [remote(sqb.at[0], sqd.at[k], qss.at[k], qsr.at[k], dpeer[k]) for k in range(nd - 1)]
    for c in qd:
        c.start()
    for c in qd:
        c.wait_recv()
    for k in range(nd - 1):
        squares = squares + sqd[k]
    sqb[1] = squares
    qz = [remote(sqb.at[1], sqz.at[k], rss.at[k], rsr.at[k], zpeer[k]) for k in range(nh - 1)]
    for c in qz:
        c.start()
    for c in qz:
        c.wait_recv()
    for k in range(nh - 1):
        squares = squares + sqz[k]
    everything = jnp.sum(jnp.sum(squares, 1, keepdims=True), 0, keepdims=True)
    norm[...] = jnp.broadcast_to(jnp.sqrt(everything), norm.shape)
    for c in [first] + sz + sd + second + third + qd + qz:
        c.wait_send()


def call(kernel, cid, outs, scratch, ins, out_specs=None, limit=60, pack=None):
    shapes = [jax.ShapeDtypeStruct(s, t) for s, t in outs]
    specs = out_specs or [VM] * len(outs)
    if pack is not None:
        shapes = shapes[: pack[0]] + [shapes[pack[0] :]]
        specs = specs[: pack[0]] + [specs[pack[0] :]]
    result = pl.pallas_call(
        kernel,
        out_shape=shapes,
        in_specs=[spec for spec, _ in ins],
        out_specs=specs,
        scratch_shapes=scratch,
        compiler_params=pltpu.CompilerParams(
            collective_id=cid, has_side_effects=True, vmem_limit_bytes=limit * 2**20
        ),
    )(*[value for _, value in ins])
    if pack is not None:
        result = list(result[: pack[0]]) + list(result[pack[0]])
    return result


def adam_update(weight, grad, first, second, rate, factor):
    clipped = grad * factor
    first_new = beta_first * first + (1.0 - beta_first) * clipped
    second_new = beta_second * second + (1.0 - beta_second) * clipped * clipped
    first_hat = first_new / (1.0 - beta_first**STEP)
    second_hat = second_new / (1.0 - beta_second**STEP)
    weight_new = weight - rate * (
        first_hat / (jnp.sqrt(second_hat) + adam_epsilon) + weight_decay * weight
    )
    return (first_new, second_new, weight_new)


def shards(
    tokens,
    seq_count,
    out_grad,
    norm_params,
    norm_first,
    norm_second,
    controller_weight,
    router_first,
    router_second,
    attn_in,
    attn_in_first,
    attn_in_second,
    attn_in_average,
    attn_out,
    attn_out_first,
    attn_out_second,
    attn_out_average,
    expert_in,
    expert_in_first,
    expert_in_second,
    expert_in_average,
    expert_out,
    expert_out_first,
    expert_out_second,
    expert_out_average,
):
    ema_keep = (1.0 + STEP) / (10.0 + STEP)
    nd = lax.axis_size("dp")
    nh = lax.axis_size("hid")
    chips = nd // 2
    slots, seq, _ = tokens.shape
    experts = controller_weight.shape[1]
    r = attn_in.shape[0]
    el = experts * GB
    groups = seq * slots // GROUP
    blocks = seq // BLK
    hidden = expert_in.shape[2]
    er = 8 + experts
    wblk = jnp.concatenate([attn_in.reshape(r, 3 * FS), attn_out], 1).astype(bf16)
    pblk = jnp.concatenate([norm_params, jnp.zeros((4, FS), f32), controller_weight.T], 0)
    z3 = nh - 1

    etypes = [((nh, (b + 1) * BLK, 2 * BLK), bf16) for b in range(blocks)]
    slices = ((nh, seq, FS), bf16)
    wtype = ((nh, chips, 2, r, D), bf16)
    qtype = ((nh, seq, 3 * FS), bf16)
    ttype = ((nh, FS, seq), bf16)
    rtype = ((nh, seq, FS), f32)
    htype = ((seq, D), f32)
    stype = ((nh, er, seq), f32)
    ptype = ((nh, er, FS), f32)
    ytype = ((nd, 2, groups, FS), bf16)
    gtype = ((groups // GB, GB * GROUP, el), bf16)

    def vmem(*types):
        return [pltpu.VMEM(*t) for t in types]

    x, w, p, qkv, kt, heads, recip, h1, h1f, stf, *es = call(
        functools.partial(forward_kernel, nd, nh, experts),
        1,
        [slices, wtype, ptype, qtype, ttype, slices, rtype, htype, slices, stype] + etypes,
        vmem(slices, wtype, qtype, ttype, slices, rtype, htype)
        + vmem(((BLK, D), bf16), ttype)
        + [vmem(*etypes)]
        + vmem(slices, ((er, seq), f32), ((2, FS, D), f32))
        + [DMA((blocks, z3))] * 2
        + [DMA((z3,))] * 2
        + [DMA((nh, chips - 1))] * 2
        + [DMA((1,))] * 2
        + [DMA((z3,))] * 2
        + [DMA((blocks, z3))] * 4
        + [DMA((4,)), DMA((blocks, 6)), DMA((blocks, 2)), DMA((blocks,))],
        [(VM, tokens), (VM, wblk), (VM, pblk)],
        [HB, HB, VM, HB, HB, HB, HB, HB, VM, VM] + [HB] * blocks,
        pack=(10, blocks),
    )
    gates, yin, g_in, g_out, sqe = call(
        functools.partial(expert_kernel, nd, nh, experts),
        2,
        [gtype, ytype, ((D, hidden), f32), ((hidden, D), f32), ((8, FS), f32)],
        vmem(
            ytype,
            ((nh, nd, 2, groups, FS), bf16),
            ((nd, groups, hidden), bf16),
            ((nd, groups, hidden), bf16),
            ((nh, nh, 2, groups, FS), bf16),
            ((nd, nh, 2, groups, FS), bf16),
            ((nd, nh, 2, groups, FS), bf16),
            ytype,
            ((2, D, D), f32),
            ((D, hidden), bf16),
            ((hidden, D), bf16),
        )
        + [DMA((nd,))] * 2
        + [DMA((nd, z3))] * 4
        + [DMA((nd, nh))] * 4
        + [DMA((nd,))] * 2
        + [DMA((4,))],
        [
            (SM, seq_count),
            (VM, h1f),
            (VM, stf),
            (VM, out_grad),
            (VM, norm_params),
            (HB, expert_in[0]),
            (HB, expert_out[0]),
        ],
    )
    block_out, fg, tgf, gw, sg = call(
        functools.partial(backward_kernel, nh, experts),
        3,
        [slices, ((8, FS), f32), slices, wtype, ptype],
        vmem(slices, stype, slices, stype)
        + vmem(slices, wtype, qtype, ttype, slices, rtype, htype)
        + vmem(
            ((seq, D), bf16),
            rtype,
            rtype,
            qtype,
            ((seq, D), bf16),
            slices,
            ((2, FS, D), f32),
            ((er, D), f32),
        )
        + [vmem(*etypes)]
        + [DMA((blocks, z3))] * 6
        + [DMA((blocks,)), DMA((blocks, 2)), DMA((7,)), DMA((blocks,))],
        [(SM, seq_count)]
        + [(VM, v) for v in (h1f, stf, out_grad, norm_params, gates, yin, p)]
        + [(HB, v) for v in (x, w, qkv, kt, heads, recip, h1)]
        + [([HB] * blocks, list(es))],
    )
    gsum, ssum, norm = call(
        functools.partial(reduce_kernel, nd, nh, experts),
        4,
        [((r, D), f32), ((er, FS), f32), ((8, FS), f32)],
        [
            pltpu.VMEM((nh, chips, r, D), bf16),
            pltpu.VMEM((nh, chips, r, D), bf16),
            pltpu.VMEM((8, FS), f32),
            pltpu.VMEM((chips - 1, nh, r, D), bf16),
            pltpu.VMEM((z3, r, D), bf16),
            pltpu.VMEM((nh, r, D), bf16),
            pltpu.VMEM((z3, er, FS), f32),
            pltpu.VMEM((nd - 1, er, FS), f32),
            pltpu.VMEM((nd - 1, 8, FS), f32),
            pltpu.VMEM((z3, 8, FS), f32),
            pltpu.VMEM((er, FS), f32),
            pltpu.VMEM((2, 8, FS), f32),
        ]
        + [DMA((1,))] * 2
        + [DMA((chips - 1,))] * 2
        + [DMA((z3,))] * 4
        + [DMA((nd - 1,))] * 4
        + [DMA((z3,))] * 2,
        [(VM, gw), (VM, sg), (VM, fg), (VM, sqe)],
    )
    grad_norm = norm[0, 0]
    tokens_grad = tgf.astype(f32)
    attn_in_sum = gsum[:, : 3 * FS].reshape(attn_in.shape)
    attn_out_sum = gsum[:, 3 * FS :]
    norm_sum = ssum[0:4]
    router_sum = ssum[8:].T
    expert_in_sum = g_in[None]
    expert_out_sum = g_out[None]
    factor = jnp.minimum(1.0, clip_limit / grad_norm)
    norm_up = adam_update(norm_params, norm_sum, norm_first, norm_second, 0.6, factor)
    router_up = adam_update(
        controller_weight, router_sum, router_first, router_second, (4 * D) ** (-0.5), factor
    )
    attn_in_up = adam_update(
        attn_in, attn_in_sum, attn_in_first, attn_in_second, 0.5 * D ** (-0.5), factor
    )
    attn_out_up = adam_update(
        attn_out,
        attn_out_sum,
        attn_out_first,
        attn_out_second,
        0.5 * (HEADS * HS // 16) ** (-0.5),
        factor,
    )
    expert_in_up = adam_update(
        expert_in,
        expert_in_sum,
        expert_in_first,
        expert_in_second,
        2.5 * (D // GROUP) ** (-0.5),
        factor,
    )
    expert_out_up = adam_update(
        expert_out, expert_out_sum, expert_out_first, expert_out_second, 0.5 * H ** (-0.5), factor
    )
    return (
        block_out,
        tokens_grad,
        grad_norm,
        norm_up[0],
        norm_up[1],
        norm_up[2],
        router_up[0],
        router_up[1],
        router_up[2],
        attn_in_up[0],
        attn_in_up[1],
        attn_in_up[2],
        ema_keep * attn_in_average + (1.0 - ema_keep) * attn_in_up[2],
        attn_out_up[0],
        attn_out_up[1],
        attn_out_up[2],
        ema_keep * attn_out_average + (1.0 - ema_keep) * attn_out_up[2],
        expert_in_up[0],
        expert_in_up[1],
        expert_in_up[2],
        ema_keep * expert_in_average + (1.0 - ema_keep) * expert_in_up[2],
        expert_out_up[0],
        expert_out_up[1],
        expert_out_up[2],
        ema_keep * expert_out_average + (1.0 - ema_keep) * expert_out_up[2],
    )


def solution(mesh):
    return jax.shard_map(
        shards,
        mesh=mesh,
        in_specs=(
            P("dp", None, "hid"),
            P("dp"),
            P("dp", None, "hid"),
            P(None, "hid"),
            P(None, "hid"),
            P(None, "hid"),
            P("hid", None),
            P("hid", None),
            P("hid", None),
            P("dp", None, "hid"),
            P("dp", None, "hid"),
            P("dp", None, "hid"),
            P("dp", None, "hid"),
            P("dp", "hid"),
            P("dp", "hid"),
            P("dp", "hid"),
            P("dp", "hid"),
            P("dp", None, "hid"),
            P("dp", None, "hid"),
            P("dp", None, "hid"),
            P("dp", None, "hid"),
            P("dp", "hid", None),
            P("dp", "hid", None),
            P("dp", "hid", None),
            P("dp", "hid", None),
        ),
        out_specs=(
            P("dp", None, "hid"),
            P("dp", None, "hid"),
            P(),
            P(None, "hid"),
            P(None, "hid"),
            P(None, "hid"),
            P("hid", None),
            P("hid", None),
            P("hid", None),
            P("dp", None, "hid"),
            P("dp", None, "hid"),
            P("dp", None, "hid"),
            P("dp", None, "hid"),
            P("dp", "hid"),
            P("dp", "hid"),
            P("dp", "hid"),
            P("dp", "hid"),
            P("dp", None, "hid"),
            P("dp", None, "hid"),
            P("dp", None, "hid"),
            P("dp", None, "hid"),
            P("dp", "hid", None),
            P("dp", "hid", None),
            P("dp", "hid", None),
            P("dp", "hid", None),
        ),
        check_vma=False,
    )
```

```python
import functools

import jax
import jax.numpy as jnp
from jax import lax
from jax.experimental import pallas as pl
from jax.experimental.pallas import tpu as pltpu
from jax.sharding import PartitionSpec as P

D = 512
HEADS = 8
HS = 64
H = 2048
GROUP = 32
STEP = 10
BLK = 256
FS = 128
GB = 16

norm_epsilon = 1e-05
fill_value = -1e30
clip_limit = 1.0
beta_first = 0.9
beta_second = 0.95
adam_epsilon = 1e-08
weight_decay = 0.1

f32 = jnp.float32
bf16 = jnp.bfloat16
MESH = pl.DeviceIdType.MESH
EXACT = lax.Precision.HIGHEST
VM = pl.BlockSpec(memory_space=pltpu.VMEM)
HB = pl.BlockSpec(memory_space=pl.ANY)
SM = pl.BlockSpec(memory_space=pltpu.SMEM)
DMA = pltpu.SemaphoreType.DMA


def dot(a, b, precision=None):
    return lax.dot_general(
        a, b, (((1,), (0,)), ((), ())), precision=precision, preferred_element_type=f32
    )


def dot_last(a, b, precision=None):
    return lax.dot_general(
        a, b, (((1,), (1,)), ((), ())), precision=precision, preferred_element_type=f32
    )


def dot_first(a, b, precision=None):
    return lax.dot_general(
        a, b, (((0,), (0,)), ((), ())), precision=precision, preferred_element_type=f32
    )


def greet(peers):
    barrier = pltpu.get_barrier_semaphore()
    for peer in peers:
        pl.semaphore_signal(barrier, inc=1, device_id=peer, device_id_type=MESH)
    pl.semaphore_wait(barrier, len(peers))


def remote(src, dst, send, recv, peer):
    return pltpu.make_async_remote_copy(
        src_ref=src, dst_ref=dst, send_sem=send, recv_sem=recv, device_id=peer, device_id_type=MESH
    )


def lanes(ref_like, index):
    return pl.ds(pl.multiple_of(index * ref_like, ref_like), ref_like)


def features(ref, rows):
    return jnp.concatenate([ref[f, rows, :] for f in range(ref.shape[0])], axis=1)


def row_of(ref, row):
    return jnp.concatenate([ref[f, row : row + 1, :] for f in range(ref.shape[0])], axis=1)


def split(v):
    high = v.astype(bf16)
    return high, (v - high.astype(f32)).astype(bf16)


def split3(v):
    high, _ = split(v)
    rest = v - high.astype(f32)
    mid, low = split(rest)
    return high, mid, low


def iota(shape, dim):
    return lax.broadcasted_iota(jnp.int32, shape, dim)


def standardize(v):
    center = jnp.sum(v, -1, keepdims=True) / v.shape[-1]
    dev = v - center
    inv = lax.rsqrt(jnp.sum(dev * dev, -1, keepdims=True) / v.shape[-1] + norm_epsilon)
    return dev * inv, center, inv


def controller_rows(p, pad, experts):
    pad[...] = jnp.zeros_like(pad)
    for f in range(p.shape[0]):
        high, low = split(p[f, 8 : 8 + experts, :])
        pad[0, 0:experts, f * FS : (f + 1) * FS] = high.astype(f32)
        pad[1, 0:experts, f * FS : (f + 1) * FS] = low.astype(f32)


def both_heads(v):
    low = iota(v.shape, 1) < HS
    zero = jnp.zeros_like(v)
    return jnp.concatenate([jnp.where(low, v, zero), jnp.where(low, zero, v)], 0)


def forward_kernel(
    nd, nh, experts, tok, wblk, pblk,
    xo, wout, p, qkvo, kto, headso, recipo, h1o, h1f, stf, eouts,
    x, w, qkv, kt, heads, recip, h1, a1, vt, es, h1b, st, pad,
    tss, tsr, wss, wsr, dss, dsr, css, csr, pss, psr, hss, hsr, sss, ssr, loc, esem, mine_sem, save
):
    n = lax.axis_index("dp")
    h = lax.axis_index("hid")
    core = lax.rem(n, 2)
    chip = lax.div(n, 2)
    chips = nd // 2
    seq = tok.shape[1]
    blocks = seq // BLK
    zpeer = [{"hid": lax.rem(h + k, nh)} for k in range(1, nh)]
    cpeer = [{"dp": lax.rem(chip + k, chips) * 2 + core} for k in range(1, chips)]
    partner = {"dp": chip * 2 + 1 - core}
    greet(zpeer + cpeer + [partner])
    locals_ = [
        pltpu.make_async_copy(wblk, w.at[h, chip, core], loc.at[0]),
        pltpu.make_async_copy(pblk, p.at[h], loc.at[1]),
        pltpu.make_async_copy(tok.at[h], x.at[h], loc.at[2]),
    ]
    for c in locals_:
        c.start()
    wz = [
        remote(wblk, w.at[h, chip, core], wss.at[k], wsr.at[k], zpeer[k]) for k in range(nh - 1)
    ]
    pz = [remote(pblk, p.at[h], pss.at[k], psr.at[k], zpeer[k]) for k in range(nh - 1)]
    for c in wz + pz:
        c.start()
    tz = []
    for b in range(blocks):
        rows = pl.ds(b * BLK, BLK)
        for k in range(nh - 1):
            c = remote(
                tok.at[lax.rem(h + k + 1, nh), rows],
                x.at[h, rows],
                tss.at[b, k],
                tsr.at[b, k],
                zpeer[k],
            )
            c.start()
            tz.append(c)
    locals_[0].wait()
    wc = []
    for j in range(nh):
        piece = lax.rem(h - j + nh, nh)
        if j > 0:
            wz[j - 1].wait_recv()
        for k in range(chips - 1):
            c = remote(
                w.at[piece, chip, core], w.at[piece, chip, core],
                dss.at[j, k], dsr.at[j, k], cpeer[k]
            )
            c.start()
            wc.append(c)
    for c in pz + wc:
        c.wait_recv()
    wp = remote(w.at[:, :, core], w.at[:, :, core], css.at[0], csr.at[0], partner)
    wp.start()
    for c in locals_[1:]:
        c.wait()
    controller_rows(p, pad, experts)
    gain1 = row_of(p, 0)
    bias1 = row_of(p, 1)
    gain2 = row_of(p, 2)
    bias2 = row_of(p, 3)
    scale = jnp.where(iota((BLK, 3 * FS), 1) < FS, HS**-0.5, 1.0).astype(bf16)
    lane = iota((BLK, FS), 1)
    low_half = lane < HS
    causal = iota((BLK, 2 * BLK), 0) <= (iota((BLK, 2 * BLK), 1) & (BLK - 1))
    one = jnp.ones((FS, BLK), bf16)
    low_rows = iota((FS, BLK), 0) < HS
    sends = []
    for b in range(blocks):
        rows = pl.ds(b * BLK, BLK)
        past = b * BLK
        e_ref = es[b]
        for k in range(nh - 1):
            tz[b * (nh - 1) + k].wait_recv()
        normed, _, _ = standardize(features(x, rows).astype(f32))
        a1[...] = (normed * gain1 + bias1).astype(bf16)
        if b == 0:
            wp.wait_recv()
            c = pltpu.make_async_copy(w, wout, loc.at[3])
            c.start()
            sends.append(c)

        def pair(hp, carry):
            proj = dot(a1[...], w[hp].reshape(D, D)[:, : 3 * FS])
            low = proj.astype(bf16) * scale
            qkv[hp, rows, :] = low
            kt[hp, :, rows] = proj[:, FS : 2 * FS].T.astype(bf16)
            vt[hp, :, rows] = proj[:, 2 * FS :].T.astype(bf16)
            q = both_heads(low[:, :FS])
            s_now = dot_last(low[:, FS : 2 * FS], q)
            s_now = jnp.where(causal, s_now, fill_value)
            peak = jnp.max(s_now, 0, keepdims=True)
            if b > 0:
                s_past = dot_last(qkv[hp, 0:past, FS : 2 * FS], q)
                peak = jnp.maximum(peak, jnp.max(s_past, 0, keepdims=True))
                e_ref[hp, 0:past, :] = jnp.exp(s_past - peak).astype(bf16)
            e_ref[hp, past : past + BLK, :] = jnp.exp(s_now - peak).astype(bf16)
            outs = []
            for half in range(2):
                total = jnp.zeros((FS, BLK), f32)
                for j in range(b + 1):
                    keys = slice(j * BLK, (j + 1) * BLK)
                    v = vt[hp, :, keys]
                    v = jnp.where(low_rows, v, one) if half == 0 else jnp.where(low_rows, one, v)
                    total = total + dot(v, e_ref[hp, keys, half * BLK : (half + 1) * BLK])
                outs.append(total.T)
            value = jnp.where(low_half, outs[0], outs[1])
            total = jnp.where(low_half, pltpu.roll(outs[0], HS, 1), pltpu.roll(outs[1], HS, 1))
            inv = 1.0 / total
            recip[hp, rows, :] = inv
            heads[hp, rows, :] = (value * inv).astype(bf16)
            return carry

        lax.fori_loop(0, nh, pair, 0)
        saves = [
            (e_ref, eouts[b]),
            (x.at[:, rows], xo.at[:, rows]),
            (qkv.at[:, rows], qkvo.at[:, rows]),
            (kt.at[:, :, rows], kto.at[:, :, rows]),
            (heads.at[:, rows], headso.at[:, rows]),
            (recip.at[:, rows], recipo.at[:, rows]),
        ]
        for k, (src, dst) in enumerate(saves):
            c = pltpu.make_async_copy(src, dst, esem.at[b, k])
            c.start()
            sends.append(c)
        attn = jnp.zeros((BLK, D), f32)
        for hp in range(nh):
            attn = attn + dot_last(heads[hp, rows, :], w[hp].reshape(D, D)[:, 3 * FS :])
        hidden = features(x, rows).astype(f32) + attn
        h1[rows, :] = hidden
        c = pltpu.make_async_copy(h1.at[rows], h1o.at[rows], save.at[b])
        c.start()
        sends.append(c)
        normed, center, inv = standardize(hidden)
        u = normed * gain2 + bias2
        uh, ul = split(u)
        cols = dot_last(
            jnp.concatenate([uh, ul, uh], 1),
            jnp.concatenate([pad[0], pad[0], pad[1]], 1).astype(bf16),
        )
        cols = jnp.where(lane == experts, center, jnp.where(lane == experts + 1, inv, cols))
        st[:, rows] = cols.T[0 : experts + 8, :]
        for f in range(nh):
            h1b[f, rows, :] = hidden[:, f * FS : (f + 1) * FS].astype(bf16)
        mine = [
            pltpu.make_async_copy(h1b.at[h, rows], h1f.at[h, rows], mine_sem.at[b, 0]),
            pltpu.make_async_copy(st.at[:, rows], stf.at[h, :, rows], mine_sem.at[b, 1]),
        ]
        for c in mine:
            c.start()
        for k in range(nh - 1):
            c = remote(
                h1b.at[lax.rem(h + k + 1, nh), rows],
                h1f.at[h, rows],
                hss.at[b, k],
                hsr.at[b, k],
                zpeer[k],
            )
            s = remote(
                st.at[:, rows], stf.at[h, :, rows], sss.at[b, k], ssr.at[b, k], zpeer[k]
            )
            c.start()
            s.start()
            sends += [c, s]
        sends += mine
    for c in sends:
        c.wait()
    for c in wz + pz + tz + wc + [wp]:
        c.wait_send()


def expand(stb, experts, el, gates):
    height = stb.shape[1]
    width = (el if gates else 0) + 2 * FS
    rows = iota((3 * height, width), 0)
    cols = iota((3 * height, width), 1)
    rows = jnp.where(rows >= 2 * height, rows - 2 * height, rows)
    rows = jnp.where(rows >= height, rows - height, rows)
    base = el if gates else 0
    target = jnp.where(cols < base + FS, experts, experts + 1)
    if gates:
        target = jnp.where(cols < el, lax.shift_right_logical(cols, 4), target)
    pick = jnp.where(rows == target, 1.0, 0.0).astype(bf16)
    return [
        dot_first(jnp.concatenate(split3(stb[s]), 0), pick) for s in range(stb.shape[0])
    ]


def own_group(tokens, el):
    group = lax.shift_right_logical(iota((tokens, el), 0), 3) & (GB - 1)
    return (iota((tokens, el), 1) & (GB - 1)) == group


def block_values(h1f, og, gain, bias, live, rows, mean, inv):
    slots = h1f.shape[0]
    nhat, u, dy, hid = [], [], [], []
    for s in range(slots):
        hidden = h1f[s, rows, :].astype(f32)
        hat = (hidden - mean[s]) * inv[s]
        nhat.append(hat)
        u.append((hat * gain + bias).astype(bf16))
        hid.append(hidden)
        grad = og[s, rows, :]
        dy.append(jnp.where(s < live, grad, jnp.zeros_like(grad)))
    return nhat, u, dy, hid


def expert_kernel(
    nd, nh, experts, count, h1f, stf, og, npar, win, wout, gates, yin, g_in, g_out, sq,
    mout, xz, act, dpre, ps, inl, inr, yo, wf, wi, wo,
    dss, dsr, xsr, xsl, xrl, xrr, isr, isl, irl, irr, yss, ysr, loc
):
    n = lax.axis_index("dp")
    h = lax.axis_index("hid")
    seq = h1f.shape[1]
    slots = h1f.shape[0]
    el = experts * GB
    span = GB * GROUP // slots
    top = nh - 1
    right = {"hid": jnp.minimum(h + 1, top)}
    left = {"hid": jnp.maximum(h - 1, 0)}
    weights = [
        pltpu.make_async_copy(win, wf.at[0], loc.at[0]),
        pltpu.make_async_copy(wout, wf.at[1], loc.at[1]),
    ]
    for c in weights:
        c.start()
    greet([{"hid": lax.rem(h + k, nh)} for k in range(1, nh)] + [
        {"dp": lax.rem(n + k, nd)} for k in range(1, nd)
    ])
    live = count[0]
    gain = npar[2:3, :]
    bias = npar[3:4, :]
    mask = own_group(slots * span, el)

    def gate_block(b, carry):
        rows = pl.ds(pl.multiple_of(b * span, span), span)
        grows = pl.ds(pl.multiple_of(b * GB, GB), GB)
        spread = expand(stf[:, :, rows], experts, el, True)
        logits = jnp.stack(
            [jnp.where(s < live, spread[s][:, :el], fill_value) for s in range(slots)]
        ).reshape(slots, GB, span // GB, el)
        peak = jnp.max(logits, axis=(0, 2), keepdims=True)
        e = jnp.exp(logits - peak)
        gate = e / jnp.sum(e, axis=(0, 2), keepdims=True)
        gate = jnp.where(mask, gate.reshape(slots * span, el), 0.0).astype(bf16)
        gates[b] = gate
        mean = [v[:, el : el + FS] for v in spread]
        inv = [v[:, el + FS :] for v in spread]
        _, u, dy, _ = block_values(h1f, og, gain, bias, live, rows, mean, inv)
        both = jnp.concatenate([jnp.concatenate(u, 0), jnp.concatenate(dy, 0)], 1)
        mixed = dot_first(gate, both).astype(bf16)
        mout[:, 0, grows, :] = mixed[:, :FS].reshape(experts, GB, FS)
        mout[:, 1, grows, :] = mixed[:, FS:].reshape(experts, GB, FS)
        return carry

    lax.fori_loop(0, seq // span, gate_block, 0)

    def source(k):
        return lax.rem(n - k + nd, nd)

    def to_expert(k):
        e = lax.rem(n + k, nd)
        return remote(mout.at[e], xz.at[h, n], dss.at[k], dsr.at[k], {"dp": e})

    def go_right(k, j):
        piece = xz.at[jnp.maximum(h - j, 0), source(k)]
        return remote(piece, piece, xsr.at[k, j], xrl.at[k, j], right)

    def go_left(k, j):
        piece = xz.at[jnp.minimum(h + j, top), source(k)]
        return remote(piece, piece, xsl.at[k, j], xrr.at[k, j], left)

    def sum_right(k, d):
        piece = inl.at[k, jnp.minimum(h + d, top)]
        return remote(piece, piece, isr.at[k, d], irl.at[k, d - 1], right)

    def sum_left(k, d):
        piece = inr.at[k, jnp.maximum(h - d, 0)]
        return remote(piece, piece, isl.at[k, d], irr.at[k, d - 1], left)

    def from_left(k, d):
        piece = inl.at[k, jnp.minimum(h + d, top)]
        return remote(piece, piece, isr.at[k, d], irl.at[k, d], right)

    def from_right(k, d):
        piece = inr.at[k, jnp.maximum(h - d, 0)]
        return remote(piece, piece, isl.at[k, d], irr.at[k, d], left)

    def to_home(k):
        src = source(k)
        return remote(yo.at[k], yin.at[n], yss.at[k], ysr.at[k], {"dp": src})

    own = pltpu.make_async_copy(mout.at[n], xz.at[h, n], loc.at[2])
    own.start()

    def start_expert(k, carry):
        to_expert(k).start()
        return carry

    lax.fori_loop(1, nd, start_expert, 0)
    for c in weights:
        c.wait()
    wi[...] = wf[0].astype(bf16)
    wo[...] = wf[1].astype(bf16)
    own.wait()

    def expert(k):
        src = source(k)
        slot = lax.rem(k, nh)
        mixed = jnp.concatenate([xz[f, src, 0] for f in range(nh)], axis=1)
        drows = jnp.concatenate([xz[f, src, 1] for f in range(nh)], axis=1)
        pre = dot(mixed, wi[...])
        cube = 0.7978845608028654
        t = jnp.tanh(cube * (pre + 0.044715 * (pre * pre * pre)))
        a = (0.5 * pre * (1.0 + t)).astype(bf16)
        slope = 0.5 * (1.0 + t) + 0.5 * pre * (1.0 - t * t) * (
            cube * (1.0 + 3.0 * 0.044715 * (pre * pre))
        )
        rows = dot(a, wo[...])
        d = (dot_last(drows, wo[...]) * slope).astype(bf16)
        dmix = dot_last(d, wi[...])
        act[src] = a
        dpre[src] = d
        for f in range(nh):
            ps[slot, f, 0] = rows[:, f * FS : (f + 1) * FS].astype(bf16)
            ps[slot, f, 1] = dmix[:, f * FS : (f + 1) * FS].astype(bf16)

    def step(t, carry):
        @pl.when(t < nd)
        def _():
            @pl.when(t > 0)
            def _():
                to_expert(t).wait_recv()

            @pl.when(h < top)
            def _():
                go_right(t, 0).start()

            @pl.when(h > 0)
            def _():
                go_left(t, 0).start()

        for j in range(1, nh):
            k = t - j
            here = jnp.logical_and(k >= 0, k < nd)

            @pl.when(jnp.logical_and(here, h >= j))
            def _(k=k, j=j):
                go_right(k, j - 1).wait_recv()
                if j < top:

                    @pl.when(h < top)
                    def _():
                        go_right(k, j).start()

            @pl.when(jnp.logical_and(here, h + j <= top))
            def _(k=k, j=j):
                go_left(k, j - 1).wait_recv()
                if j < top:

                    @pl.when(h > 0)
                    def _():
                        go_left(k, j).start()

        ke = t - top

        @pl.when(jnp.logical_and(ke >= 0, ke < nd))
        def _():
            expert(ke)

        kr = t - top - h

        @pl.when(jnp.logical_and(kr >= 0, kr < nd))
        def _():
            slot = lax.rem(kr, nh)
            for d in range(nh):

                @pl.when(h + d <= top)
                def _(d=d):
                    dest = jnp.minimum(h + d, top)

                    @pl.when(h > 0)
                    def _():
                        from_left(kr, d).wait_recv()
                        if d > 0:
                            value = inl[kr, dest].astype(f32) + ps[slot, dest].astype(f32)
                            inl[kr, dest] = value.astype(bf16)

                    if d > 0:

                        @pl.when(h == 0)
                        def _():
                            inl[kr, dest] = ps[slot, dest]

                        sum_right(kr, d).start()

        kl = t - top - (top - h)

        @pl.when(jnp.logical_and(kl >= 0, kl < nd))
        def _():
            slot = lax.rem(kl, nh)
            for d in range(nh):

                @pl.when(h - d >= 0)
                def _(d=d):
                    dest = jnp.maximum(h - d, 0)

                    @pl.when(h < top)
                    def _():
                        from_right(kl, d).wait_recv()
                        if d > 0:
                            value = inr[kl, dest].astype(f32) + ps[slot, dest].astype(f32)
                            inr[kl, dest] = value.astype(bf16)

                    if d > 0:

                        @pl.when(h == top)
                        def _():
                            inr[kl, dest] = ps[slot, dest]

                        sum_left(kl, d).start()

        kf = t - 2 * top

        @pl.when(kf >= 0)
        def _():
            slot = lax.rem(kf, nh)

            @pl.when(h == 0)
            def _():
                yo[kf] = (ps[slot, h].astype(f32) + inr[kf, h].astype(f32)).astype(bf16)

            @pl.when(h == top)
            def _():
                yo[kf] = (ps[slot, h].astype(f32) + inl[kf, h].astype(f32)).astype(bf16)

            @pl.when(jnp.logical_and(h > 0, h < top))
            def _():
                value = ps[slot, h].astype(f32) + inl[kf, h].astype(f32)
                yo[kf] = (value + inr[kf, h].astype(f32)).astype(bf16)

            @pl.when(kf > 0)
            def _():
                to_home(kf).start()

        return carry

    lax.fori_loop(0, nd + 2 * top, step, 0)
    mine = pltpu.make_async_copy(yo.at[0], yin.at[n], loc.at[3])
    mine.start()
    total = nd * act.shape[1]
    squares = jnp.zeros((8, FS), f32)
    a_all = act[...].reshape(total, act.shape[2])
    d_all = dpre[...].reshape(total, dpre.shape[2])
    for f in range(nh):
        cols = pl.ds(f * FS, FS)
        gi = dot_first(xz[f, :, 0].reshape(total, FS), d_all)
        go = dot_first(a_all, xz[f, :, 1].reshape(total, FS))
        g_in[cols, :] = gi
        g_out[:, cols] = go
        for m in range(nh):
            part = gi[:, m * FS : (m + 1) * FS]
            squares = squares + jnp.sum((part * part).reshape(FS // 8, 8, FS), 0)
        squares = squares + jnp.sum((go * go).reshape(D // 8, 8, FS), 0)
    sq[...] = squares

    def finish(k, carry):
        @pl.when(k > 0)
        def _():
            to_expert(k).wait_send()
            to_home(k).wait()

        for j in range(top):

            @pl.when(jnp.logical_and(h < top, h >= j))
            def _(j=j):
                go_right(k, j).wait_send()

            @pl.when(jnp.logical_and(h > 0, h + j <= top))
            def _(j=j):
                go_left(k, j).wait_send()

        for d in range(1, nh):

            @pl.when(h + d <= top)
            def _(d=d):
                sum_right(k, d).wait_send()

            @pl.when(h - d >= 0)
            def _(d=d):
                sum_left(k, d).wait_send()

        return carry

    lax.fori_loop(0, nd, finish, 0)
    mine.wait()


def backward_kernel(
    nh, experts, count, h1f, stf, og, npar, gates, yin, p, xi, win, qkvi, kti, headsi, recipi, h1i,
    ein, block_out, fg, tgf, gw, sg,
    p1, py, p1s, pay, x, w, qkv, kt, heads, recip, h1, a1, dk, dv, dqkv, dattn, tgb, pad, small,
    es, pss, psr, sss, ssr, hss, hsr, loc, mloc, lsem, esem
):
    h = lax.axis_index("hid")
    seq = h1f.shape[1]
    slots = h1f.shape[0]
    blocks = seq // BLK
    el = experts * GB
    span = GB * GROUP // slots
    per = BLK // span
    zpeer = [{"hid": lax.rem(h + k, nh)} for k in range(1, nh)]
    held = [(xi, x), (win, w), (h1i, h1), (qkvi, qkv), (kti, kt), (headsi, heads), (recipi, recip)]
    held = [pltpu.make_async_copy(src, dst, lsem.at[i]) for i, (src, dst) in enumerate(held)]
    for c in held:
        c.start()
    loads = [pltpu.make_async_copy(ein[b], es[b], esem.at[b]) for b in range(blocks)]
    for c in reversed(loads):
        c.start()
    greet(zpeer)
    live = count[0]
    gain = npar[2:3, :]
    bias = npar[3:4, :]
    height = experts + 8
    srow = iota((height, el + 2 * FS), 0)
    scol = iota((height, el + 2 * FS), 1)
    target = jnp.where(scol < el, lax.shift_right_logical(scol, 4), experts)
    target = jnp.where(scol >= el + FS, experts + 1, target)
    fold = jnp.where(srow == target, 1.0, 0.0).astype(bf16)
    fold = jnp.concatenate([fold, fold], 1)
    fg[...] = jnp.zeros_like(fg)

    def back_block(b, carry):
        rows = pl.ds(pl.multiple_of(b * span, span), span)
        grows = pl.ds(pl.multiple_of(b * GB, GB), GB)
        spread = expand(stf[:, :, rows], experts, el, False)
        mean = [v[:, :FS] for v in spread]
        inv = [v[:, FS:] for v in spread]
        nhat, u, dy, hid = block_values(h1f, og, gain, bias, live, rows, mean, inv)
        y = jnp.concatenate(
            [yin[:, 0, grows, :].reshape(el, FS), yin[:, 1, grows, :].reshape(el, FS)], 1
        )
        gate = gates[b]
        bd = dot(gate, y)
        dgates = dot_last(
            jnp.concatenate([jnp.concatenate(dy, 0), jnp.concatenate(u, 0)], 1), y
        )
        gate = gate.astype(f32)
        gd = gate * dgates
        gd4 = gd.reshape(slots, GB, span // GB, el)
        inner = jnp.sum(gd4, axis=(0, 2), keepdims=True)
        dlog = gd4 - gate.reshape(slots, GB, span // GB, el) * inner
        dlog = dlog.reshape(slots * span, el)
        qs, qn = [], []
        acc_gain = jnp.zeros((1, FS), f32)
        acc_bias = jnp.zeros((1, FS), f32)
        for s in range(slots):
            part = slice(s * span, (s + 1) * span)
            back = bd[part, :FS]
            du = bd[part, FS:]
            block_out[s, rows, :] = jnp.where(s < live, hid[s] + back, 0.0).astype(bf16)
            q = du * gain
            p1[s, rows, :] = (dy[s].astype(f32) + inv[s] * q).astype(bf16)
            acc_gain = acc_gain + jnp.sum(du * nhat[s], 0, keepdims=True)
            acc_bias = acc_bias + jnp.sum(du, 0, keepdims=True)
            qs.append(q)
            qn.append(q * nhat[s])
        high, low = split(
            jnp.concatenate([dlog, jnp.concatenate(qs, 0), jnp.concatenate(qn, 0)], 1)
        )
        folded = dot_last(fold, jnp.concatenate([high, low], 1))
        for s in range(slots):
            py[s, :, rows] = folded[:, s * span : (s + 1) * span]
        fg[2:3, :] += acc_gain
        fg[3:4, :] += acc_bias
        return carry

    arrive = [None] * blocks
    sends = []
    for c in reversed(range(blocks)):
        lax.fori_loop(c * per, (c + 1) * per, back_block, 0)
        rows = pl.ds(c * BLK, BLK)
        mine = [
            pltpu.make_async_copy(p1.at[h, rows], p1s.at[h, rows], mloc.at[c, 0]),
            pltpu.make_async_copy(py.at[h, :, rows], pay.at[h, :, rows], mloc.at[c, 1]),
        ]
        for m in mine:
            m.start()
        far = []
        for k in range(nh - 1):
            peer = lax.rem(h + k + 1, nh)
            a = remote(p1.at[peer, rows], p1s.at[h, rows], pss.at[c, k], psr.at[c, k], zpeer[k])
            s = remote(
                py.at[peer, :, rows], pay.at[h, :, rows], sss.at[c, k], ssr.at[c, k], zpeer[k]
            )
            a.start()
            s.start()
            far += [a, s]
        arrive[c] = (mine, far)
    controller_rows(p, pad, experts)
    gain1 = row_of(p, 0)
    bias1 = row_of(p, 1)
    gain2 = row_of(p, 2)
    bias2 = row_of(p, 3)
    lane = iota((BLK, FS), 1)
    low_half = lane < HS
    er = iota((3 * height, FS), 0)
    er = jnp.where(er >= 2 * height, er - 2 * height, er)
    er = jnp.where(er >= height, er - height, er)
    eye = jnp.where(er == iota((3 * height, FS), 1), 1.0, 0.0).astype(bf16)
    pick = iota((8, 2 * FS), 1) & (FS - 1)
    row = iota((8, 2 * FS), 0)
    pick = ((row == 0) & (pick < HS)) | ((row == 1) & (pick >= HS))
    pick = jnp.where(pick, 1.0, 0.0).astype(bf16)
    small[...] = jnp.zeros_like(small)
    for c in held:
        c.wait()
    for b in reversed(range(blocks)):
        rows = pl.ds(b * BLK, BLK)
        last = b == blocks - 1
        e_ref = es[b]
        mine, far = arrive[b]
        for c in mine:
            c.wait()
        for c in far:
            c.wait_recv()
        total = pay[0, :, rows]
        for f in range(1, nh):
            total = total + pay[f, :, rows]
        cols = dot_first(jnp.concatenate(split3(total), 0), eye)
        s1 = cols[:, experts : experts + 1]
        s2 = cols[:, experts + 1 : experts + 2]
        hidden = h1[rows, :]
        nhat, _, inv = standardize(hidden)
        ch, cl = split(jnp.where(lane < experts, cols, 0.0))
        du = dot(
            jnp.concatenate([ch, cl, ch], 1),
            jnp.concatenate([pad[0], pad[0], pad[1]], 0).astype(bf16),
        )
        q = du * gain2
        mq = (s1 + jnp.sum(q, -1, keepdims=True)) / D
        mqn = (s2 + jnp.sum(q * nhat, -1, keepdims=True)) / D
        dh1 = features(p1s, rows).astype(f32) + inv * (q - mq - nhat * mqn)
        small[2:3, :] += jnp.sum(du * nhat, 0, keepdims=True)
        small[3:4, :] += jnp.sum(du, 0, keepdims=True)
        routed = dot_first(
            jnp.concatenate([ch, cl], 1), (nhat * gain2 + bias2).astype(bf16)
        )
        small[8 : 8 + experts, :] += routed[0:experts] + routed[FS : FS + experts]
        dattn[rows, :] = dh1.astype(bf16)
        loads[b].wait()

        def pair(hp, carry):
            dh = dot(dattn[rows, :], w[hp].reshape(D, D)[:, 3 * FS :]).astype(bf16).astype(f32)
            dh = dh * recip[hp, rows, :]
            high, rest = split(dh * heads[hp, rows, :].astype(f32))
            inner = dot_last(pick, jnp.concatenate([high, rest], 1))
            inner = jnp.concatenate([inner[0:1], inner[1:2]], 1)
            dhs = both_heads(dh.astype(bf16))
            qs = both_heads(qkv[hp, rows, 0:FS])
            dqt = jnp.zeros((FS, 2 * BLK), f32)
            for j in range(b + 1):
                keys = slice(j * BLK, (j + 1) * BLK)
                e = e_ref[hp, keys, :]
                dp = dot_last(qkv[hp, keys, 2 * FS :], dhs)
                ds = (e.astype(f32) * (dp - inner)).astype(bf16)
                dqt = dqt + dot(kt[hp, :, keys], ds)
                if last:
                    dk[hp, keys, :] = dot(ds, qs)
                    dv[hp, keys, :] = dot(e, dhs)
                else:
                    dk[hp, keys, :] += dot(ds, qs)
                    dv[hp, keys, :] += dot(e, dhs)
            dq = jnp.where(low_half, dqt[:, :BLK].T, dqt[:, BLK:].T)
            dqkv[hp, rows, 0:FS] = (dq * HS**-0.5).astype(bf16)
            dqkv[hp, rows, FS : 2 * FS] = dk[hp, rows, :].astype(bf16)
            dqkv[hp, rows, 2 * FS :] = dv[hp, rows, :].astype(bf16)
            return carry

        lax.fori_loop(0, nh, pair, 0)
        da1 = jnp.zeros((BLK, D), f32)
        for hp in range(nh):
            da1 = da1 + dot_last(dqkv[hp, rows, :], w[hp].reshape(D, D)[:, : 3 * FS])
        hat, _, inv1 = standardize(features(x, rows).astype(f32))
        a1[rows, :] = (hat * gain1 + bias1).astype(bf16)
        q1 = da1 * gain1
        m1 = jnp.sum(q1, -1, keepdims=True) / D
        m2 = jnp.sum(q1 * hat, -1, keepdims=True) / D
        tg = dh1 + inv1 * (q1 - m1 - hat * m2)
        small[0:1, :] += jnp.sum(da1 * hat, 0, keepdims=True)
        small[1:2, :] += jnp.sum(da1, 0, keepdims=True)
        for f in range(nh):
            tgb[f, rows, :] = tg[:, f * FS : (f + 1) * FS].astype(bf16)
        mine = pltpu.make_async_copy(tgb.at[h, rows], tgf.at[h, rows], loc.at[b])
        mine.start()
        sends.append(mine)
        for k in range(nh - 1):
            peer = lax.rem(h + k + 1, nh)
            c = remote(tgb.at[peer, rows], tgf.at[h, rows], hss.at[b, k], hsr.at[b, k], zpeer[k])
            c.start()
            sends.append(c)

    def weight_grads(hp, carry):
        gi = dot_first(a1[...], dqkv[hp]).astype(bf16)
        go = dot_first(dattn[...], heads[hp]).astype(bf16)
        gw[hp] = jnp.concatenate([gi, go], 1).reshape(gw.shape[1:])
        return carry

    lax.fori_loop(0, nh, weight_grads, 0)
    for f in range(nh):
        sg[f] = small[:, f * FS : (f + 1) * FS]
    for _, far in arrive:
        for c in far:
            c.wait_send()
    for c in sends:
        c.wait()


def block_kernel(
    nd, nh, experts, count, tok, attn_in, attn_out, npar, control, og_in, win, wout,
    block_out, tgf, g_in, g_out, gsum, ssum, norm,
    wblk, pblk, x, w, p, a1, qkv, kt, vt, heads, recip, h1, es, h1b, st, h1f, stf, og, gates, mout, xz,
    act, dpre, ps, inl, inr, yin, wi, wo, py, p1s, pay, dk, dv, dattn, pad, small,
    fg, sg, dacc, gwb, wc_in, ch, wr, zs, zr, szr, sdb, sdr, sqb, sqd, sqz,
    tss, tsr, wss, wsr, dss, dsr, css, csr, pss, psr, hss, hsr, sss, ssr,
    ess, esr, xsr, xsl, xrl, xrr, isr, isl, irl, irr, yss, ysr,
    bss, bsr, vss, vsr, gss, gsr, ass, asr, cts, ctr, zss, zsr, sms, smr, sns, snr,
    qss, qsr, rss, rsr, loc, hloc, ploc, gloc, wloc, oloc
):
    n = lax.axis_index("dp")
    h = lax.axis_index("hid")
    core = lax.rem(n, 2)
    chip = lax.div(n, 2)
    chips = nd // 2
    top = nh - 1
    slots, seq = h1f.shape[0], h1f.shape[1]
    blocks = seq // BLK
    el = experts * GB
    span = GB * GROUP // slots
    per = BLK // span
    right = {"hid": jnp.minimum(h + 1, top)}
    left = {"hid": jnp.maximum(h - 1, 0)}
    zid = [lax.rem(h + k, nh) for k in range(1, nh)]
    zpeer = [{"hid": z} for z in zid]
    did = [lax.rem(n + k, nd) for k in range(1, nd)]
    cid = [lax.rem(chip + k, chips) * 2 + core for k in range(1, chips)]
    partner = {"dp": chip * 2 + 1 - core}
    ends = []
    sent = []
    gathers = []
    scatters = []
    for m in range(3):
        wblk[:, m * FS : (m + 1) * FS] = attn_in[m].astype(bf16)
    wblk[:, 3 * FS :] = attn_out[...].astype(bf16)
    pblk[0:4, :] = npar[...]
    pblk[4:8, :] = jnp.zeros((4, FS), f32)
    pblk[8:, :] = control[...]

    def local(src, dst, sem):
        c = pltpu.make_async_copy(src, dst, sem)
        c.start()
        return c

    def far(src, dst, send, recv, peer):
        c = remote(src, dst, send, recv, peer)
        c.start()
        sent.append(c)
        return c

    og_load = local(og_in, og, loc.at[0])
    x_load = local(tok.at[h], x.at[h], loc.at[1])
    w_loads = []
    for f in range(nh):
        cols = pl.ds(f * FS, FS)
        w_loads.append(local(win.at[:, cols], dk.at[f, 0:D], wloc.at[f, 0]))
        w_loads.append(local(wout.at[:, cols], dk.at[f, D : 2 * D], wloc.at[f, 1]))
    greet(zpeer + [{"dp": d} for d in did])
    w_own = local(wblk, w.at[h, chip, core], loc.at[2])
    p_own = local(pblk, p.at[h], loc.at[3])
    wz = [
        far(wblk, w.at[h, chip, core], wss.at[k], wsr.at[k], zpeer[k]) for k in range(nh - 1)
    ]
    pz = [far(pblk, p.at[h], pss.at[k], psr.at[k], zpeer[k]) for k in range(nh - 1)]

    def rows_of(b):
        return pl.ds(b * BLK, BLK)

    def send_tokens(b):
        rows = rows_of(b)
        return [
            far(tok.at[zid[k], rows], x.at[h, rows], tss.at[b, k], tsr.at[b, k], zpeer[k])
            for k in range(nh - 1)
        ]

    tz = {b: send_tokens(b) for b in range(blocks)}
    w_own.wait()
    wc = []
    for j in range(nh):
        piece = lax.rem(h - j + nh, nh)
        if j > 0:
            wz[j - 1].wait_recv()
        part = w.at[piece, chip, core]
        wc.append(
            [far(part, part, dss.at[j, k], dsr.at[j, k], {"dp": cid[k]}) for k in range(chips - 1)]
        )
    p_own.wait()
    for c in pz:
        c.wait_recv()
    controller_rows(p, pad, experts)
    gain1 = row_of(p, 0)
    bias1 = row_of(p, 1)
    gain2 = row_of(p, 2)
    bias2 = row_of(p, 3)
    scale = jnp.where(iota((BLK, 3 * FS), 1) < FS, HS**-0.5, 1.0).astype(bf16)
    lane = iota((BLK, FS), 1)
    low_half = lane < HS
    causal = iota((BLK, 2 * BLK), 0) <= (iota((BLK, 2 * BLK), 1) & (BLK - 1))
    one = jnp.ones((FS, BLK), bf16)
    low_rows = iota((FS, BLK), 0) < HS
    wp = []

    def pass_weights(j):
        for c in wc[j]:
            c.wait_recv()
        part = w.at[lax.rem(h - j + nh, nh), :, core]
        wp.append(far(part, part, css.at[j], csr.at[j], partner))

    def begin(b):
        for c in tz[b]:
            c.wait_recv()
        normed, _, _ = standardize(features(x, rows_of(b)).astype(f32))
        a1[rows_of(b), :] = (normed * gain1 + bias1).astype(bf16)

    def attend(b, hp):
        rows = rows_of(b)
        past = b * BLK
        e_ref = es[b]
        proj = dot(a1[rows, :], w[hp].reshape(D, D)[:, : 3 * FS])
        low = proj.astype(bf16) * scale
        qkv[hp, rows, :] = low
        kt[hp, :, rows] = proj[:, FS : 2 * FS].T.astype(bf16)
        vt[hp, :, rows] = proj[:, 2 * FS :].T.astype(bf16)
        q = both_heads(low[:, :FS])
        s_now = dot_last(low[:, FS : 2 * FS], q)
        s_now = jnp.where(causal, s_now, fill_value)
        peak = jnp.max(s_now, 0, keepdims=True)
        if b > 0:
            s_past = dot_last(qkv[hp, 0:past, FS : 2 * FS], q)
            peak = jnp.maximum(peak, jnp.max(s_past, 0, keepdims=True))
            e_ref[hp, 0:past, :] = jnp.exp(s_past - peak).astype(bf16)
        e_ref[hp, past : past + BLK, :] = jnp.exp(s_now - peak).astype(bf16)
        outs = []
        for half in range(2):
            total = jnp.zeros((FS, BLK), f32)
            for j in range(b + 1):
                keys = slice(j * BLK, (j + 1) * BLK)
                v = vt[hp, :, keys]
                v = jnp.where(low_rows, v, one) if half == 0 else jnp.where(low_rows, one, v)
                total = total + dot(v, e_ref[hp, keys, half * BLK : (half + 1) * BLK])
            outs.append(total.T)
        value = jnp.where(low_half, outs[0], outs[1])
        total = jnp.where(low_half, pltpu.roll(outs[0], HS, 1), pltpu.roll(outs[1], HS, 1))
        inv = 1.0 / total
        recip[hp, rows, :] = inv
        heads[hp, rows, :] = (value * inv).astype(bf16)

    def attend_loop(b, first, last):
        def body(hp, carry):
            attend(b, hp)
            return carry

        lax.fori_loop(first, last, body, 0)

    hz = {}

    def finish(b):
        rows = rows_of(b)
        attn = jnp.zeros((BLK, D), f32)
        for hp in range(nh):
            attn = attn + dot_last(heads[hp, rows, :], w[hp].reshape(D, D)[:, 3 * FS :])
        hidden = features(x, rows).astype(f32) + attn
        h1[rows, :] = hidden
        normed, center, inv = standardize(hidden)
        u = normed * gain2 + bias2
        uh, ul = split(u)
        cols = dot_last(
            jnp.concatenate([uh, ul, uh], 1),
            jnp.concatenate([pad[0], pad[0], pad[1]], 1).astype(bf16),
        )
        cols = jnp.where(lane == experts, center, jnp.where(lane == experts + 1, inv, cols))
        st[:, rows] = cols.T[0 : experts + 8, :]
        for f in range(nh):
            h1b[f, rows, :] = hidden[:, f * FS : (f + 1) * FS].astype(bf16)
        mine = [
            local(h1b.at[h, rows], h1f.at[h, rows], hloc.at[b, 0]),
            local(st.at[:, rows], stf.at[h, :, rows], hloc.at[b, 1]),
        ]
        away = []
        for k in range(nh - 1):
            away.append(
                far(h1b.at[zid[k], rows], h1f.at[h, rows], hss.at[b, k], hsr.at[b, k], zpeer[k])
            )
            away.append(
                far(st.at[:, rows], stf.at[h, :, rows], sss.at[b, k], ssr.at[b, k], zpeer[k])
            )
        hz[b] = (mine, away)

    live = count[0]
    gain = npar[2:3, :]
    bias = npar[3:4, :]
    mask = own_group(slots * span, el)

    def gate(c):
        mine, away = hz[c]
        for v in mine:
            v.wait()
        for v in away:
            v.wait_recv()

        def body(i, carry):
            rows = pl.ds(pl.multiple_of(c * BLK + i * span, span), span)
            grows = pl.ds(pl.multiple_of(i * GB, GB), GB)
            spread = expand(stf[:, :, rows], experts, el, True)
            logits = jnp.stack(
                [jnp.where(s < live, spread[s][:, :el], fill_value) for s in range(slots)]
            ).reshape(slots, GB, span // GB, el)
            peak = jnp.max(logits, axis=(0, 2), keepdims=True)
            e = jnp.exp(logits - peak)
            g = e / jnp.sum(e, axis=(0, 2), keepdims=True)
            g = jnp.where(mask, g.reshape(slots * span, el), 0.0).astype(bf16)
            gates[c * per + i] = g
            mean = [v[:, el : el + FS] for v in spread]
            inv = [v[:, el + FS :] for v in spread]
            _, u, dy, _ = block_values(h1f, og, gain, bias, live, rows, mean, inv)
            both = jnp.concatenate([jnp.concatenate(u, 0), jnp.concatenate(dy, 0)], 1)
            mixed = dot_first(g, both).astype(bf16)
            mout[c, :, 0, grows, :] = mixed[:, :FS].reshape(experts, GB, FS)
            mout[c, :, 1, grows, :] = mixed[:, FS:].reshape(experts, GB, FS)
            return carry

        lax.fori_loop(0, per, body, 0)
        ez[c] = [
            far(mout.at[c, did[k]], xz.at[c, h, n], ess.at[c, k], esr.at[c, k], {"dp": did[k]})
            for k in range(nd - 1)
        ]
        xz[c, h, n] = mout[c, n]

    ez = {}

    def go_right(c, j):
        piece = xz.at[c, jnp.maximum(h - j, 0)]
        return remote(piece, piece, xsr.at[c, j], xrl.at[c, j], right)

    def go_left(c, j):
        piece = xz.at[c, jnp.minimum(h + j, top)]
        return remote(piece, piece, xsl.at[c, j], xrr.at[c, j], left)

    def gather(c, j):
        if j < top:
            gathers.append((c, j))
        if j == 0:
            for v in ez[c]:
                v.wait_recv()

            @pl.when(h < top)
            def _():
                go_right(c, 0).start()

            @pl.when(h > 0)
            def _():
                go_left(c, 0).start()

            return

        @pl.when(h >= j)
        def _():
            go_right(c, j - 1).wait_recv()
            if j < top:

                @pl.when(h < top)
                def _():
                    go_right(c, j).start()

        @pl.when(h + j <= top)
        def _():
            go_left(c, j - 1).wait_recv()
            if j < top:

                @pl.when(h > 0)
                def _():
                    go_left(c, j).start()

    count_rows = xz.shape[2] * xz.shape[4]

    def rows_at(c, f, kind):
        return xz[c, f, :, kind].reshape(count_rows, FS)

    def expert(c):
        mixed = jnp.concatenate([rows_at(c, f, 0) for f in range(nh)], axis=1)
        drows = jnp.concatenate([rows_at(c, f, 1) for f in range(nh)], axis=1)
        pre = dot(mixed, wi[...])
        cube = 0.7978845608028654
        t = jnp.tanh(cube * (pre + 0.044715 * (pre * pre * pre)))
        a = (0.5 * pre * (1.0 + t)).astype(bf16)
        slope = 0.5 * (1.0 + t) + 0.5 * pre * (1.0 - t * t) * (
            cube * (1.0 + 3.0 * 0.044715 * (pre * pre))
        )
        act[c] = a
        rows = dot(a, wo[...])
        d = (dot_last(drows, wo[...]) * slope).astype(bf16)
        dpre[c] = d
        dmix = dot_last(d, wi[...])
        shape = (xz.shape[2], xz.shape[4], FS)
        for f in range(nh):
            ps[c, f, :, 0] = rows[:, f * FS : (f + 1) * FS].astype(bf16).reshape(shape)
            ps[c, f, :, 1] = dmix[:, f * FS : (f + 1) * FS].astype(bf16).reshape(shape)

    def sum_right(c, d, mark):
        piece = inl.at[c, jnp.minimum(h + d, top)]
        return remote(piece, piece, isr.at[c, d], irl.at[c, mark], right)

    def sum_left(c, d, mark):
        piece = inr.at[c, jnp.maximum(h - d, 0)]
        return remote(piece, piece, isl.at[c, d], irr.at[c, mark], left)

    def scatter(c, stage):
        scatters.append((c, stage))

        @pl.when(h == stage)
        def _():
            for d in range(nh - stage):
                dest = stage + d
                if stage > 0:
                    sum_right(c, d, d).wait_recv()
                if d > 0:
                    if stage > 0:
                        value = inl[c, dest].astype(f32) + ps[c, dest].astype(f32)
                        inl[c, dest] = value.astype(bf16)
                    else:
                        inl[c, dest] = ps[c, dest]
                    sum_right(c, d, d - 1).start()

        @pl.when(h == top - stage)
        def _():
            for d in range(nh - stage):
                dest = top - stage - d
                if stage > 0:
                    sum_left(c, d, d).wait_recv()
                if d > 0:
                    if stage > 0:
                        value = inr[c, dest].astype(f32) + ps[c, dest].astype(f32)
                        inr[c, dest] = value.astype(bf16)
                    else:
                        inr[c, dest] = ps[c, dest]
                    sum_left(c, d, d - 1).start()

    yz = {}

    def home(c):
        for v in ez[c]:
            v.wait_send()
            sent[:] = [o for o in sent if o is not v]
        @pl.when(h == 0)
        def _():
            mout[c] = (ps[c, 0].astype(f32) + inr[c, 0].astype(f32)).astype(bf16)

        @pl.when(h == top)
        def _():
            mout[c] = (ps[c, top].astype(f32) + inl[c, top].astype(f32)).astype(bf16)

        for m in range(1, top):

            @pl.when(h == m)
            def _(m=m):
                value = ps[c, m].astype(f32) + inl[c, m].astype(f32)
                mout[c] = (value + inr[c, m].astype(f32)).astype(bf16)

        yz[c] = []
        for k in range(1, nd):
            src = lax.rem(n - k + nd, nd)
            yz[c].append(
                far(mout.at[c, src], yin.at[c, n], yss.at[c, k], ysr.at[c, k], {"dp": src})
            )
        yin[c, n] = mout[c, n]

    height = experts + 8
    srow = iota((height, el + 2 * FS), 0)
    scol = iota((height, el + 2 * FS), 1)
    target = jnp.where(scol < el, lax.shift_right_logical(scol, 4), experts)
    target = jnp.where(scol >= el + FS, experts + 1, target)
    fold = jnp.where(srow == target, 1.0, 0.0).astype(bf16)
    fold = jnp.concatenate([fold, fold], 1)
    fg[...] = jnp.zeros_like(fg)

    def back(c):
        for v in yz[c]:
            v.wait_recv()

        def body(i, carry):
            rows = pl.ds(pl.multiple_of(c * BLK + i * span, span), span)
            grows = pl.ds(pl.multiple_of(i * GB, GB), GB)
            spread = expand(stf[:, :, rows], experts, el, False)
            mean = [v[:, :FS] for v in spread]
            inv = [v[:, FS:] for v in spread]
            nhat, u, dy, hid = block_values(h1f, og, gain, bias, live, rows, mean, inv)
            y = jnp.concatenate(
                [yin[c, :, 0, grows, :].reshape(el, FS), yin[c, :, 1, grows, :].reshape(el, FS)], 1
            )
            g = gates[c * per + i]
            bd = dot(g, y)
            dgates = dot_last(
                jnp.concatenate([jnp.concatenate(dy, 0), jnp.concatenate(u, 0)], 1), y
            )
            g = g.astype(f32)
            gd = (g * dgates).reshape(slots, GB, span // GB, el)
            inner = jnp.sum(gd, axis=(0, 2), keepdims=True)
            dlog = gd - g.reshape(slots, GB, span // GB, el) * inner
            dlog = dlog.reshape(slots * span, el)
            qs, qn = [], []
            acc_gain = jnp.zeros((1, FS), f32)
            acc_bias = jnp.zeros((1, FS), f32)
            for s in range(slots):
                part = slice(s * span, (s + 1) * span)
                du = bd[part, FS:]
                h1f[s, rows, :] = jnp.where(s < live, hid[s] + bd[part, :FS], 0.0).astype(bf16)
                q = du * gain
                og[s, rows, :] = (dy[s].astype(f32) + inv[s] * q).astype(bf16)
                acc_gain = acc_gain + jnp.sum(du * nhat[s], 0, keepdims=True)
                acc_bias = acc_bias + jnp.sum(du, 0, keepdims=True)
                qs.append(q)
                qn.append(q * nhat[s])
            high, low = split(
                jnp.concatenate([dlog, jnp.concatenate(qs, 0), jnp.concatenate(qn, 0)], 1)
            )
            folded = dot_last(fold, jnp.concatenate([high, low], 1))
            for s in range(slots):
                py[s, :, rows] = folded[:, s * span : (s + 1) * span]
            fg[2:3, :] += acc_gain
            fg[3:4, :] += acc_bias
            return carry

        lax.fori_loop(0, per, body, 0)
        rows = rows_of(c)
        ends.append(local(h1f.at[:, rows], block_out.at[:, rows], oloc.at[c]))

    dz = {}

    def send_back(c):
        rows = rows_of(c)
        mine = [
            local(og.at[h, rows], p1s.at[h, rows], ploc.at[c, 0]),
            local(py.at[h, :, rows], pay.at[h, :, rows], ploc.at[c, 1]),
        ]
        away = []
        for k in range(nh - 1):
            away.append(
                far(og.at[zid[k], rows], p1s.at[h, rows], bss.at[c, k], bsr.at[c, k], zpeer[k])
            )
            away.append(
                far(py.at[zid[k], :, rows], pay.at[h, :, rows], vss.at[c, k], vsr.at[c, k], zpeer[k])
            )
        dz[c] = (mine, away)

    def expert_grads():
        total = blocks * count_rows
        squares = jnp.zeros((8, FS), f32)
        a_all = act[...].reshape(total, act.shape[2])
        d_all = dpre[...].reshape(total, dpre.shape[2])
        for f in range(nh):
            gi = dot_first(xz[:, f, :, 0].reshape(total, FS), d_all)
            go = dot_first(a_all, xz[:, f, :, 1].reshape(total, FS))
            dv[f, 0:D, :] = go
            for m in range(nh):
                part = gi[:, m * FS : (m + 1) * FS]
                dv[m, D + f * FS : D + (f + 1) * FS, :] = part
                squares = squares + jnp.sum((part * part).reshape(FS // 8, 8, FS), 0)
            squares = squares + jnp.sum((go * go).reshape(D // 8, 8, FS), 0)
        sqb[0] = squares
        for f in range(nh):
            cols = pl.ds(f * FS, FS)
            grads.append(local(dv.at[f, 0:D], g_out.at[:, cols], wloc.at[f, 0]))
            grads.append(local(dv.at[f, D : 2 * D], g_in.at[:, cols], wloc.at[f, 1]))

    grads = []

    x_load.wait()
    og_load.wait()
    for v in w_loads:
        v.wait()
    for f in range(nh):
        cols = pl.ds(f * FS, FS)
        wi[:, cols] = dk[f, 0:D].astype(bf16)
        wo[:, cols] = dk[f, D : 2 * D].astype(bf16)
    pass_weights(0)
    begin(0)
    for j in range(nh):
        if j + 1 < nh:
            pass_weights(j + 1)
        wp[j].wait_recv()
        attend(0, lax.rem(h - j + nh, nh))
    finish(0)
    begin(1)
    attend_loop(1, 0, nh)
    finish(1)
    begin(2)
    attend_loop(2, 0, 2)
    gate(0)
    attend_loop(2, 2, nh)
    gather(0, 0)
    finish(2)
    begin(3)
    attend_loop(3, 0, 1)
    gate(1)
    gather(0, 1)
    attend_loop(3, 1, 2)
    gather(1, 0)
    gather(0, 2)
    attend_loop(3, 2, 3)
    gather(1, 1)
    gather(0, 3)
    expert(0)
    scatter(0, 0)
    attend_loop(3, 3, nh)
    finish(3)
    gate(2)
    scatter(0, 1)
    gather(1, 2)
    gather(2, 0)
    gather(1, 3)
    expert(1)
    scatter(1, 0)
    scatter(0, 2)
    gate(3)
    gather(2, 1)
    scatter(1, 1)
    scatter(0, 3)
    home(0)
    gather(3, 0)
    gather(2, 2)
    scatter(1, 2)
    back(0)
    gather(3, 1)
    gather(2, 3)
    expert(2)
    scatter(2, 0)
    scatter(1, 3)
    home(1)
    gather(3, 2)
    scatter(2, 1)
    back(1)
    gather(3, 3)
    expert(3)
    scatter(3, 0)
    scatter(2, 2)
    scatter(3, 1)
    scatter(2, 3)
    home(2)
    scatter(3, 2)
    back(2)
    scatter(3, 3)
    home(3)
    expert_grads()
    back(3)
    for c in reversed(range(blocks)):
        send_back(c)
    er = iota((3 * height, FS), 0)
    er = jnp.where(er >= 2 * height, er - 2 * height, er)
    er = jnp.where(er >= height, er - height, er)
    eye = jnp.where(er == iota((3 * height, FS), 1), 1.0, 0.0).astype(bf16)
    pick = iota((8, 2 * FS), 1) & (FS - 1)
    row = iota((8, 2 * FS), 0)
    pick = ((row == 0) & (pick < HS)) | ((row == 1) & (pick >= HS))
    pick = jnp.where(pick, 1.0, 0.0).astype(bf16)
    small[...] = jnp.zeros_like(small)
    for b in range(blocks):
        for v in hz[b][1]:
            v.wait_send()
            sent[:] = [c for c in sent if c is not v]
    tgb = h1b

    def arrive(b):
        rows = rows_of(b)
        mine, away = dz[b]
        for v in mine:
            v.wait()
        for v in away:
            v.wait_recv()
        total = pay[0, :, rows]
        for f in range(1, nh):
            total = total + pay[f, :, rows]
        cols = dot_first(jnp.concatenate(split3(total), 0), eye)
        s1 = cols[:, experts : experts + 1]
        s2 = cols[:, experts + 1 : experts + 2]
        nhat, _, inv = standardize(h1[rows, :])
        ch, cl = split(jnp.where(lane < experts, cols, 0.0))
        du = dot(
            jnp.concatenate([ch, cl, ch], 1),
            jnp.concatenate([pad[0], pad[0], pad[1]], 0).astype(bf16),
        )
        q = du * gain2
        mq = (s1 + jnp.sum(q, -1, keepdims=True)) / D
        mqn = (s2 + jnp.sum(q * nhat, -1, keepdims=True)) / D
        dh1 = features(p1s, rows).astype(f32) + inv * (q - mq - nhat * mqn)
        small[2:3, :] += jnp.sum(du * nhat, 0, keepdims=True)
        small[3:4, :] += jnp.sum(du, 0, keepdims=True)
        routed = dot_first(jnp.concatenate([ch, cl], 1), (nhat * gain2 + bias2).astype(bf16))
        small[8 : 8 + experts, :] += routed[0:experts] + routed[FS : FS + experts]
        dattn[rows, :] = dh1.astype(bf16)
        h1[rows, :] = dh1

    def pair(b, hp):
        rows = rows_of(b)
        e_ref = es[b]
        dh = dot(dattn[rows, :], w[hp].reshape(D, D)[:, 3 * FS :]).astype(bf16).astype(f32)
        dh = dh * recip[hp, rows, :]
        high, rest = split(dh * heads[hp, rows, :].astype(f32))
        inner = dot_last(pick, jnp.concatenate([high, rest], 1))
        inner = jnp.concatenate([inner[0:1], inner[1:2]], 1)
        dhs = both_heads(dh.astype(bf16))
        qs = both_heads(qkv[hp, rows, 0:FS])
        dqt = jnp.zeros((FS, 2 * BLK), f32)
        for j in range(b + 1):
            keys = slice(j * BLK, (j + 1) * BLK)
            e = e_ref[hp, keys, :]
            dp = dot_last(qkv[hp, keys, 2 * FS :], dhs)
            ds = (e.astype(f32) * (dp - inner)).astype(bf16)
            dqt = dqt + dot(kt[hp, :, keys], ds)
            if b == blocks - 1:
                dk[hp, keys, :] = dot(ds, qs)
                dv[hp, keys, :] = dot(e, dhs)
            else:
                dk[hp, keys, :] += dot(ds, qs)
                dv[hp, keys, :] += dot(e, dhs)
        dq = jnp.where(low_half, dqt[:, :BLK].T, dqt[:, BLK:].T)
        qkv[hp, rows, 0:FS] = (dq * HS**-0.5).astype(bf16)
        qkv[hp, rows, FS : 2 * FS] = dk[hp, rows, :].astype(bf16)
        qkv[hp, rows, 2 * FS :] = dv[hp, rows, :].astype(bf16)

    def pairs(b, first, last):
        def body(hp, carry):
            pair(b, hp)
            return carry

        lax.fori_loop(first, last, body, 0)
        total = jnp.zeros((BLK, D), f32)
        for hp in range(first, last):
            total = total + dot_last(qkv[hp, rows_of(b), :], w[hp].reshape(D, D)[:, : 3 * FS])
        return total

    def settle(b, da1):
        rows = rows_of(b)
        hat, _, inv1 = standardize(features(x, rows).astype(f32))
        q1 = da1 * gain1
        m1 = jnp.sum(q1, -1, keepdims=True) / D
        m2 = jnp.sum(q1 * hat, -1, keepdims=True) / D
        tg = h1[rows, :] + inv1 * (q1 - m1 - hat * m2)
        small[0:1, :] += jnp.sum(da1 * hat, 0, keepdims=True)
        small[1:2, :] += jnp.sum(da1, 0, keepdims=True)
        for f in range(nh):
            tgb[f, rows, :] = tg[:, f * FS : (f + 1) * FS].astype(bf16)
        ends.append(local(tgb.at[h, rows], tgf.at[h, rows], gloc.at[b]))
        for k in range(nh - 1):
            c = remote(
                tgb.at[zid[k], rows], tgf.at[h, rows], gss.at[b, k], gsr.at[b, k], zpeer[k]
            )
            c.start()
            ends.append(c)

    ring = {}

    def weight_grads(hp):
        gi = dot_first(a1[...], qkv[hp]).astype(bf16)
        go = dot_first(dattn[...], heads[hp]).astype(bf16)
        gwb[hp] = jnp.concatenate([gi, go], 1).reshape(gwb.shape[1:])
        ring[hp] = far(gwb.at[hp, :, 1 - core], wc_in.at[hp], ass.at[hp], asr.at[hp], partner)

    cnum = [lax.rem(chip + k, chips) for k in range(1, chips)]

    def over_chips(hp):
        ring[hp].wait_recv()
        ch[hp] = (gwb[hp, :, core].astype(f32) + wc_in[hp].astype(f32)).astype(bf16)
        ring[hp] = [
            far(ch.at[hp, cnum[k]], wr.at[hp, k], cts.at[hp, k], ctr.at[hp, k], {"dp": cid[k]})
            for k in range(chips - 1)
        ]

    def to_owner(hp):
        return remote(zs.at[hp], zr.at[h], zss.at[hp], zsr.at[h], {"hid": hp})

    def over_z(hp):
        for v in ring[hp]:
            v.wait_recv()
        total = ch[hp, chip].astype(f32)
        for k in range(chips - 1):
            total = total + wr[hp, k].astype(f32)
        zs[hp] = total.astype(bf16)

        @pl.when(h != hp)
        def _():
            to_owner(hp).start()

        @pl.when(h == hp)
        def _():
            zr[hp] = zs[hp]

    half = nh // 2
    for b in reversed(range(blocks)):
        arrive(b)
        if b == blocks - 1:
            for v in grads:
                v.wait()
        dacc[rows_of(b), :] = pairs(b, 0, half)
    for hp in range(half):
        weight_grads(hp)
    for b in reversed(range(blocks)):
        settle(b, dacc[rows_of(b), :] + pairs(b, half, nh))
        if b == blocks - 1:
            for hp in range(half):
                over_chips(hp)
        elif b == blocks - 2:
            for hp in range(half):
                over_z(hp)
    for hp in range(half, nh):
        weight_grads(hp)
    for f in range(nh):
        sg[f] = small[:, f * FS : (f + 1) * FS]
    sz = [far(sg.at[zid[k]], szr.at[k], sms.at[k], smr.at[k], zpeer[k]) for k in range(nh - 1)]
    for hp in range(half, nh):
        over_chips(hp)
    for c in sz:
        c.wait_recv()
    part = sg[h]
    for k in range(nh - 1):
        part = part + szr[k]
    part = jnp.concatenate([part[0:8] + fg[...], part[8:]], 0)
    sdb[...] = part
    sd = [
        far(sdb, sdr.at[k], sns.at[k], snr.at[k], {"dp": did[k]}) for k in range(nd - 1)
    ]
    for hp in range(half, nh):
        over_z(hp)
    for c in sd:
        c.wait_recv()
    for k in range(nd - 1):
        part = part + sdr[k]
    ssum[...] = part
    squares = sqb[0] + jnp.where(
        n == 0, jnp.sum((part * part).reshape(part.shape[0] // 8, 8, FS), 0), 0.0
    )
    for src in range(nh):

        @pl.when(h != src)
        def _(src=src):
            remote(zs.at[src], zr.at[src], zss.at[src], zsr.at[src], {"hid": src}).wait_recv()

    block = zr[0].astype(f32)
    for src in range(1, nh):
        block = block + zr[src].astype(f32)
    gsum[...] = block
    for f in range(nh):
        part = block[:, f * FS : (f + 1) * FS]
        squares = squares + jnp.sum((part * part).reshape(part.shape[0] // 8, 8, FS), 0)
    sqb[1] = squares
    qd = [
        far(sqb.at[1], sqd.at[k], qss.at[k], qsr.at[k], {"dp": did[k]}) for k in range(nd - 1)
    ]
    for c in qd:
        c.wait_recv()
    for k in range(nd - 1):
        squares = squares + sqd[k]
    sqb[2] = squares
    qz = [far(sqb.at[2], sqz.at[k], rss.at[k], rsr.at[k], zpeer[k]) for k in range(nh - 1)]
    for c in qz:
        c.wait_recv()
    for k in range(nh - 1):
        squares = squares + sqz[k]
    everything = jnp.sum(jnp.sum(squares, 1, keepdims=True), 0, keepdims=True)
    norm[...] = jnp.broadcast_to(jnp.sqrt(everything), norm.shape)
    for c in sent:
        c.wait_send()
    for hp in range(nh):

        @pl.when(h != hp)
        def _(hp=hp):
            to_owner(hp).wait_send()

    for c, j in gathers:

        @pl.when(jnp.logical_and(h < top, h >= j))
        def _(c=c, j=j):
            go_right(c, j).wait_send()

        @pl.when(jnp.logical_and(h > 0, h + j <= top))
        def _(c=c, j=j):
            go_left(c, j).wait_send()

    for c, stage in scatters:

        @pl.when(h == stage)
        def _(c=c, stage=stage):
            for d in range(1, nh - stage):
                sum_right(c, d, d - 1).wait_send()

        @pl.when(h == top - stage)
        def _(c=c, stage=stage):
            for d in range(1, nh - stage):
                sum_left(c, d, d - 1).wait_send()

    for c in ends:
        c.wait()


def reduce_kernel(
    nd, nh, experts, gw, sg, fg, sqe, gsum, ssum, norm,
    wc, ch, own, wr, zr, zs, szr, sdr, sqd, sqz, sdb, sqb,
    css, csr, dss, dsr, zss, zsr, ass, asr, bss, bsr, qss, qsr, rss, rsr
):
    n = lax.axis_index("dp")
    h = lax.axis_index("hid")
    core = lax.rem(n, 2)
    chip = lax.div(n, 2)
    chips = nd // 2
    zid = [lax.rem(h + k, nh) for k in range(1, nh)]
    zpeer = [{"hid": z} for z in zid]
    did = [lax.rem(n + k, nd) for k in range(1, nd)]
    dpeer = [{"dp": d} for d in did]
    greet(zpeer + dpeer)
    partner = {"dp": chip * 2 + 1 - core}
    first = remote(gw.at[:, :, 1 - core], wc, css.at[0], csr.at[0], partner)
    first.start()
    sz = [remote(sg.at[zid[k]], szr.at[k], ass.at[k], asr.at[k], zpeer[k]) for k in range(nh - 1)]
    for c in sz:
        c.start()
    for c in sz:
        c.wait_recv()
    small = sg[h]
    for k in range(nh - 1):
        small = small + szr[k]
    small = jnp.concatenate([small[0:8] + fg[...], small[8:]], 0)
    sdb[...] = small
    sd = [remote(sdb, sdr.at[k], bss.at[k], bsr.at[k], dpeer[k]) for k in range(nd - 1)]
    for c in sd:
        c.start()
    first.wait_recv()
    for hp in range(nh):
        ch[hp] = (gw[hp, :, core].astype(f32) + wc[hp].astype(f32)).astype(bf16)
    cid = [lax.rem(chip + k, chips) for k in range(1, chips)]
    second = [
        remote(ch.at[:, cid[k]], wr.at[k], dss.at[k], dsr.at[k], {"dp": cid[k] * 2 + core})
        for k in range(chips - 1)
    ]
    for c in second:
        c.start()
    for c in sd:
        c.wait_recv()
    for k in range(nd - 1):
        small = small + sdr[k]
    ssum[...] = small
    for c in second:
        c.wait_recv()
    total = ch[:, chip].astype(f32)
    for k in range(chips - 1):
        total = total + wr[k].astype(f32)
    zs[...] = total.astype(bf16)
    third = [
        remote(zs.at[zid[k]], zr.at[k], zss.at[k], zsr.at[k], zpeer[k]) for k in range(nh - 1)
    ]
    for c in third:
        c.start()
    for c in third:
        c.wait_recv()
    block = zs[h].astype(f32)
    for k in range(nh - 1):
        block = block + zr[k].astype(f32)
    gsum[...] = block
    squares = sqe[...]
    for f in range(nh):
        part = block[:, f * FS : (f + 1) * FS]
        squares = squares + jnp.sum((part * part).reshape(part.shape[0] // 8, 8, FS), 0)
    both = jnp.sum((small * small).reshape(small.shape[0] // 8, 8, FS), 0)
    squares = squares + jnp.where(n == 0, both, 0.0)
    sqb[0] = squares
    qd = [remote(sqb.at[0], sqd.at[k], qss.at[k], qsr.at[k], dpeer[k]) for k in range(nd - 1)]
    for c in qd:
        c.start()
    for c in qd:
        c.wait_recv()
    for k in range(nd - 1):
        squares = squares + sqd[k]
    sqb[1] = squares
    qz = [remote(sqb.at[1], sqz.at[k], rss.at[k], rsr.at[k], zpeer[k]) for k in range(nh - 1)]
    for c in qz:
        c.start()
    for c in qz:
        c.wait_recv()
    for k in range(nh - 1):
        squares = squares + sqz[k]
    everything = jnp.sum(jnp.sum(squares, 1, keepdims=True), 0, keepdims=True)
    norm[...] = jnp.broadcast_to(jnp.sqrt(everything), norm.shape)
    for c in [first] + sz + sd + second + third + qd + qz:
        c.wait_send()


def call(kernel, cid, outs, scratch, ins, out_specs=None, limit=60, pack=None):
    shapes = [jax.ShapeDtypeStruct(s, t) for s, t in outs]
    specs = out_specs or [VM] * len(outs)
    if pack is not None:
        shapes = shapes[: pack[0]] + [shapes[pack[0] :]]
        specs = specs[: pack[0]] + [specs[pack[0] :]]
    result = pl.pallas_call(
        kernel,
        out_shape=shapes,
        in_specs=[spec for spec, _ in ins],
        out_specs=specs,
        scratch_shapes=scratch,
        compiler_params=pltpu.CompilerParams(
            collective_id=cid, has_side_effects=True, vmem_limit_bytes=limit * 2**20
        ),
    )(*[value for _, value in ins])
    if pack is not None:
        result = list(result[: pack[0]]) + list(result[pack[0]])
    return result


def adam_update(weight, grad, first, second, rate, factor):
    clipped = grad * factor
    first_new = beta_first * first + (1.0 - beta_first) * clipped
    second_new = beta_second * second + (1.0 - beta_second) * clipped * clipped
    first_hat = first_new / (1.0 - beta_first**STEP)
    second_hat = second_new / (1.0 - beta_second**STEP)
    weight_new = weight - rate * (
        first_hat / (jnp.sqrt(second_hat) + adam_epsilon) + weight_decay * weight
    )
    return (first_new, second_new, weight_new)


def shards(
    tokens,
    seq_count,
    out_grad,
    norm_params,
    norm_first,
    norm_second,
    controller_weight,
    router_first,
    router_second,
    attn_in,
    attn_in_first,
    attn_in_second,
    attn_in_average,
    attn_out,
    attn_out_first,
    attn_out_second,
    attn_out_average,
    expert_in,
    expert_in_first,
    expert_in_second,
    expert_in_average,
    expert_out,
    expert_out_first,
    expert_out_second,
    expert_out_average,
):
    ema_keep = (1.0 + STEP) / (10.0 + STEP)
    nd = lax.axis_size("dp")
    nh = lax.axis_size("hid")
    chips = nd // 2
    slots, seq, _ = tokens.shape
    experts = controller_weight.shape[1]
    r = attn_in.shape[0]
    el = experts * GB
    groups = seq * slots // GROUP
    blocks = seq // BLK
    hidden = expert_in.shape[2]
    er = 8 + experts
    z3 = nh - 1

    etypes = [((nh, (b + 1) * BLK, 2 * BLK), bf16) for b in range(blocks)]
    slices = ((nh, seq, FS), bf16)
    wtype = ((nh, chips, 2, r, D), bf16)
    qtype = ((nh, seq, 3 * FS), bf16)
    ttype = ((nh, FS, seq), bf16)
    rtype = ((nh, seq, FS), f32)
    htype = ((seq, D), f32)
    stype = ((nh, er, seq), f32)
    ptype = ((nh, er, FS), f32)
    ytype = ((nd, 2, groups, FS), bf16)
    gtype = ((groups // GB, GB * GROUP, el), bf16)

    def vmem(*types):
        return [pltpu.VMEM(*t) for t in types]

    share = groups // blocks
    xtype = ((blocks, nh, nd, 2, share, FS), bf16)
    if nd <= 8 and blocks == 4 and slots == nh:
        block_out, tgf, g_in, g_out, gsum, ssum, norm = call(
            functools.partial(block_kernel, nd, nh, experts),
            5,
            [
                slices,
                slices,
                ((D, hidden), f32),
                ((hidden, D), f32),
                ((r, D), f32),
                ((er, FS), f32),
                ((8, FS), f32),
            ],
            vmem(((r, D), bf16), ((er, FS), f32))
            + vmem(slices, wtype, ptype, ((seq, D), bf16), qtype, ttype, ttype, slices, rtype, htype)
            + [vmem(*etypes)]
            + vmem(
                slices,
                ((er, seq), f32),
                slices,
                stype,
                slices,
                gtype,
                ((blocks, experts, 2, share, FS), bf16),
                xtype,
                ((blocks, nd * share, hidden), bf16),
                ((blocks, nd * share, hidden), bf16),
                xtype,
                xtype,
                xtype,
                ((blocks, nd, 2, share, FS), bf16),
                ((D, hidden), bf16),
                ((hidden, D), bf16),
                stype,
                slices,
                stype,
                rtype,
                rtype,
                ((seq, D), bf16),
                ((2, FS, D), f32),
                ((er, D), f32),
                ((8, FS), f32),
                ptype,
                htype,
                wtype,
                ((nh, chips, r, D), bf16),
                ((nh, chips, r, D), bf16),
                ((nh, chips - 1, r, D), bf16),
                ((nh, r, D), bf16),
                ((nh, r, D), bf16),
                ((z3, er, FS), f32),
                ((er, FS), f32),
                ((nd - 1, er, FS), f32),
                ((3, 8, FS), f32),
                ((nd - 1, 8, FS), f32),
                ((z3, 8, FS), f32),
            )
            + [DMA((blocks, z3))] * 2
            + [DMA((z3,))] * 2
            + [DMA((nh, chips - 1))] * 2
            + [DMA((nh,))] * 2
            + [DMA((z3,))] * 2
            + [DMA((blocks, z3))] * 4
            + [DMA((blocks, nd - 1))] * 2
            + [DMA((blocks, z3))] * 4
            + [DMA((blocks, nh))] * 4
            + [DMA((blocks, nd))] * 2
            + [DMA((blocks, z3))] * 6
            + [DMA((nh,))] * 2
            + [DMA((nh, chips - 1))] * 2
            + [DMA((nh,))] * 2
            + [DMA((z3,))] * 2
            + [DMA((nd - 1,))] * 4
            + [DMA((z3,))] * 2
            + [DMA((4,)), DMA((blocks, 2)), DMA((blocks, 2)), DMA((blocks,))]
            + [DMA((nh, 2)), DMA((blocks,))],
            [
                (SM, seq_count),
                (HB, tokens),
                (VM, attn_in.transpose(1, 0, 2)),
                (VM, attn_out),
                (VM, norm_params),
                (VM, controller_weight.T),
                (HB, out_grad),
                (HB, expert_in[0]),
                (HB, expert_out[0]),
            ],
            [HB, VM, HB, HB, VM, VM, VM],
        )
    else:
        wblk = jnp.concatenate([attn_in.reshape(r, 3 * FS), attn_out], 1).astype(bf16)
        pblk = jnp.concatenate([norm_params, jnp.zeros((4, FS), f32), controller_weight.T], 0)
        x, w, p, qkv, kt, heads, recip, h1, h1f, stf, *es = call(
            functools.partial(forward_kernel, nd, nh, experts),
            1,
            [slices, wtype, ptype, qtype, ttype, slices, rtype, htype, slices, stype] + etypes,
            vmem(slices, wtype, qtype, ttype, slices, rtype, htype)
            + vmem(((BLK, D), bf16), ttype)
            + [vmem(*etypes)]
            + vmem(slices, ((er, seq), f32), ((2, FS, D), f32))
            + [DMA((blocks, z3))] * 2
            + [DMA((z3,))] * 2
            + [DMA((nh, chips - 1))] * 2
            + [DMA((1,))] * 2
            + [DMA((z3,))] * 2
            + [DMA((blocks, z3))] * 4
            + [DMA((4,)), DMA((blocks, 6)), DMA((blocks, 2)), DMA((blocks,))],
            [(VM, tokens), (VM, wblk), (VM, pblk)],
            [HB, HB, VM, HB, HB, HB, HB, HB, VM, VM] + [HB] * blocks,
            pack=(10, blocks),
        )
        gates, yin, g_in, g_out, sqe = call(
            functools.partial(expert_kernel, nd, nh, experts),
            2,
            [gtype, ytype, ((D, hidden), f32), ((hidden, D), f32), ((8, FS), f32)],
            vmem(
                ytype,
                ((nh, nd, 2, groups, FS), bf16),
                ((nd, groups, hidden), bf16),
                ((nd, groups, hidden), bf16),
                ((nh, nh, 2, groups, FS), bf16),
                ((nd, nh, 2, groups, FS), bf16),
                ((nd, nh, 2, groups, FS), bf16),
                ytype,
                ((2, D, D), f32),
                ((D, hidden), bf16),
                ((hidden, D), bf16),
            )
            + [DMA((nd,))] * 2
            + [DMA((nd, z3))] * 4
            + [DMA((nd, nh))] * 4
            + [DMA((nd,))] * 2
            + [DMA((4,))],
            [
                (SM, seq_count),
                (VM, h1f),
                (VM, stf),
                (VM, out_grad),
                (VM, norm_params),
                (HB, expert_in[0]),
                (HB, expert_out[0]),
            ],
        )
        block_out, fg, tgf, gw, sg = call(
            functools.partial(backward_kernel, nh, experts),
            3,
            [slices, ((8, FS), f32), slices, wtype, ptype],
            vmem(slices, stype, slices, stype)
            + vmem(slices, wtype, qtype, ttype, slices, rtype, htype)
            + vmem(
                ((seq, D), bf16),
                rtype,
                rtype,
                qtype,
                ((seq, D), bf16),
                slices,
                ((2, FS, D), f32),
                ((er, D), f32),
            )
            + [vmem(*etypes)]
            + [DMA((blocks, z3))] * 6
            + [DMA((blocks,)), DMA((blocks, 2)), DMA((7,)), DMA((blocks,))],
            [(SM, seq_count)]
            + [(VM, v) for v in (h1f, stf, out_grad, norm_params, gates, yin, p)]
            + [(HB, v) for v in (x, w, qkv, kt, heads, recip, h1)]
            + [([HB] * blocks, list(es))],
        )
        gsum, ssum, norm = call(
            functools.partial(reduce_kernel, nd, nh, experts),
            4,
            [((r, D), f32), ((er, FS), f32), ((8, FS), f32)],
            [
                pltpu.VMEM((nh, chips, r, D), bf16),
                pltpu.VMEM((nh, chips, r, D), bf16),
                pltpu.VMEM((8, FS), f32),
                pltpu.VMEM((chips - 1, nh, r, D), bf16),
                pltpu.VMEM((z3, r, D), bf16),
                pltpu.VMEM((nh, r, D), bf16),
                pltpu.VMEM((z3, er, FS), f32),
                pltpu.VMEM((nd - 1, er, FS), f32),
                pltpu.VMEM((nd - 1, 8, FS), f32),
                pltpu.VMEM((z3, 8, FS), f32),
                pltpu.VMEM((er, FS), f32),
                pltpu.VMEM((2, 8, FS), f32),
            ]
            + [DMA((1,))] * 2
            + [DMA((chips - 1,))] * 2
            + [DMA((z3,))] * 4
            + [DMA((nd - 1,))] * 4
            + [DMA((z3,))] * 2,
            [(VM, gw), (VM, sg), (VM, fg), (VM, sqe)],
        )
    grad_norm = norm[0, 0]
    tokens_grad = tgf.astype(f32)
    attn_in_sum = gsum[:, : 3 * FS].reshape(attn_in.shape)
    attn_out_sum = gsum[:, 3 * FS :]
    norm_sum = ssum[0:4]
    router_sum = ssum[8:].T
    expert_in_sum = g_in[None]
    expert_out_sum = g_out[None]
    factor = jnp.minimum(1.0, clip_limit / grad_norm)
    norm_up = adam_update(norm_params, norm_sum, norm_first, norm_second, 0.6, factor)
    router_up = adam_update(
        controller_weight, router_sum, router_first, router_second, (4 * D) ** (-0.5), factor
    )
    attn_in_up = adam_update(
        attn_in, attn_in_sum, attn_in_first, attn_in_second, 0.5 * D ** (-0.5), factor
    )
    attn_out_up = adam_update(
        attn_out,
        attn_out_sum,
        attn_out_first,
        attn_out_second,
        0.5 * (HEADS * HS // 16) ** (-0.5),
        factor,
    )
    expert_in_up = adam_update(
        expert_in,
        expert_in_sum,
        expert_in_first,
        expert_in_second,
        2.5 * (D // GROUP) ** (-0.5),
        factor,
    )
    expert_out_up = adam_update(
        expert_out, expert_out_sum, expert_out_first, expert_out_second, 0.5 * H ** (-0.5), factor
    )
    return (
        block_out,
        tokens_grad,
        grad_norm,
        norm_up[0],
        norm_up[1],
        norm_up[2],
        router_up[0],
        router_up[1],
        router_up[2],
        attn_in_up[0],
        attn_in_up[1],
        attn_in_up[2],
        ema_keep * attn_in_average + (1.0 - ema_keep) * attn_in_up[2],
        attn_out_up[0],
        attn_out_up[1],
        attn_out_up[2],
        ema_keep * attn_out_average + (1.0 - ema_keep) * attn_out_up[2],
        expert_in_up[0],
        expert_in_up[1],
        expert_in_up[2],
        ema_keep * expert_in_average + (1.0 - ema_keep) * expert_in_up[2],
        expert_out_up[0],
        expert_out_up[1],
        expert_out_up[2],
        ema_keep * expert_out_average + (1.0 - ema_keep) * expert_out_up[2],
    )


def solution(mesh):
    return jax.shard_map(
        shards,
        mesh=mesh,
        in_specs=(
            P("dp", None, "hid"),
            P("dp"),
            P("dp", None, "hid"),
            P(None, "hid"),
            P(None, "hid"),
            P(None, "hid"),
            P("hid", None),
            P("hid", None),
            P("hid", None),
            P("dp", None, "hid"),
            P("dp", None, "hid"),
            P("dp", None, "hid"),
            P("dp", None, "hid"),
            P("dp", "hid"),
            P("dp", "hid"),
            P("dp", "hid"),
            P("dp", "hid"),
            P("dp", None, "hid"),
            P("dp", None, "hid"),
            P("dp", None, "hid"),
            P("dp", None, "hid"),
            P("dp", "hid", None),
            P("dp", "hid", None),
            P("dp", "hid", None),
            P("dp", "hid", None),
        ),
        out_specs=(
            P("dp", None, "hid"),
            P("dp", None, "hid"),
            P(),
            P(None, "hid"),
            P(None, "hid"),
            P(None, "hid"),
            P("hid", None),
            P("hid", None),
            P("hid", None),
            P("dp", None, "hid"),
            P("dp", None, "hid"),
            P("dp", None, "hid"),
            P("dp", None, "hid"),
            P("dp", "hid"),
            P("dp", "hid"),
            P("dp", "hid"),
            P("dp", "hid"),
            P("dp", None, "hid"),
            P("dp", None, "hid"),
            P("dp", None, "hid"),
            P("dp", None, "hid"),
            P("dp", "hid", None),
            P("dp", "hid", None),
            P("dp", "hid", None),
            P("dp", "hid", None),
        ),
        check_vma=False,
    )
```

```python
import functools

import jax
import jax.numpy as jnp
from jax import lax
from jax.experimental import pallas as pl
from jax.experimental.pallas import tpu as pltpu
from jax.sharding import PartitionSpec as P

D = 512
HEADS = 8
HS = 64
H = 2048
GROUP = 32
STEP = 10
BLK = 256
FS = 128
GB = 16

norm_epsilon = 1e-05
fill_value = -1e30
clip_limit = 1.0
beta_first = 0.9
beta_second = 0.95
adam_epsilon = 1e-08
weight_decay = 0.1

f32 = jnp.float32
bf16 = jnp.bfloat16
MESH = pl.DeviceIdType.MESH
EXACT = lax.Precision.HIGHEST
VM = pl.BlockSpec(memory_space=pltpu.VMEM)
HB = pl.BlockSpec(memory_space=pl.ANY)
SM = pl.BlockSpec(memory_space=pltpu.SMEM)
DMA = pltpu.SemaphoreType.DMA


def dot(a, b, precision=None):
    return lax.dot_general(
        a, b, (((1,), (0,)), ((), ())), precision=precision, preferred_element_type=f32
    )


def dot_last(a, b, precision=None):
    return lax.dot_general(
        a, b, (((1,), (1,)), ((), ())), precision=precision, preferred_element_type=f32
    )


def dot_first(a, b, precision=None):
    return lax.dot_general(
        a, b, (((0,), (0,)), ((), ())), precision=precision, preferred_element_type=f32
    )


def greet(peers):
    barrier = pltpu.get_barrier_semaphore()
    for peer in peers:
        pl.semaphore_signal(barrier, inc=1, device_id=peer, device_id_type=MESH)
    pl.semaphore_wait(barrier, len(peers))


def remote(src, dst, send, recv, peer):
    return pltpu.make_async_remote_copy(
        src_ref=src, dst_ref=dst, send_sem=send, recv_sem=recv, device_id=peer, device_id_type=MESH
    )


def lanes(ref_like, index):
    return pl.ds(pl.multiple_of(index * ref_like, ref_like), ref_like)


def features(ref, rows):
    return jnp.concatenate([ref[f, rows, :] for f in range(ref.shape[0])], axis=1)


def row_of(ref, row):
    return jnp.concatenate([ref[f, row : row + 1, :] for f in range(ref.shape[0])], axis=1)


def split(v):
    high = v.astype(bf16)
    return high, (v - high.astype(f32)).astype(bf16)


def split3(v):
    high, _ = split(v)
    rest = v - high.astype(f32)
    mid, low = split(rest)
    return high, mid, low


def iota(shape, dim):
    return lax.broadcasted_iota(jnp.int32, shape, dim)


def standardize(v):
    center = jnp.sum(v, -1, keepdims=True) / v.shape[-1]
    dev = v - center
    inv = lax.rsqrt(jnp.sum(dev * dev, -1, keepdims=True) / v.shape[-1] + norm_epsilon)
    return dev * inv, center, inv


def controller_rows(p, pad, experts):
    pad[...] = jnp.zeros_like(pad)
    for f in range(p.shape[0]):
        high, low = split(p[f, 8 : 8 + experts, :])
        pad[0, 0:experts, f * FS : (f + 1) * FS] = high.astype(f32)
        pad[1, 0:experts, f * FS : (f + 1) * FS] = low.astype(f32)


def both_heads(v):
    low = iota(v.shape, 1) < HS
    zero = jnp.zeros_like(v)
    return jnp.concatenate([jnp.where(low, v, zero), jnp.where(low, zero, v)], 0)


def forward_kernel(
    nd, nh, experts, tok, wblk, pblk,
    xo, wout, p, qkvo, kto, headso, recipo, h1o, h1f, stf, eouts,
    x, w, qkv, kt, heads, recip, h1, a1, vt, es, h1b, st, pad,
    tss, tsr, wss, wsr, dss, dsr, css, csr, pss, psr, hss, hsr, sss, ssr, loc, esem, mine_sem, save
):
    n = lax.axis_index("dp")
    h = lax.axis_index("hid")
    core = lax.rem(n, 2)
    chip = lax.div(n, 2)
    chips = nd // 2
    seq = tok.shape[1]
    blocks = seq // BLK
    zpeer = [{"hid": lax.rem(h + k, nh)} for k in range(1, nh)]
    cpeer = [{"dp": lax.rem(chip + k, chips) * 2 + core} for k in range(1, chips)]
    partner = {"dp": chip * 2 + 1 - core}
    greet(zpeer + cpeer + [partner])
    locals_ = [
        pltpu.make_async_copy(wblk, w.at[h, chip, core], loc.at[0]),
        pltpu.make_async_copy(pblk, p.at[h], loc.at[1]),
        pltpu.make_async_copy(tok.at[h], x.at[h], loc.at[2]),
    ]
    for c in locals_:
        c.start()
    wz = [
        remote(wblk, w.at[h, chip, core], wss.at[k], wsr.at[k], zpeer[k]) for k in range(nh - 1)
    ]
    pz = [remote(pblk, p.at[h], pss.at[k], psr.at[k], zpeer[k]) for k in range(nh - 1)]
    for c in wz + pz:
        c.start()
    tz = []
    for b in range(blocks):
        rows = pl.ds(b * BLK, BLK)
        for k in range(nh - 1):
            c = remote(
                tok.at[lax.rem(h + k + 1, nh), rows],
                x.at[h, rows],
                tss.at[b, k],
                tsr.at[b, k],
                zpeer[k],
            )
            c.start()
            tz.append(c)
    locals_[0].wait()
    wc = []
    for j in range(nh):
        piece = lax.rem(h - j + nh, nh)
        if j > 0:
            wz[j - 1].wait_recv()
        for k in range(chips - 1):
            c = remote(
                w.at[piece, chip, core], w.at[piece, chip, core],
                dss.at[j, k], dsr.at[j, k], cpeer[k]
            )
            c.start()
            wc.append(c)
    for c in pz + wc:
        c.wait_recv()
    wp = remote(w.at[:, :, core], w.at[:, :, core], css.at[0], csr.at[0], partner)
    wp.start()
    for c in locals_[1:]:
        c.wait()
    controller_rows(p, pad, experts)
    gain1 = row_of(p, 0)
    bias1 = row_of(p, 1)
    gain2 = row_of(p, 2)
    bias2 = row_of(p, 3)
    scale = jnp.where(iota((BLK, 3 * FS), 1) < FS, HS**-0.5, 1.0).astype(bf16)
    lane = iota((BLK, FS), 1)
    low_half = lane < HS
    causal = iota((BLK, 2 * BLK), 0) <= (iota((BLK, 2 * BLK), 1) & (BLK - 1))
    one = jnp.ones((FS, BLK), bf16)
    low_rows = iota((FS, BLK), 0) < HS
    sends = []
    for b in range(blocks):
        rows = pl.ds(b * BLK, BLK)
        past = b * BLK
        e_ref = es[b]
        for k in range(nh - 1):
            tz[b * (nh - 1) + k].wait_recv()
        normed, _, _ = standardize(features(x, rows).astype(f32))
        a1[...] = (normed * gain1 + bias1).astype(bf16)
        if b == 0:
            wp.wait_recv()
            c = pltpu.make_async_copy(w, wout, loc.at[3])
            c.start()
            sends.append(c)

        def pair(hp, carry):
            proj = dot(a1[...], w[hp].reshape(D, D)[:, : 3 * FS])
            low = proj.astype(bf16) * scale
            qkv[hp, rows, :] = low
            kt[hp, :, rows] = proj[:, FS : 2 * FS].T.astype(bf16)
            vt[hp, :, rows] = proj[:, 2 * FS :].T.astype(bf16)
            q = both_heads(low[:, :FS])
            s_now = dot_last(low[:, FS : 2 * FS], q)
            s_now = jnp.where(causal, s_now, fill_value)
            peak = jnp.max(s_now, 0, keepdims=True)
            if b > 0:
                s_past = dot_last(qkv[hp, 0:past, FS : 2 * FS], q)
                peak = jnp.maximum(peak, jnp.max(s_past, 0, keepdims=True))
                e_ref[hp, 0:past, :] = jnp.exp(s_past - peak).astype(bf16)
            e_ref[hp, past : past + BLK, :] = jnp.exp(s_now - peak).astype(bf16)
            outs = []
            for half in range(2):
                total = jnp.zeros((FS, BLK), f32)
                for j in range(b + 1):
                    keys = slice(j * BLK, (j + 1) * BLK)
                    v = vt[hp, :, keys]
                    v = jnp.where(low_rows, v, one) if half == 0 else jnp.where(low_rows, one, v)
                    total = total + dot(v, e_ref[hp, keys, half * BLK : (half + 1) * BLK])
                outs.append(total.T)
            value = jnp.where(low_half, outs[0], outs[1])
            total = jnp.where(low_half, pltpu.roll(outs[0], HS, 1), pltpu.roll(outs[1], HS, 1))
            inv = 1.0 / total
            recip[hp, rows, :] = inv
            heads[hp, rows, :] = (value * inv).astype(bf16)
            return carry

        lax.fori_loop(0, nh, pair, 0)
        saves = [
            (e_ref, eouts[b]),
            (x.at[:, rows], xo.at[:, rows]),
            (qkv.at[:, rows], qkvo.at[:, rows]),
            (kt.at[:, :, rows], kto.at[:, :, rows]),
            (heads.at[:, rows], headso.at[:, rows]),
            (recip.at[:, rows], recipo.at[:, rows]),
        ]
        for k, (src, dst) in enumerate(saves):
            c = pltpu.make_async_copy(src, dst, esem.at[b, k])
            c.start()
            sends.append(c)
        attn = jnp.zeros((BLK, D), f32)
        for hp in range(nh):
            attn = attn + dot_last(heads[hp, rows, :], w[hp].reshape(D, D)[:, 3 * FS :])
        hidden = features(x, rows).astype(f32) + attn
        h1[rows, :] = hidden
        c = pltpu.make_async_copy(h1.at[rows], h1o.at[rows], save.at[b])
        c.start()
        sends.append(c)
        normed, center, inv = standardize(hidden)
        u = normed * gain2 + bias2
        uh, ul = split(u)
        cols = dot_last(
            jnp.concatenate([uh, ul, uh], 1),
            jnp.concatenate([pad[0], pad[0], pad[1]], 1).astype(bf16),
        )
        cols = jnp.where(lane == experts, center, jnp.where(lane == experts + 1, inv, cols))
        st[:, rows] = cols.T[0 : experts + 8, :]
        for f in range(nh):
            h1b[f, rows, :] = hidden[:, f * FS : (f + 1) * FS].astype(bf16)
        mine = [
            pltpu.make_async_copy(h1b.at[h, rows], h1f.at[h, rows], mine_sem.at[b, 0]),
            pltpu.make_async_copy(st.at[:, rows], stf.at[h, :, rows], mine_sem.at[b, 1]),
        ]
        for c in mine:
            c.start()
        for k in range(nh - 1):
            c = remote(
                h1b.at[lax.rem(h + k + 1, nh), rows],
                h1f.at[h, rows],
                hss.at[b, k],
                hsr.at[b, k],
                zpeer[k],
            )
            s = remote(
                st.at[:, rows], stf.at[h, :, rows], sss.at[b, k], ssr.at[b, k], zpeer[k]
            )
            c.start()
            s.start()
            sends += [c, s]
        sends += mine
    for c in sends:
        c.wait()
    for c in wz + pz + tz + wc + [wp]:
        c.wait_send()


def expand(stb, experts, el, gates):
    height = stb.shape[1]
    width = (el if gates else 0) + 2 * FS
    rows = iota((3 * height, width), 0)
    cols = iota((3 * height, width), 1)
    rows = jnp.where(rows >= 2 * height, rows - 2 * height, rows)
    rows = jnp.where(rows >= height, rows - height, rows)
    base = el if gates else 0
    target = jnp.where(cols < base + FS, experts, experts + 1)
    if gates:
        target = jnp.where(cols < el, lax.shift_right_logical(cols, 4), target)
    pick = jnp.where(rows == target, 1.0, 0.0).astype(bf16)
    return [
        dot_first(jnp.concatenate(split3(stb[s]), 0), pick) for s in range(stb.shape[0])
    ]


def own_group(tokens, el):
    group = lax.shift_right_logical(iota((tokens, el), 0), 3) & (GB - 1)
    return (iota((tokens, el), 1) & (GB - 1)) == group


def block_values(h1f, og, gain, bias, live, rows, mean, inv):
    slots = h1f.shape[0]
    nhat, u, dy, hid = [], [], [], []
    for s in range(slots):
        hidden = h1f[s, rows, :].astype(f32)
        hat = (hidden - mean[s]) * inv[s]
        nhat.append(hat)
        u.append((hat * gain + bias).astype(bf16))
        hid.append(hidden)
        grad = og[s, rows, :]
        dy.append(jnp.where(s < live, grad, jnp.zeros_like(grad)))
    return nhat, u, dy, hid


def expert_kernel(
    nd, nh, experts, count, h1f, stf, og, npar, win, wout, gates, yin, g_in, g_out, sq,
    mout, xz, act, dpre, ps, inl, inr, yo, wf, wi, wo,
    dss, dsr, xsr, xsl, xrl, xrr, isr, isl, irl, irr, yss, ysr, loc
):
    n = lax.axis_index("dp")
    h = lax.axis_index("hid")
    seq = h1f.shape[1]
    slots = h1f.shape[0]
    el = experts * GB
    span = GB * GROUP // slots
    top = nh - 1
    right = {"hid": jnp.minimum(h + 1, top)}
    left = {"hid": jnp.maximum(h - 1, 0)}
    weights = [
        pltpu.make_async_copy(win, wf.at[0], loc.at[0]),
        pltpu.make_async_copy(wout, wf.at[1], loc.at[1]),
    ]
    for c in weights:
        c.start()
    greet([{"hid": lax.rem(h + k, nh)} for k in range(1, nh)] + [
        {"dp": lax.rem(n + k, nd)} for k in range(1, nd)
    ])
    live = count[0]
    gain = npar[2:3, :]
    bias = npar[3:4, :]
    mask = own_group(slots * span, el)

    def gate_block(b, carry):
        rows = pl.ds(pl.multiple_of(b * span, span), span)
        grows = pl.ds(pl.multiple_of(b * GB, GB), GB)
        spread = expand(stf[:, :, rows], experts, el, True)
        logits = jnp.stack(
            [jnp.where(s < live, spread[s][:, :el], fill_value) for s in range(slots)]
        ).reshape(slots, GB, span // GB, el)
        peak = jnp.max(logits, axis=(0, 2), keepdims=True)
        e = jnp.exp(logits - peak)
        gate = e / jnp.sum(e, axis=(0, 2), keepdims=True)
        gate = jnp.where(mask, gate.reshape(slots * span, el), 0.0).astype(bf16)
        gates[b] = gate
        mean = [v[:, el : el + FS] for v in spread]
        inv = [v[:, el + FS :] for v in spread]
        _, u, dy, _ = block_values(h1f, og, gain, bias, live, rows, mean, inv)
        both = jnp.concatenate([jnp.concatenate(u, 0), jnp.concatenate(dy, 0)], 1)
        mixed = dot_first(gate, both).astype(bf16)
        mout[:, 0, grows, :] = mixed[:, :FS].reshape(experts, GB, FS)
        mout[:, 1, grows, :] = mixed[:, FS:].reshape(experts, GB, FS)
        return carry

    lax.fori_loop(0, seq // span, gate_block, 0)

    def source(k):
        return lax.rem(n - k + nd, nd)

    def to_expert(k):
        e = lax.rem(n + k, nd)
        return remote(mout.at[e], xz.at[h, n], dss.at[k], dsr.at[k], {"dp": e})

    def go_right(k, j):
        piece = xz.at[jnp.maximum(h - j, 0), source(k)]
        return remote(piece, piece, xsr.at[k, j], xrl.at[k, j], right)

    def go_left(k, j):
        piece = xz.at[jnp.minimum(h + j, top), source(k)]
        return remote(piece, piece, xsl.at[k, j], xrr.at[k, j], left)

    def sum_right(k, d):
        piece = inl.at[k, jnp.minimum(h + d, top)]
        return remote(piece, piece, isr.at[k, d], irl.at[k, d - 1], right)

    def sum_left(k, d):
        piece = inr.at[k, jnp.maximum(h - d, 0)]
        return remote(piece, piece, isl.at[k, d], irr.at[k, d - 1], left)

    def from_left(k, d):
        piece = inl.at[k, jnp.minimum(h + d, top)]
        return remote(piece, piece, isr.at[k, d], irl.at[k, d], right)

    def from_right(k, d):
        piece = inr.at[k, jnp.maximum(h - d, 0)]
        return remote(piece, piece, isl.at[k, d], irr.at[k, d], left)

    def to_home(k):
        src = source(k)
        return remote(yo.at[k], yin.at[n], yss.at[k], ysr.at[k], {"dp": src})

    own = pltpu.make_async_copy(mout.at[n], xz.at[h, n], loc.at[2])
    own.start()

    def start_expert(k, carry):
        to_expert(k).start()
        return carry

    lax.fori_loop(1, nd, start_expert, 0)
    for c in weights:
        c.wait()
    wi[...] = wf[0].astype(bf16)
    wo[...] = wf[1].astype(bf16)
    own.wait()

    def expert(k):
        src = source(k)
        slot = lax.rem(k, nh)
        mixed = jnp.concatenate([xz[f, src, 0] for f in range(nh)], axis=1)
        drows = jnp.concatenate([xz[f, src, 1] for f in range(nh)], axis=1)
        pre = dot(mixed, wi[...])
        cube = 0.7978845608028654
        t = jnp.tanh(cube * (pre + 0.044715 * (pre * pre * pre)))
        a = (0.5 * pre * (1.0 + t)).astype(bf16)
        slope = 0.5 * (1.0 + t) + 0.5 * pre * (1.0 - t * t) * (
            cube * (1.0 + 3.0 * 0.044715 * (pre * pre))
        )
        rows = dot(a, wo[...])
        d = (dot_last(drows, wo[...]) * slope).astype(bf16)
        dmix = dot_last(d, wi[...])
        act[src] = a
        dpre[src] = d
        for f in range(nh):
            ps[slot, f, 0] = rows[:, f * FS : (f + 1) * FS].astype(bf16)
            ps[slot, f, 1] = dmix[:, f * FS : (f + 1) * FS].astype(bf16)

    def step(t, carry):
        @pl.when(t < nd)
        def _():
            @pl.when(t > 0)
            def _():
                to_expert(t).wait_recv()

            @pl.when(h < top)
            def _():
                go_right(t, 0).start()

            @pl.when(h > 0)
            def _():
                go_left(t, 0).start()

        for j in range(1, nh):
            k = t - j
            here = jnp.logical_and(k >= 0, k < nd)

            @pl.when(jnp.logical_and(here, h >= j))
            def _(k=k, j=j):
                go_right(k, j - 1).wait_recv()
                if j < top:

                    @pl.when(h < top)
                    def _():
                        go_right(k, j).start()

            @pl.when(jnp.logical_and(here, h + j <= top))
            def _(k=k, j=j):
                go_left(k, j - 1).wait_recv()
                if j < top:

                    @pl.when(h > 0)
                    def _():
                        go_left(k, j).start()

        ke = t - top

        @pl.when(jnp.logical_and(ke >= 0, ke < nd))
        def _():
            expert(ke)

        kr = t - top - h

        @pl.when(jnp.logical_and(kr >= 0, kr < nd))
        def _():
            slot = lax.rem(kr, nh)
            for d in range(nh):

                @pl.when(h + d <= top)
                def _(d=d):
                    dest = jnp.minimum(h + d, top)

                    @pl.when(h > 0)
                    def _():
                        from_left(kr, d).wait_recv()
                        if d > 0:
                            value = inl[kr, dest].astype(f32) + ps[slot, dest].astype(f32)
                            inl[kr, dest] = value.astype(bf16)

                    if d > 0:

                        @pl.when(h == 0)
                        def _():
                            inl[kr, dest] = ps[slot, dest]

                        sum_right(kr, d).start()

        kl = t - top - (top - h)

        @pl.when(jnp.logical_and(kl >= 0, kl < nd))
        def _():
            slot = lax.rem(kl, nh)
            for d in range(nh):

                @pl.when(h - d >= 0)
                def _(d=d):
                    dest = jnp.maximum(h - d, 0)

                    @pl.when(h < top)
                    def _():
                        from_right(kl, d).wait_recv()
                        if d > 0:
                            value = inr[kl, dest].astype(f32) + ps[slot, dest].astype(f32)
                            inr[kl, dest] = value.astype(bf16)

                    if d > 0:

                        @pl.when(h == top)
                        def _():
                            inr[kl, dest] = ps[slot, dest]

                        sum_left(kl, d).start()

        kf = t - 2 * top

        @pl.when(kf >= 0)
        def _():
            slot = lax.rem(kf, nh)

            @pl.when(h == 0)
            def _():
                yo[kf] = (ps[slot, h].astype(f32) + inr[kf, h].astype(f32)).astype(bf16)

            @pl.when(h == top)
            def _():
                yo[kf] = (ps[slot, h].astype(f32) + inl[kf, h].astype(f32)).astype(bf16)

            @pl.when(jnp.logical_and(h > 0, h < top))
            def _():
                value = ps[slot, h].astype(f32) + inl[kf, h].astype(f32)
                yo[kf] = (value + inr[kf, h].astype(f32)).astype(bf16)

            @pl.when(kf > 0)
            def _():
                to_home(kf).start()

        return carry

    lax.fori_loop(0, nd + 2 * top, step, 0)
    mine = pltpu.make_async_copy(yo.at[0], yin.at[n], loc.at[3])
    mine.start()
    total = nd * act.shape[1]
    squares = jnp.zeros((8, FS), f32)
    a_all = act[...].reshape(total, act.shape[2])
    d_all = dpre[...].reshape(total, dpre.shape[2])
    for f in range(nh):
        cols = pl.ds(f * FS, FS)
        gi = dot_first(xz[f, :, 0].reshape(total, FS), d_all)
        go = dot_first(a_all, xz[f, :, 1].reshape(total, FS))
        g_in[cols, :] = gi
        g_out[:, cols] = go
        for m in range(nh):
            part = gi[:, m * FS : (m + 1) * FS]
            squares = squares + jnp.sum((part * part).reshape(FS // 8, 8, FS), 0)
        squares = squares + jnp.sum((go * go).reshape(D // 8, 8, FS), 0)
    sq[...] = squares

    def finish(k, carry):
        @pl.when(k > 0)
        def _():
            to_expert(k).wait_send()
            to_home(k).wait()

        for j in range(top):

            @pl.when(jnp.logical_and(h < top, h >= j))
            def _(j=j):
                go_right(k, j).wait_send()

            @pl.when(jnp.logical_and(h > 0, h + j <= top))
            def _(j=j):
                go_left(k, j).wait_send()

        for d in range(1, nh):

            @pl.when(h + d <= top)
            def _(d=d):
                sum_right(k, d).wait_send()

            @pl.when(h - d >= 0)
            def _(d=d):
                sum_left(k, d).wait_send()

        return carry

    lax.fori_loop(0, nd, finish, 0)
    mine.wait()


def backward_kernel(
    nh, experts, count, h1f, stf, og, npar, gates, yin, p, xi, win, qkvi, kti, headsi, recipi, h1i,
    ein, block_out, fg, tgf, gw, sg,
    p1, py, p1s, pay, x, w, qkv, kt, heads, recip, h1, a1, dk, dv, dqkv, dattn, tgb, pad, small,
    es, pss, psr, sss, ssr, hss, hsr, loc, mloc, lsem, esem
):
    h = lax.axis_index("hid")
    seq = h1f.shape[1]
    slots = h1f.shape[0]
    blocks = seq // BLK
    el = experts * GB
    span = GB * GROUP // slots
    per = BLK // span
    zpeer = [{"hid": lax.rem(h + k, nh)} for k in range(1, nh)]
    held = [(xi, x), (win, w), (h1i, h1), (qkvi, qkv), (kti, kt), (headsi, heads), (recipi, recip)]
    held = [pltpu.make_async_copy(src, dst, lsem.at[i]) for i, (src, dst) in enumerate(held)]
    for c in held:
        c.start()
    loads = [pltpu.make_async_copy(ein[b], es[b], esem.at[b]) for b in range(blocks)]
    for c in reversed(loads):
        c.start()
    greet(zpeer)
    live = count[0]
    gain = npar[2:3, :]
    bias = npar[3:4, :]
    height = experts + 8
    srow = iota((height, el + 2 * FS), 0)
    scol = iota((height, el + 2 * FS), 1)
    target = jnp.where(scol < el, lax.shift_right_logical(scol, 4), experts)
    target = jnp.where(scol >= el + FS, experts + 1, target)
    fold = jnp.where(srow == target, 1.0, 0.0).astype(bf16)
    fold = jnp.concatenate([fold, fold], 1)
    fg[...] = jnp.zeros_like(fg)

    def back_block(b, carry):
        rows = pl.ds(pl.multiple_of(b * span, span), span)
        grows = pl.ds(pl.multiple_of(b * GB, GB), GB)
        spread = expand(stf[:, :, rows], experts, el, False)
        mean = [v[:, :FS] for v in spread]
        inv = [v[:, FS:] for v in spread]
        nhat, u, dy, hid = block_values(h1f, og, gain, bias, live, rows, mean, inv)
        y = jnp.concatenate(
            [yin[:, 0, grows, :].reshape(el, FS), yin[:, 1, grows, :].reshape(el, FS)], 1
        )
        gate = gates[b]
        bd = dot(gate, y)
        dgates = dot_last(
            jnp.concatenate([jnp.concatenate(dy, 0), jnp.concatenate(u, 0)], 1), y
        )
        gate = gate.astype(f32)
        gd = gate * dgates
        gd4 = gd.reshape(slots, GB, span // GB, el)
        inner = jnp.sum(gd4, axis=(0, 2), keepdims=True)
        dlog = gd4 - gate.reshape(slots, GB, span // GB, el) * inner
        dlog = dlog.reshape(slots * span, el)
        qs, qn = [], []
        acc_gain = jnp.zeros((1, FS), f32)
        acc_bias = jnp.zeros((1, FS), f32)
        for s in range(slots):
            part = slice(s * span, (s + 1) * span)
            back = bd[part, :FS]
            du = bd[part, FS:]
            block_out[s, rows, :] = jnp.where(s < live, hid[s] + back, 0.0).astype(bf16)
            q = du * gain
            p1[s, rows, :] = (dy[s].astype(f32) + inv[s] * q).astype(bf16)
            acc_gain = acc_gain + jnp.sum(du * nhat[s], 0, keepdims=True)
            acc_bias = acc_bias + jnp.sum(du, 0, keepdims=True)
            qs.append(q)
            qn.append(q * nhat[s])
        high, low = split(
            jnp.concatenate([dlog, jnp.concatenate(qs, 0), jnp.concatenate(qn, 0)], 1)
        )
        folded = dot_last(fold, jnp.concatenate([high, low], 1))
        for s in range(slots):
            py[s, :, rows] = folded[:, s * span : (s + 1) * span]
        fg[2:3, :] += acc_gain
        fg[3:4, :] += acc_bias
        return carry

    arrive = [None] * blocks
    sends = []
    for c in reversed(range(blocks)):
        lax.fori_loop(c * per, (c + 1) * per, back_block, 0)
        rows = pl.ds(c * BLK, BLK)
        mine = [
            pltpu.make_async_copy(p1.at[h, rows], p1s.at[h, rows], mloc.at[c, 0]),
            pltpu.make_async_copy(py.at[h, :, rows], pay.at[h, :, rows], mloc.at[c, 1]),
        ]
        for m in mine:
            m.start()
        far = []
        for k in range(nh - 1):
            peer = lax.rem(h + k + 1, nh)
            a = remote(p1.at[peer, rows], p1s.at[h, rows], pss.at[c, k], psr.at[c, k], zpeer[k])
            s = remote(
                py.at[peer, :, rows], pay.at[h, :, rows], sss.at[c, k], ssr.at[c, k], zpeer[k]
            )
            a.start()
            s.start()
            far += [a, s]
        arrive[c] = (mine, far)
    controller_rows(p, pad, experts)
    gain1 = row_of(p, 0)
    bias1 = row_of(p, 1)
    gain2 = row_of(p, 2)
    bias2 = row_of(p, 3)
    lane = iota((BLK, FS), 1)
    low_half = lane < HS
    er = iota((3 * height, FS), 0)
    er = jnp.where(er >= 2 * height, er - 2 * height, er)
    er = jnp.where(er >= height, er - height, er)
    eye = jnp.where(er == iota((3 * height, FS), 1), 1.0, 0.0).astype(bf16)
    pick = iota((8, 2 * FS), 1) & (FS - 1)
    row = iota((8, 2 * FS), 0)
    pick = ((row == 0) & (pick < HS)) | ((row == 1) & (pick >= HS))
    pick = jnp.where(pick, 1.0, 0.0).astype(bf16)
    small[...] = jnp.zeros_like(small)
    for c in held:
        c.wait()
    for b in reversed(range(blocks)):
        rows = pl.ds(b * BLK, BLK)
        last = b == blocks - 1
        e_ref = es[b]
        mine, far = arrive[b]
        for c in mine:
            c.wait()
        for c in far:
            c.wait_recv()
        total = pay[0, :, rows]
        for f in range(1, nh):
            total = total + pay[f, :, rows]
        cols = dot_first(jnp.concatenate(split3(total), 0), eye)
        s1 = cols[:, experts : experts + 1]
        s2 = cols[:, experts + 1 : experts + 2]
        hidden = h1[rows, :]
        nhat, _, inv = standardize(hidden)
        ch, cl = split(jnp.where(lane < experts, cols, 0.0))
        du = dot(
            jnp.concatenate([ch, cl, ch], 1),
            jnp.concatenate([pad[0], pad[0], pad[1]], 0).astype(bf16),
        )
        q = du * gain2
        mq = (s1 + jnp.sum(q, -1, keepdims=True)) / D
        mqn = (s2 + jnp.sum(q * nhat, -1, keepdims=True)) / D
        dh1 = features(p1s, rows).astype(f32) + inv * (q - mq - nhat * mqn)
        small[2:3, :] += jnp.sum(du * nhat, 0, keepdims=True)
        small[3:4, :] += jnp.sum(du, 0, keepdims=True)
        routed = dot_first(
            jnp.concatenate([ch, cl], 1), (nhat * gain2 + bias2).astype(bf16)
        )
        small[8 : 8 + experts, :] += routed[0:experts] + routed[FS : FS + experts]
        dattn[rows, :] = dh1.astype(bf16)
        loads[b].wait()

        def pair(hp, carry):
            dh = dot(dattn[rows, :], w[hp].reshape(D, D)[:, 3 * FS :]).astype(bf16).astype(f32)
            dh = dh * recip[hp, rows, :]
            high, rest = split(dh * heads[hp, rows, :].astype(f32))
            inner = dot_last(pick, jnp.concatenate([high, rest], 1))
            inner = jnp.concatenate([inner[0:1], inner[1:2]], 1)
            dhs = both_heads(dh.astype(bf16))
            qs = both_heads(qkv[hp, rows, 0:FS])
            dqt = jnp.zeros((FS, 2 * BLK), f32)
            for j in range(b + 1):
                keys = slice(j * BLK, (j + 1) * BLK)
                e = e_ref[hp, keys, :]
                dp = dot_last(qkv[hp, keys, 2 * FS :], dhs)
                ds = (e.astype(f32) * (dp - inner)).astype(bf16)
                dqt = dqt + dot(kt[hp, :, keys], ds)
                if last:
                    dk[hp, keys, :] = dot(ds, qs)
                    dv[hp, keys, :] = dot(e, dhs)
                else:
                    dk[hp, keys, :] += dot(ds, qs)
                    dv[hp, keys, :] += dot(e, dhs)
            dq = jnp.where(low_half, dqt[:, :BLK].T, dqt[:, BLK:].T)
            dqkv[hp, rows, 0:FS] = (dq * HS**-0.5).astype(bf16)
            dqkv[hp, rows, FS : 2 * FS] = dk[hp, rows, :].astype(bf16)
            dqkv[hp, rows, 2 * FS :] = dv[hp, rows, :].astype(bf16)
            return carry

        lax.fori_loop(0, nh, pair, 0)
        da1 = jnp.zeros((BLK, D), f32)
        for hp in range(nh):
            da1 = da1 + dot_last(dqkv[hp, rows, :], w[hp].reshape(D, D)[:, : 3 * FS])
        hat, _, inv1 = standardize(features(x, rows).astype(f32))
        a1[rows, :] = (hat * gain1 + bias1).astype(bf16)
        q1 = da1 * gain1
        m1 = jnp.sum(q1, -1, keepdims=True) / D
        m2 = jnp.sum(q1 * hat, -1, keepdims=True) / D
        tg = dh1 + inv1 * (q1 - m1 - hat * m2)
        small[0:1, :] += jnp.sum(da1 * hat, 0, keepdims=True)
        small[1:2, :] += jnp.sum(da1, 0, keepdims=True)
        for f in range(nh):
            tgb[f, rows, :] = tg[:, f * FS : (f + 1) * FS].astype(bf16)
        mine = pltpu.make_async_copy(tgb.at[h, rows], tgf.at[h, rows], loc.at[b])
        mine.start()
        sends.append(mine)
        for k in range(nh - 1):
            peer = lax.rem(h + k + 1, nh)
            c = remote(tgb.at[peer, rows], tgf.at[h, rows], hss.at[b, k], hsr.at[b, k], zpeer[k])
            c.start()
            sends.append(c)

    def weight_grads(hp, carry):
        gi = dot_first(a1[...], dqkv[hp]).astype(bf16)
        go = dot_first(dattn[...], heads[hp]).astype(bf16)
        gw[hp] = jnp.concatenate([gi, go], 1).reshape(gw.shape[1:])
        return carry

    lax.fori_loop(0, nh, weight_grads, 0)
    for f in range(nh):
        sg[f] = small[:, f * FS : (f + 1) * FS]
    for _, far in arrive:
        for c in far:
            c.wait_send()
    for c in sends:
        c.wait()


def block_kernel(
    nd, nh, experts, count, tok, attn_in, attn_out, npar, control, og_in, win, wout,
    block_out, tgf, g_in, g_out, gsum, ssum, norm,
    wblk, pblk, x, w, p, a1, qkv, kt, vt, heads, recip, h1, es, h1b, st, h1f, stf, og, gates, mout, xz,
    act, dpre, ps, inl, inr, yin, wi, wo, py, p1s, pay, dk, dv, pad, small,
    fg, sg, dacc, gwb, wc_in, ch, wr, zs, zr, szr, sdb, sdr, sqb, sqd, sqz,
    tss, tsr, wss, wsr, dss, dsr, css, csr, pss, psr, hss, hsr, sss, ssr,
    ess, esr, xsr, xsl, xrl, xrr, isr, isl, irl, irr, yss, ysr,
    bss, bsr, vss, vsr, gss, gsr, ass, asr, cts, ctr, zss, zsr, sms, smr, sns, snr,
    qss, qsr, rss, rsr, loc, hloc, ploc, gloc, wloc, oloc
):
    n = lax.axis_index("dp")
    h = lax.axis_index("hid")
    core = lax.rem(n, 2)
    chip = lax.div(n, 2)
    chips = nd // 2
    top = nh - 1
    slots, seq = h1f.shape[0], h1f.shape[1]
    blocks = seq // BLK
    el = experts * GB
    span = GB * GROUP // slots
    per = BLK // span
    right = {"hid": jnp.minimum(h + 1, top)}
    left = {"hid": jnp.maximum(h - 1, 0)}
    zid = [lax.rem(h + k, nh) for k in range(1, nh)]
    zpeer = [{"hid": z} for z in zid]
    did = [lax.rem(n + k, nd) for k in range(1, nd)]
    cid = [lax.rem(chip + k, chips) * 2 + core for k in range(1, chips)]
    partner = {"dp": chip * 2 + 1 - core}
    ends = []
    sent = []
    gathers = []
    scatters = []
    for m in range(3):
        wblk[:, m * FS : (m + 1) * FS] = attn_in[m].astype(bf16)
    wblk[:, 3 * FS :] = attn_out[...].astype(bf16)
    pblk[0:4, :] = npar[...]
    pblk[4:8, :] = jnp.zeros((4, FS), f32)
    pblk[8:, :] = control[...]

    def local(src, dst, sem):
        c = pltpu.make_async_copy(src, dst, sem)
        c.start()
        return c

    def far(src, dst, send, recv, peer):
        c = remote(src, dst, send, recv, peer)
        c.start()
        sent.append(c)
        return c

    og_load = local(og_in, og, loc.at[0])
    x_load = local(tok.at[h], x.at[h], loc.at[1])
    w_loads = []
    for f in range(nh):
        cols = pl.ds(f * FS, FS)
        w_loads.append(local(win.at[:, cols], dk.at[f, 0:D], wloc.at[f, 0]))
        w_loads.append(local(wout.at[:, cols], dk.at[f, D : 2 * D], wloc.at[f, 1]))
    greet(zpeer + [{"dp": d} for d in did])
    w_own = local(wblk, w.at[h, chip, core], loc.at[2])
    p_own = local(pblk, p.at[h], loc.at[3])
    wz = [
        far(wblk, w.at[h, chip, core], wss.at[k], wsr.at[k], zpeer[k]) for k in range(nh - 1)
    ]
    pz = [far(pblk, p.at[h], pss.at[k], psr.at[k], zpeer[k]) for k in range(nh - 1)]

    def rows_of(b):
        return pl.ds(b * BLK, BLK)

    def send_tokens(b):
        rows = rows_of(b)
        return [
            far(tok.at[zid[k], rows], x.at[h, rows], tss.at[b, k], tsr.at[b, k], zpeer[k])
            for k in range(nh - 1)
        ]

    tz = {b: send_tokens(b) for b in range(blocks)}
    w_own.wait()
    wc = []
    for j in range(nh):
        piece = lax.rem(h - j + nh, nh)
        if j > 0:
            wz[j - 1].wait_recv()
        part = w.at[piece, chip, core]
        wc.append(
            [far(part, part, dss.at[j, k], dsr.at[j, k], {"dp": cid[k]}) for k in range(chips - 1)]
        )
    p_own.wait()
    for c in pz:
        c.wait_recv()
    controller_rows(p, pad, experts)
    gain1 = row_of(p, 0)
    bias1 = row_of(p, 1)
    gain2 = row_of(p, 2)
    bias2 = row_of(p, 3)
    scale = jnp.where(iota((BLK, 3 * FS), 1) < FS, HS**-0.5, 1.0).astype(bf16)
    lane = iota((BLK, FS), 1)
    low_half = lane < HS
    causal = iota((BLK, 2 * BLK), 0) <= (iota((BLK, 2 * BLK), 1) & (BLK - 1))
    one = jnp.ones((FS, BLK), bf16)
    low_rows = iota((FS, BLK), 0) < HS
    wp = []

    def pass_weights(j):
        for c in wc[j]:
            c.wait_recv()
        part = w.at[lax.rem(h - j + nh, nh), :, core]
        wp.append(far(part, part, css.at[j], csr.at[j], partner))

    def begin(b):
        for c in tz[b]:
            c.wait_recv()
        normed, _, _ = standardize(features(x, rows_of(b)).astype(f32))
        a1[rows_of(b), :] = (normed * gain1 + bias1).astype(bf16)

    def attend(b, hp):
        rows = rows_of(b)
        past = b * BLK
        e_ref = es[b]
        proj = dot(a1[rows, :], w[hp].reshape(D, D)[:, : 3 * FS])
        low = proj.astype(bf16) * scale
        qkv[hp, rows, :] = low
        kt[hp, :, rows] = proj[:, FS : 2 * FS].T.astype(bf16)
        vt[hp, :, rows] = proj[:, 2 * FS :].T.astype(bf16)
        q = both_heads(low[:, :FS])
        s_now = dot_last(low[:, FS : 2 * FS], q)
        s_now = jnp.where(causal, s_now, fill_value)
        peak = jnp.max(s_now, 0, keepdims=True)
        if b > 0:
            s_past = dot_last(qkv[hp, 0:past, FS : 2 * FS], q)
            peak = jnp.maximum(peak, jnp.max(s_past, 0, keepdims=True))
            e_ref[hp, 0:past, :] = jnp.exp(s_past - peak).astype(bf16)
        e_ref[hp, past : past + BLK, :] = jnp.exp(s_now - peak).astype(bf16)
        outs = []
        for half in range(2):
            total = jnp.zeros((FS, BLK), f32)
            for j in range(b + 1):
                keys = slice(j * BLK, (j + 1) * BLK)
                v = vt[hp, :, keys]
                v = jnp.where(low_rows, v, one) if half == 0 else jnp.where(low_rows, one, v)
                total = total + dot(v, e_ref[hp, keys, half * BLK : (half + 1) * BLK])
            outs.append(total.T)
        value = jnp.where(low_half, outs[0], outs[1])
        total = jnp.where(low_half, pltpu.roll(outs[0], HS, 1), pltpu.roll(outs[1], HS, 1))
        inv = 1.0 / total
        recip[hp, rows, :] = inv
        heads[hp, rows, :] = (value * inv).astype(bf16)

    def attend_loop(b, first, last):
        def body(hp, carry):
            attend(b, hp)
            return carry

        lax.fori_loop(first, last, body, 0)

    hz = {}

    def finish(b):
        rows = rows_of(b)
        attn = jnp.zeros((BLK, D), f32)
        for hp in range(nh):
            attn = attn + dot_last(heads[hp, rows, :], w[hp].reshape(D, D)[:, 3 * FS :])
        hidden = features(x, rows).astype(f32) + attn
        h1[rows, :] = hidden
        normed, center, inv = standardize(hidden)
        u = normed * gain2 + bias2
        uh, ul = split(u)
        cols = dot_last(
            jnp.concatenate([uh, ul, uh], 1),
            jnp.concatenate([pad[0], pad[0], pad[1]], 1).astype(bf16),
        )
        cols = jnp.where(lane == experts, center, jnp.where(lane == experts + 1, inv, cols))
        st[:, rows] = cols.T[0 : experts + 8, :]
        for f in range(nh):
            h1b[f, rows, :] = hidden[:, f * FS : (f + 1) * FS].astype(bf16)
        mine = [
            local(h1b.at[h, rows], h1f.at[h, rows], hloc.at[b, 0]),
            local(st.at[:, rows], stf.at[h, :, rows], hloc.at[b, 1]),
        ]
        away = []
        for k in range(nh - 1):
            away.append(
                far(h1b.at[zid[k], rows], h1f.at[h, rows], hss.at[b, k], hsr.at[b, k], zpeer[k])
            )
            away.append(
                far(st.at[:, rows], stf.at[h, :, rows], sss.at[b, k], ssr.at[b, k], zpeer[k])
            )
        hz[b] = (mine, away)

    live = count[0]
    gain = npar[2:3, :]
    bias = npar[3:4, :]
    mask = own_group(slots * span, el)

    def gate(c):
        mine, away = hz[c]
        for v in mine:
            v.wait()
        for v in away:
            v.wait_recv()

        def body(i, carry):
            rows = pl.ds(pl.multiple_of(c * BLK + i * span, span), span)
            grows = pl.ds(pl.multiple_of(i * GB, GB), GB)
            spread = expand(stf[:, :, rows], experts, el, True)
            logits = jnp.stack(
                [jnp.where(s < live, spread[s][:, :el], fill_value) for s in range(slots)]
            ).reshape(slots, GB, span // GB, el)
            peak = jnp.max(logits, axis=(0, 2), keepdims=True)
            e = jnp.exp(logits - peak)
            g = e / jnp.sum(e, axis=(0, 2), keepdims=True)
            g = jnp.where(mask, g.reshape(slots * span, el), 0.0).astype(bf16)
            gates[c * per + i] = g
            mean = [v[:, el : el + FS] for v in spread]
            inv = [v[:, el + FS :] for v in spread]
            _, u, dy, _ = block_values(h1f, og, gain, bias, live, rows, mean, inv)
            both = jnp.concatenate([jnp.concatenate(u, 0), jnp.concatenate(dy, 0)], 1)
            mixed = dot_first(g, both).astype(bf16)
            mout[c, :, 0, grows, :] = mixed[:, :FS].reshape(experts, GB, FS)
            mout[c, :, 1, grows, :] = mixed[:, FS:].reshape(experts, GB, FS)
            return carry

        lax.fori_loop(0, per, body, 0)
        ez[c] = [
            far(mout.at[c, did[k]], xz.at[c, h, n], ess.at[c, k], esr.at[c, k], {"dp": did[k]})
            for k in range(nd - 1)
        ]
        xz[c, h, n] = mout[c, n]

    ez = {}

    def go_right(c, j):
        piece = xz.at[c, jnp.maximum(h - j, 0)]
        return remote(piece, piece, xsr.at[c, j], xrl.at[c, j], right)

    def go_left(c, j):
        piece = xz.at[c, jnp.minimum(h + j, top)]
        return remote(piece, piece, xsl.at[c, j], xrr.at[c, j], left)

    def gather(c, j):
        if j < top:
            gathers.append((c, j))
        if j == 0:
            for v in ez[c]:
                v.wait_recv()

            @pl.when(h < top)
            def _():
                go_right(c, 0).start()

            @pl.when(h > 0)
            def _():
                go_left(c, 0).start()

            return

        @pl.when(h >= j)
        def _():
            go_right(c, j - 1).wait_recv()
            if j < top:

                @pl.when(h < top)
                def _():
                    go_right(c, j).start()

        @pl.when(h + j <= top)
        def _():
            go_left(c, j - 1).wait_recv()
            if j < top:

                @pl.when(h > 0)
                def _():
                    go_left(c, j).start()

    count_rows = xz.shape[2] * xz.shape[4]

    def rows_at(c, f, kind):
        return xz[c, f, :, kind].reshape(count_rows, FS)

    def expert(c):
        mixed = jnp.concatenate([rows_at(c, f, 0) for f in range(nh)], axis=1)
        drows = jnp.concatenate([rows_at(c, f, 1) for f in range(nh)], axis=1)
        pre = dot(mixed, wi[...])
        cube = 0.7978845608028654
        t = jnp.tanh(cube * (pre + 0.044715 * (pre * pre * pre)))
        a = (0.5 * pre * (1.0 + t)).astype(bf16)
        slope = 0.5 * (1.0 + t) + 0.5 * pre * (1.0 - t * t) * (
            cube * (1.0 + 3.0 * 0.044715 * (pre * pre))
        )
        act[c] = a
        rows = dot(a, wo[...])
        d = (dot_last(drows, wo[...]) * slope).astype(bf16)
        dpre[c] = d
        dmix = dot_last(d, wi[...])
        shape = (xz.shape[2], xz.shape[4], FS)
        for f in range(nh):
            ps[c, f, :, 0] = rows[:, f * FS : (f + 1) * FS].astype(bf16).reshape(shape)
            ps[c, f, :, 1] = dmix[:, f * FS : (f + 1) * FS].astype(bf16).reshape(shape)

    def sum_right(c, d, mark):
        piece = inl.at[c, jnp.minimum(h + d, top)]
        return remote(piece, piece, isr.at[c, d], irl.at[c, mark], right)

    def sum_left(c, d, mark):
        piece = inr.at[c, jnp.maximum(h - d, 0)]
        return remote(piece, piece, isl.at[c, d], irr.at[c, mark], left)

    def scatter(c, stage):
        scatters.append((c, stage))

        @pl.when(h == stage)
        def _():
            for d in reversed(range(1, nh - stage)):
                dest = stage + d
                if stage > 0:
                    sum_right(c, d, d).wait_recv()
                    value = inl[c, dest].astype(f32) + ps[c, dest].astype(f32)
                    inl[c, dest] = value.astype(bf16)
                else:
                    inl[c, dest] = ps[c, dest]
                sum_right(c, d, d - 1).start()

        @pl.when(h == top - stage)
        def _():
            for d in reversed(range(1, nh - stage)):
                dest = top - stage - d
                if stage > 0:
                    sum_left(c, d, d).wait_recv()
                    value = inr[c, dest].astype(f32) + ps[c, dest].astype(f32)
                    inr[c, dest] = value.astype(bf16)
                else:
                    inr[c, dest] = ps[c, dest]
                sum_left(c, d, d - 1).start()

    yz = {}

    def home(c):
        for v in ez[c]:
            v.wait_send()
            sent[:] = [o for o in sent if o is not v]
        @pl.when(h > 0)
        def _():
            sum_right(c, 0, 0).wait_recv()

        @pl.when(h < top)
        def _():
            sum_left(c, 0, 0).wait_recv()

        @pl.when(h == 0)
        def _():
            mout[c] = (ps[c, 0].astype(f32) + inr[c, 0].astype(f32)).astype(bf16)

        @pl.when(h == top)
        def _():
            mout[c] = (ps[c, top].astype(f32) + inl[c, top].astype(f32)).astype(bf16)

        for m in range(1, top):

            @pl.when(h == m)
            def _(m=m):
                value = ps[c, m].astype(f32) + inl[c, m].astype(f32)
                mout[c] = (value + inr[c, m].astype(f32)).astype(bf16)

        yz[c] = []
        for k in range(1, nd):
            src = lax.rem(n - k + nd, nd)
            yz[c].append(
                far(mout.at[c, src], yin.at[c, n], yss.at[c, k], ysr.at[c, k], {"dp": src})
            )
        yin[c, n] = mout[c, n]

    height = experts + 8
    srow = iota((height, el + 2 * FS), 0)
    scol = iota((height, el + 2 * FS), 1)
    target = jnp.where(scol < el, lax.shift_right_logical(scol, 4), experts)
    target = jnp.where(scol >= el + FS, experts + 1, target)
    fold = jnp.where(srow == target, 1.0, 0.0).astype(bf16)
    fold = jnp.concatenate([fold, fold], 1)
    fg[...] = jnp.zeros_like(fg)

    def back(c):
        for v in yz[c]:
            v.wait_recv()

        def body(i, carry):
            rows = pl.ds(pl.multiple_of(c * BLK + i * span, span), span)
            grows = pl.ds(pl.multiple_of(i * GB, GB), GB)
            spread = expand(stf[:, :, rows], experts, el, False)
            mean = [v[:, :FS] for v in spread]
            inv = [v[:, FS:] for v in spread]
            nhat, u, dy, hid = block_values(h1f, og, gain, bias, live, rows, mean, inv)
            y = jnp.concatenate(
                [yin[c, :, 0, grows, :].reshape(el, FS), yin[c, :, 1, grows, :].reshape(el, FS)], 1
            )
            g = gates[c * per + i]
            bd = dot(g, y)
            dgates = dot_last(
                jnp.concatenate([jnp.concatenate(dy, 0), jnp.concatenate(u, 0)], 1), y
            )
            g = g.astype(f32)
            gd = (g * dgates).reshape(slots, GB, span // GB, el)
            inner = jnp.sum(gd, axis=(0, 2), keepdims=True)
            dlog = gd - g.reshape(slots, GB, span // GB, el) * inner
            dlog = dlog.reshape(slots * span, el)
            qs, qn = [], []
            acc_gain = jnp.zeros((1, FS), f32)
            acc_bias = jnp.zeros((1, FS), f32)
            for s in range(slots):
                part = slice(s * span, (s + 1) * span)
                du = bd[part, FS:]
                h1f[s, rows, :] = jnp.where(s < live, hid[s] + bd[part, :FS], 0.0).astype(bf16)
                q = du * gain
                og[s, rows, :] = (dy[s].astype(f32) + inv[s] * q).astype(bf16)
                acc_gain = acc_gain + jnp.sum(du * nhat[s], 0, keepdims=True)
                acc_bias = acc_bias + jnp.sum(du, 0, keepdims=True)
                qs.append(q)
                qn.append(q * nhat[s])
            high, low = split(
                jnp.concatenate([dlog, jnp.concatenate(qs, 0), jnp.concatenate(qn, 0)], 1)
            )
            folded = dot_last(fold, jnp.concatenate([high, low], 1))
            for s in range(slots):
                py[s, :, rows] = folded[:, s * span : (s + 1) * span].astype(bf16)
            fg[2:3, :] += acc_gain
            fg[3:4, :] += acc_bias
            return carry

        lax.fori_loop(0, per, body, 0)
        rows = rows_of(c)
        ends.append(local(h1f.at[:, rows], block_out.at[:, rows], oloc.at[c]))

    dz = {}

    def send_back(c):
        rows = rows_of(c)
        mine = [
            local(og.at[h, rows], p1s.at[h, rows], ploc.at[c, 0]),
            local(py.at[h, :, rows], pay.at[h, :, rows], ploc.at[c, 1]),
        ]
        away = []
        for k in range(nh - 1):
            away.append(
                far(og.at[zid[k], rows], p1s.at[h, rows], bss.at[c, k], bsr.at[c, k], zpeer[k])
            )
            away.append(
                far(py.at[zid[k], :, rows], pay.at[h, :, rows], vss.at[c, k], vsr.at[c, k], zpeer[k])
            )
        dz[c] = (mine, away)

    def expert_grads():
        total = blocks * count_rows
        squares = jnp.zeros((8, FS), f32)
        a_all = act[...].reshape(total, act.shape[2])
        d_all = dpre[...].reshape(total, dpre.shape[2])
        for f in range(nh):
            gi = dot_first(xz[:, f, :, 0].reshape(total, FS), d_all)
            go = dot_first(a_all, xz[:, f, :, 1].reshape(total, FS))
            dv[f, 0:D, :] = go
            for m in range(nh):
                part = gi[:, m * FS : (m + 1) * FS]
                dv[m, D + f * FS : D + (f + 1) * FS, :] = part
                squares = squares + jnp.sum((part * part).reshape(FS // 8, 8, FS), 0)
            squares = squares + jnp.sum((go * go).reshape(D // 8, 8, FS), 0)
        sqb[0] = squares
        for f in range(nh):
            cols = pl.ds(f * FS, FS)
            grads.append(local(dv.at[f, 0:D], g_out.at[:, cols], wloc.at[f, 0]))
            grads.append(local(dv.at[f, D : 2 * D], g_in.at[:, cols], wloc.at[f, 1]))

    grads = []

    x_load.wait()
    og_load.wait()
    for v in w_loads:
        v.wait()
    for f in range(nh):
        cols = pl.ds(f * FS, FS)
        wi[:, cols] = dk[f, 0:D].astype(bf16)
        wo[:, cols] = dk[f, D : 2 * D].astype(bf16)
    pass_weights(0)
    begin(0)
    for j in range(nh):
        if j + 1 < nh:
            pass_weights(j + 1)
        wp[j].wait_recv()
        attend(0, lax.rem(h - j + nh, nh))
    finish(0)
    begin(1)
    attend_loop(1, 0, nh)
    finish(1)
    gate(0)
    begin(2)
    attend_loop(2, 0, 2)
    gather(0, 0)
    attend_loop(2, 2, nh)
    finish(2)
    gate(1)
    gather(0, 1)
    begin(3)
    attend_loop(3, 0, 2)
    gather(1, 0)
    attend_loop(3, 2, 3)
    gather(0, 2)
    attend_loop(3, 3, nh)
    gather(1, 1)
    finish(3)
    gather(0, 3)
    expert(0)
    scatter(0, 0)
    gate(2)
    gather(1, 2)
    gather(2, 0)
    scatter(0, 1)
    gather(1, 3)
    expert(1)
    scatter(1, 0)
    gather(2, 1)
    gate(3)
    scatter(0, 2)
    scatter(1, 1)
    gather(2, 2)
    gather(3, 0)
    home(0)
    scatter(1, 2)
    gather(2, 3)
    expert(2)
    scatter(2, 0)
    gather(3, 1)
    scatter(2, 1)
    home(1)
    back(0)
    gather(3, 2)
    scatter(2, 2)
    gather(3, 3)
    expert(3)
    scatter(3, 0)
    home(2)
    scatter(3, 1)
    back(1)
    scatter(3, 2)
    back(2)
    home(3)
    back(3)
    for c in reversed(range(blocks)):
        send_back(c)
    expert_grads()
    er = iota((3 * height, FS), 0)
    er = jnp.where(er >= 2 * height, er - 2 * height, er)
    er = jnp.where(er >= height, er - height, er)
    eye = jnp.where(er == iota((3 * height, FS), 1), 1.0, 0.0).astype(bf16)
    pick = iota((8, 2 * FS), 1) & (FS - 1)
    row = iota((8, 2 * FS), 0)
    pick = ((row == 0) & (pick < HS)) | ((row == 1) & (pick >= HS))
    pick = jnp.where(pick, 1.0, 0.0).astype(bf16)
    small[...] = jnp.zeros_like(small)
    for b in range(blocks):
        for v in hz[b][1]:
            v.wait_send()
            sent[:] = [c for c in sent if c is not v]
    tgb = h1b

    def arrive(b):
        rows = rows_of(b)
        mine, away = dz[b]
        for v in mine:
            v.wait()
        for v in away:
            v.wait_recv()
        total = pay[0, :, rows].astype(f32)
        for f in range(1, nh):
            total = total + pay[f, :, rows].astype(f32)
        cols = dot_first(jnp.concatenate(split3(total), 0), eye)
        s1 = cols[:, experts : experts + 1]
        s2 = cols[:, experts + 1 : experts + 2]
        nhat, _, inv = standardize(h1[rows, :])
        ch, cl = split(jnp.where(lane < experts, cols, 0.0))
        du = dot(
            jnp.concatenate([ch, cl, ch], 1),
            jnp.concatenate([pad[0], pad[0], pad[1]], 0).astype(bf16),
        )
        q = du * gain2
        mq = (s1 + jnp.sum(q, -1, keepdims=True)) / D
        mqn = (s2 + jnp.sum(q * nhat, -1, keepdims=True)) / D
        dh1 = features(p1s, rows).astype(f32) + inv * (q - mq - nhat * mqn)
        small[2:3, :] += jnp.sum(du * nhat, 0, keepdims=True)
        small[3:4, :] += jnp.sum(du, 0, keepdims=True)
        routed = dot_first(jnp.concatenate([ch, cl], 1), (nhat * gain2 + bias2).astype(bf16))
        small[8 : 8 + experts, :] += routed[0:experts] + routed[FS : FS + experts]
        act[b] = dh1.astype(bf16)
        h1[rows, :] = dh1

    def pair(b, hp):
        rows = rows_of(b)
        e_ref = es[b]
        dh = dot(act[b], w[hp].reshape(D, D)[:, 3 * FS :]).astype(bf16).astype(f32)
        dh = dh * recip[hp, rows, :]
        high, rest = split(dh * heads[hp, rows, :].astype(f32))
        inner = dot_last(pick, jnp.concatenate([high, rest], 1))
        inner = jnp.concatenate([inner[0:1], inner[1:2]], 1)
        dhs = both_heads(dh.astype(bf16))
        qs = both_heads(qkv[hp, rows, 0:FS])
        stop = (b + 1) * BLK
        e = e_ref[hp]
        dp = dot_last(qkv[hp, 0:stop, 2 * FS :], dhs)
        ds = (e.astype(f32) * (dp - inner)).astype(bf16)
        dqt = dot(kt[hp, :, 0:stop], ds)
        if b == blocks - 1:
            dk[hp] = dot(ds, qs)
            dv[hp] = dot(e, dhs)
        else:
            dk[hp, 0:stop, :] += dot(ds, qs)
            dv[hp, 0:stop, :] += dot(e, dhs)
        dq = jnp.where(low_half, dqt[:, :BLK].T, dqt[:, BLK:].T)
        qkv[hp, rows, 0:FS] = (dq * HS**-0.5).astype(bf16)
        qkv[hp, rows, FS : 2 * FS] = dk[hp, rows, :].astype(bf16)
        qkv[hp, rows, 2 * FS :] = dv[hp, rows, :].astype(bf16)

    def pairs(b, first, last):
        def body(hp, carry):
            pair(b, hp)
            return carry

        lax.fori_loop(first, last, body, 0)
        total = jnp.zeros((BLK, D), f32)
        for hp in range(first, last):
            total = total + dot_last(qkv[hp, rows_of(b), :], w[hp].reshape(D, D)[:, : 3 * FS])
        return total

    def settle(b, da1):
        rows = rows_of(b)
        hat, _, inv1 = standardize(features(x, rows).astype(f32))
        q1 = da1 * gain1
        m1 = jnp.sum(q1, -1, keepdims=True) / D
        m2 = jnp.sum(q1 * hat, -1, keepdims=True) / D
        tg = h1[rows, :] + inv1 * (q1 - m1 - hat * m2)
        small[0:1, :] += jnp.sum(da1 * hat, 0, keepdims=True)
        small[1:2, :] += jnp.sum(da1, 0, keepdims=True)
        for f in range(nh):
            tgb[f, rows, :] = tg[:, f * FS : (f + 1) * FS].astype(bf16)
        ends.append(local(tgb.at[h, rows], tgf.at[h, rows], gloc.at[b]))
        for k in range(nh - 1):
            c = remote(
                tgb.at[zid[k], rows], tgf.at[h, rows], gss.at[b, k], gsr.at[b, k], zpeer[k]
            )
            c.start()
            ends.append(c)

    ring = {}

    def weight_grads(hp):
        gi = dot_first(a1[...], qkv[hp]).astype(bf16)
        go = dot_first(act[...].reshape(seq, D), heads[hp]).astype(bf16)
        gwb[hp] = jnp.concatenate([gi, go], 1).reshape(gwb.shape[1:])
        ring[hp] = far(gwb.at[hp, :, 1 - core], wc_in.at[hp], ass.at[hp], asr.at[hp], partner)

    cnum = [lax.rem(chip + k, chips) for k in range(1, chips)]

    def over_chips(hp):
        ring[hp].wait_recv()
        ch[hp] = (gwb[hp, :, core].astype(f32) + wc_in[hp].astype(f32)).astype(bf16)
        ring[hp] = [
            far(ch.at[hp, cnum[k]], wr.at[hp, k], cts.at[hp, k], ctr.at[hp, k], {"dp": cid[k]})
            for k in range(chips - 1)
        ]

    def to_owner(hp):
        return remote(zs.at[hp], zr.at[h], zss.at[hp], zsr.at[h], {"hid": hp})

    def over_z(hp):
        for v in ring[hp]:
            v.wait_recv()
        total = ch[hp, chip].astype(f32)
        for k in range(chips - 1):
            total = total + wr[hp, k].astype(f32)
        zs[hp] = total.astype(bf16)

        @pl.when(h != hp)
        def _():
            to_owner(hp).start()

        @pl.when(h == hp)
        def _():
            zr[hp] = zs[hp]

    half = nh // 2
    for b in reversed(range(blocks)):
        arrive(b)
        if b == blocks - 1:
            for v in grads:
                v.wait()
        if b >= 2:
            settle(b, pairs(b, 0, nh))
        else:
            dacc[rows_of(b), :] = pairs(b, 0, half)
    for hp in range(half):
        weight_grads(hp)
    settle(1, dacc[rows_of(1), :] + pairs(1, half, nh))
    for hp in range(half):
        over_chips(hp)
    settle(0, dacc[rows_of(0), :] + pairs(0, half, nh))
    for hp in range(half, nh):
        weight_grads(hp)
    for hp in range(half, nh):
        over_chips(hp)
    for hp in range(half):
        over_z(hp)
    for f in range(nh):
        sg[f] = small[:, f * FS : (f + 1) * FS]
    sz = [far(sg.at[zid[k]], szr.at[k], sms.at[k], smr.at[k], zpeer[k]) for k in range(nh - 1)]
    for c in sz:
        c.wait_recv()
    part = sg[h]
    for k in range(nh - 1):
        part = part + szr[k]
    part = jnp.concatenate([part[0:8] + fg[...], part[8:]], 0)
    sdb[...] = part
    sd = [
        far(sdb, sdr.at[k], sns.at[k], snr.at[k], {"dp": did[k]}) for k in range(nd - 1)
    ]
    for hp in range(half, nh):
        over_z(hp)
    for c in sd:
        c.wait_recv()
    for k in range(nd - 1):
        part = part + sdr[k]
    ssum[...] = part
    squares = sqb[0] + jnp.where(
        n == 0, jnp.sum((part * part).reshape(part.shape[0] // 8, 8, FS), 0), 0.0
    )
    for src in range(nh):

        @pl.when(h != src)
        def _(src=src):
            remote(zs.at[src], zr.at[src], zss.at[src], zsr.at[src], {"hid": src}).wait_recv()

    block = zr[0].astype(f32)
    for src in range(1, nh):
        block = block + zr[src].astype(f32)
    gsum[...] = block
    for f in range(nh):
        part = block[:, f * FS : (f + 1) * FS]
        squares = squares + jnp.sum((part * part).reshape(part.shape[0] // 8, 8, FS), 0)
    sqb[1] = squares
    qd = [
        far(sqb.at[1], sqd.at[k], qss.at[k], qsr.at[k], {"dp": did[k]}) for k in range(nd - 1)
    ]
    for c in qd:
        c.wait_recv()
    for k in range(nd - 1):
        squares = squares + sqd[k]
    sqb[2] = squares
    qz = [far(sqb.at[2], sqz.at[k], rss.at[k], rsr.at[k], zpeer[k]) for k in range(nh - 1)]
    for c in qz:
        c.wait_recv()
    for k in range(nh - 1):
        squares = squares + sqz[k]
    everything = jnp.sum(jnp.sum(squares, 1, keepdims=True), 0, keepdims=True)
    norm[0, 0] = jnp.sqrt(everything)[0, 0]
    for c in sent:
        c.wait_send()
    for hp in range(nh):

        @pl.when(h != hp)
        def _(hp=hp):
            to_owner(hp).wait_send()

    for c, j in gathers:

        @pl.when(jnp.logical_and(h < top, h >= j))
        def _(c=c, j=j):
            go_right(c, j).wait_send()

        @pl.when(jnp.logical_and(h > 0, h + j <= top))
        def _(c=c, j=j):
            go_left(c, j).wait_send()

    for c, stage in scatters:

        @pl.when(h == stage)
        def _(c=c, stage=stage):
            for d in range(1, nh - stage):
                sum_right(c, d, d - 1).wait_send()

        @pl.when(h == top - stage)
        def _(c=c, stage=stage):
            for d in range(1, nh - stage):
                sum_left(c, d, d - 1).wait_send()

    for c in ends:
        c.wait()


def reduce_kernel(
    nd, nh, experts, gw, sg, fg, sqe, gsum, ssum, norm,
    wc, ch, own, wr, zr, zs, szr, sdr, sqd, sqz, sdb, sqb,
    css, csr, dss, dsr, zss, zsr, ass, asr, bss, bsr, qss, qsr, rss, rsr
):
    n = lax.axis_index("dp")
    h = lax.axis_index("hid")
    core = lax.rem(n, 2)
    chip = lax.div(n, 2)
    chips = nd // 2
    zid = [lax.rem(h + k, nh) for k in range(1, nh)]
    zpeer = [{"hid": z} for z in zid]
    did = [lax.rem(n + k, nd) for k in range(1, nd)]
    dpeer = [{"dp": d} for d in did]
    greet(zpeer + dpeer)
    partner = {"dp": chip * 2 + 1 - core}
    first = remote(gw.at[:, :, 1 - core], wc, css.at[0], csr.at[0], partner)
    first.start()
    sz = [remote(sg.at[zid[k]], szr.at[k], ass.at[k], asr.at[k], zpeer[k]) for k in range(nh - 1)]
    for c in sz:
        c.start()
    for c in sz:
        c.wait_recv()
    small = sg[h]
    for k in range(nh - 1):
        small = small + szr[k]
    small = jnp.concatenate([small[0:8] + fg[...], small[8:]], 0)
    sdb[...] = small
    sd = [remote(sdb, sdr.at[k], bss.at[k], bsr.at[k], dpeer[k]) for k in range(nd - 1)]
    for c in sd:
        c.start()
    first.wait_recv()
    for hp in range(nh):
        ch[hp] = (gw[hp, :, core].astype(f32) + wc[hp].astype(f32)).astype(bf16)
    cid = [lax.rem(chip + k, chips) for k in range(1, chips)]
    second = [
        remote(ch.at[:, cid[k]], wr.at[k], dss.at[k], dsr.at[k], {"dp": cid[k] * 2 + core})
        for k in range(chips - 1)
    ]
    for c in second:
        c.start()
    for c in sd:
        c.wait_recv()
    for k in range(nd - 1):
        small = small + sdr[k]
    ssum[...] = small
    for c in second:
        c.wait_recv()
    total = ch[:, chip].astype(f32)
    for k in range(chips - 1):
        total = total + wr[k].astype(f32)
    zs[...] = total.astype(bf16)
    third = [
        remote(zs.at[zid[k]], zr.at[k], zss.at[k], zsr.at[k], zpeer[k]) for k in range(nh - 1)
    ]
    for c in third:
        c.start()
    for c in third:
        c.wait_recv()
    block = zs[h].astype(f32)
    for k in range(nh - 1):
        block = block + zr[k].astype(f32)
    gsum[...] = block
    squares = sqe[...]
    for f in range(nh):
        part = block[:, f * FS : (f + 1) * FS]
        squares = squares + jnp.sum((part * part).reshape(part.shape[0] // 8, 8, FS), 0)
    both = jnp.sum((small * small).reshape(small.shape[0] // 8, 8, FS), 0)
    squares = squares + jnp.where(n == 0, both, 0.0)
    sqb[0] = squares
    qd = [remote(sqb.at[0], sqd.at[k], qss.at[k], qsr.at[k], dpeer[k]) for k in range(nd - 1)]
    for c in qd:
        c.start()
    for c in qd:
        c.wait_recv()
    for k in range(nd - 1):
        squares = squares + sqd[k]
    sqb[1] = squares
    qz = [remote(sqb.at[1], sqz.at[k], rss.at[k], rsr.at[k], zpeer[k]) for k in range(nh - 1)]
    for c in qz:
        c.start()
    for c in qz:
        c.wait_recv()
    for k in range(nh - 1):
        squares = squares + sqz[k]
    everything = jnp.sum(jnp.sum(squares, 1, keepdims=True), 0, keepdims=True)
    norm[...] = jnp.broadcast_to(jnp.sqrt(everything), norm.shape)
    for c in [first] + sz + sd + second + third + qd + qz:
        c.wait_send()


def call(kernel, cid, outs, scratch, ins, out_specs=None, limit=60, pack=None):
    shapes = [jax.ShapeDtypeStruct(s, t) for s, t in outs]
    specs = out_specs or [VM] * len(outs)
    if pack is not None:
        shapes = shapes[: pack[0]] + [shapes[pack[0] :]]
        specs = specs[: pack[0]] + [specs[pack[0] :]]
    result = pl.pallas_call(
        kernel,
        out_shape=shapes,
        in_specs=[spec for spec, _ in ins],
        out_specs=specs,
        scratch_shapes=scratch,
        compiler_params=pltpu.CompilerParams(
            collective_id=cid, has_side_effects=True, vmem_limit_bytes=limit * 2**20
        ),
    )(*[value for _, value in ins])
    if pack is not None:
        result = list(result[: pack[0]]) + list(result[pack[0]])
    return result


def adam_update(weight, grad, first, second, rate, factor):
    clipped = grad * factor
    first_new = beta_first * first + (1.0 - beta_first) * clipped
    second_new = beta_second * second + (1.0 - beta_second) * clipped * clipped
    first_hat = first_new / (1.0 - beta_first**STEP)
    second_hat = second_new / (1.0 - beta_second**STEP)
    weight_new = weight - rate * (
        first_hat / (jnp.sqrt(second_hat) + adam_epsilon) + weight_decay * weight
    )
    return (first_new, second_new, weight_new)


def shards(
    tokens,
    seq_count,
    out_grad,
    norm_params,
    norm_first,
    norm_second,
    controller_weight,
    router_first,
    router_second,
    attn_in,
    attn_in_first,
    attn_in_second,
    attn_in_average,
    attn_out,
    attn_out_first,
    attn_out_second,
    attn_out_average,
    expert_in,
    expert_in_first,
    expert_in_second,
    expert_in_average,
    expert_out,
    expert_out_first,
    expert_out_second,
    expert_out_average,
):
    ema_keep = (1.0 + STEP) / (10.0 + STEP)
    nd = lax.axis_size("dp")
    nh = lax.axis_size("hid")
    chips = nd // 2
    slots, seq, _ = tokens.shape
    experts = controller_weight.shape[1]
    r = attn_in.shape[0]
    el = experts * GB
    groups = seq * slots // GROUP
    blocks = seq // BLK
    hidden = expert_in.shape[2]
    er = 8 + experts
    z3 = nh - 1

    etypes = [((nh, (b + 1) * BLK, 2 * BLK), bf16) for b in range(blocks)]
    slices = ((nh, seq, FS), bf16)
    wtype = ((nh, chips, 2, r, D), bf16)
    qtype = ((nh, seq, 3 * FS), bf16)
    ttype = ((nh, FS, seq), bf16)
    rtype = ((nh, seq, FS), f32)
    htype = ((seq, D), f32)
    stype = ((nh, er, seq), f32)
    ptype = ((nh, er, FS), f32)
    ytype = ((nd, 2, groups, FS), bf16)
    gtype = ((groups // GB, GB * GROUP, el), bf16)

    def vmem(*types):
        return [pltpu.VMEM(*t) for t in types]

    share = groups // blocks
    xtype = ((blocks, nh, nd, 2, share, FS), bf16)
    if nd * share == BLK and blocks == 4 and slots == nh and hidden == D:
        block_out, tgf, g_in, g_out, gsum, ssum, norm = call(
            functools.partial(block_kernel, nd, nh, experts),
            5,
            [
                slices,
                slices,
                ((D, hidden), f32),
                ((hidden, D), f32),
                ((r, D), f32),
                ((er, FS), f32),
                ((1, 1), f32),
            ],
            vmem(((r, D), bf16), ((er, FS), f32))
            + vmem(slices, wtype, ptype, ((seq, D), bf16), qtype, ttype, ttype, slices, rtype, htype)
            + [vmem(*etypes)]
            + vmem(
                slices,
                ((er, seq), f32),
                slices,
                stype,
                slices,
                gtype,
                ((blocks, experts, 2, share, FS), bf16),
                xtype,
                ((blocks, nd * share, hidden), bf16),
                ((blocks, nd * share, hidden), bf16),
                xtype,
                xtype,
                xtype,
                ((blocks, nd, 2, share, FS), bf16),
                ((D, hidden), bf16),
                ((hidden, D), bf16),
                ((nh, er, seq), bf16),
                slices,
                ((nh, er, seq), bf16),
                rtype,
                rtype,
                ((2, FS, D), f32),
                ((er, D), f32),
                ((8, FS), f32),
                ptype,
                htype,
                wtype,
                ((nh, chips, r, D), bf16),
                ((nh, chips, r, D), bf16),
                ((nh, chips - 1, r, D), bf16),
                ((nh, r, D), bf16),
                ((nh, r, D), bf16),
                ((z3, er, FS), f32),
                ((er, FS), f32),
                ((nd - 1, er, FS), f32),
                ((3, 8, FS), f32),
                ((nd - 1, 8, FS), f32),
                ((z3, 8, FS), f32),
            )
            + [DMA((blocks, z3))] * 2
            + [DMA((z3,))] * 2
            + [DMA((nh, chips - 1))] * 2
            + [DMA((nh,))] * 2
            + [DMA((z3,))] * 2
            + [DMA((blocks, z3))] * 4
            + [DMA((blocks, nd - 1))] * 2
            + [DMA((blocks, z3))] * 4
            + [DMA((blocks, nh))] * 4
            + [DMA((blocks, nd))] * 2
            + [DMA((blocks, z3))] * 6
            + [DMA((nh,))] * 2
            + [DMA((nh, chips - 1))] * 2
            + [DMA((nh,))] * 2
            + [DMA((z3,))] * 2
            + [DMA((nd - 1,))] * 4
            + [DMA((z3,))] * 2
            + [DMA((4,)), DMA((blocks, 2)), DMA((blocks, 2)), DMA((blocks,))]
            + [DMA((nh, 2)), DMA((blocks,))],
            [
                (SM, seq_count),
                (HB, tokens),
                (VM, attn_in.transpose(1, 0, 2)),
                (VM, attn_out),
                (VM, norm_params),
                (VM, controller_weight.T),
                (HB, out_grad),
                (HB, expert_in[0]),
                (HB, expert_out[0]),
            ],
            [HB, VM, HB, HB, VM, VM, SM],
        )
    else:
        wblk = jnp.concatenate([attn_in.reshape(r, 3 * FS), attn_out], 1).astype(bf16)
        pblk = jnp.concatenate([norm_params, jnp.zeros((4, FS), f32), controller_weight.T], 0)
        x, w, p, qkv, kt, heads, recip, h1, h1f, stf, *es = call(
            functools.partial(forward_kernel, nd, nh, experts),
            1,
            [slices, wtype, ptype, qtype, ttype, slices, rtype, htype, slices, stype] + etypes,
            vmem(slices, wtype, qtype, ttype, slices, rtype, htype)
            + vmem(((BLK, D), bf16), ttype)
            + [vmem(*etypes)]
            + vmem(slices, ((er, seq), f32), ((2, FS, D), f32))
            + [DMA((blocks, z3))] * 2
            + [DMA((z3,))] * 2
            + [DMA((nh, chips - 1))] * 2
            + [DMA((1,))] * 2
            + [DMA((z3,))] * 2
            + [DMA((blocks, z3))] * 4
            + [DMA((4,)), DMA((blocks, 6)), DMA((blocks, 2)), DMA((blocks,))],
            [(VM, tokens), (VM, wblk), (VM, pblk)],
            [HB, HB, VM, HB, HB, HB, HB, HB, VM, VM] + [HB] * blocks,
            pack=(10, blocks),
        )
        gates, yin, g_in, g_out, sqe = call(
            functools.partial(expert_kernel, nd, nh, experts),
            2,
            [gtype, ytype, ((D, hidden), f32), ((hidden, D), f32), ((8, FS), f32)],
            vmem(
                ytype,
                ((nh, nd, 2, groups, FS), bf16),
                ((nd, groups, hidden), bf16),
                ((nd, groups, hidden), bf16),
                ((nh, nh, 2, groups, FS), bf16),
                ((nd, nh, 2, groups, FS), bf16),
                ((nd, nh, 2, groups, FS), bf16),
                ytype,
                ((2, D, D), f32),
                ((D, hidden), bf16),
                ((hidden, D), bf16),
            )
            + [DMA((nd,))] * 2
            + [DMA((nd, z3))] * 4
            + [DMA((nd, nh))] * 4
            + [DMA((nd,))] * 2
            + [DMA((4,))],
            [
                (SM, seq_count),
                (VM, h1f),
                (VM, stf),
                (VM, out_grad),
                (VM, norm_params),
                (HB, expert_in[0]),
                (HB, expert_out[0]),
            ],
        )
        block_out, fg, tgf, gw, sg = call(
            functools.partial(backward_kernel, nh, experts),
            3,
            [slices, ((8, FS), f32), slices, wtype, ptype],
            vmem(slices, stype, slices, stype)
            + vmem(slices, wtype, qtype, ttype, slices, rtype, htype)
            + vmem(
                ((seq, D), bf16),
                rtype,
                rtype,
                qtype,
                ((seq, D), bf16),
                slices,
                ((2, FS, D), f32),
                ((er, D), f32),
            )
            + [vmem(*etypes)]
            + [DMA((blocks, z3))] * 6
            + [DMA((blocks,)), DMA((blocks, 2)), DMA((7,)), DMA((blocks,))],
            [(SM, seq_count)]
            + [(VM, v) for v in (h1f, stf, out_grad, norm_params, gates, yin, p)]
            + [(HB, v) for v in (x, w, qkv, kt, heads, recip, h1)]
            + [([HB] * blocks, list(es))],
        )
        gsum, ssum, norm = call(
            functools.partial(reduce_kernel, nd, nh, experts),
            4,
            [((r, D), f32), ((er, FS), f32), ((8, FS), f32)],
            [
                pltpu.VMEM((nh, chips, r, D), bf16),
                pltpu.VMEM((nh, chips, r, D), bf16),
                pltpu.VMEM((8, FS), f32),
                pltpu.VMEM((chips - 1, nh, r, D), bf16),
                pltpu.VMEM((z3, r, D), bf16),
                pltpu.VMEM((nh, r, D), bf16),
                pltpu.VMEM((z3, er, FS), f32),
                pltpu.VMEM((nd - 1, er, FS), f32),
                pltpu.VMEM((nd - 1, 8, FS), f32),
                pltpu.VMEM((z3, 8, FS), f32),
                pltpu.VMEM((er, FS), f32),
                pltpu.VMEM((2, 8, FS), f32),
            ]
            + [DMA((1,))] * 2
            + [DMA((chips - 1,))] * 2
            + [DMA((z3,))] * 4
            + [DMA((nd - 1,))] * 4
            + [DMA((z3,))] * 2,
            [(VM, gw), (VM, sg), (VM, fg), (VM, sqe)],
        )
    grad_norm = norm[0:1, 0:1].reshape(())
    tokens_grad = tgf.astype(f32)
    attn_in_sum = gsum[:, : 3 * FS].reshape(attn_in.shape)
    attn_out_sum = gsum[:, 3 * FS :]
    norm_sum = ssum[0:4]
    router_sum = ssum[8:].T
    expert_in_sum = g_in[None]
    expert_out_sum = g_out[None]
    factor = jnp.minimum(1.0, clip_limit / grad_norm)
    norm_up = adam_update(norm_params, norm_sum, norm_first, norm_second, 0.6, factor)
    router_up = adam_update(
        controller_weight, router_sum, router_first, router_second, (4 * D) ** (-0.5), factor
    )
    attn_in_up = adam_update(
        attn_in, attn_in_sum, attn_in_first, attn_in_second, 0.5 * D ** (-0.5), factor
    )
    attn_out_up = adam_update(
        attn_out,
        attn_out_sum,
        attn_out_first,
        attn_out_second,
        0.5 * (HEADS * HS // 16) ** (-0.5),
        factor,
    )
    expert_in_up = adam_update(
        expert_in,
        expert_in_sum,
        expert_in_first,
        expert_in_second,
        2.5 * (D // GROUP) ** (-0.5),
        factor,
    )
    expert_out_up = adam_update(
        expert_out, expert_out_sum, expert_out_first, expert_out_second, 0.5 * H ** (-0.5), factor
    )
    return (
        block_out,
        tokens_grad,
        grad_norm,
        norm_up[0],
        norm_up[1],
        norm_up[2],
        router_up[0],
        router_up[1],
        router_up[2],
        attn_in_up[0],
        attn_in_up[1],
        attn_in_up[2],
        ema_keep * attn_in_average + (1.0 - ema_keep) * attn_in_up[2],
        attn_out_up[0],
        attn_out_up[1],
        attn_out_up[2],
        ema_keep * attn_out_average + (1.0 - ema_keep) * attn_out_up[2],
        expert_in_up[0],
        expert_in_up[1],
        expert_in_up[2],
        ema_keep * expert_in_average + (1.0 - ema_keep) * expert_in_up[2],
        expert_out_up[0],
        expert_out_up[1],
        expert_out_up[2],
        ema_keep * expert_out_average + (1.0 - ema_keep) * expert_out_up[2],
    )


def solution(mesh):
    return jax.shard_map(
        shards,
        mesh=mesh,
        in_specs=(
            P("dp", None, "hid"),
            P("dp"),
            P("dp", None, "hid"),
            P(None, "hid"),
            P(None, "hid"),
            P(None, "hid"),
            P("hid", None),
            P("hid", None),
            P("hid", None),
            P("dp", None, "hid"),
            P("dp", None, "hid"),
            P("dp", None, "hid"),
            P("dp", None, "hid"),
            P("dp", "hid"),
            P("dp", "hid"),
            P("dp", "hid"),
            P("dp", "hid"),
            P("dp", None, "hid"),
            P("dp", None, "hid"),
            P("dp", None, "hid"),
            P("dp", None, "hid"),
            P("dp", "hid", None),
            P("dp", "hid", None),
            P("dp", "hid", None),
            P("dp", "hid", None),
        ),
        out_specs=(
            P("dp", None, "hid"),
            P("dp", None, "hid"),
            P(),
            P(None, "hid"),
            P(None, "hid"),
            P(None, "hid"),
            P("hid", None),
            P("hid", None),
            P("hid", None),
            P("dp", None, "hid"),
            P("dp", None, "hid"),
            P("dp", None, "hid"),
            P("dp", None, "hid"),
            P("dp", "hid"),
            P("dp", "hid"),
            P("dp", "hid"),
            P("dp", "hid"),
            P("dp", None, "hid"),
            P("dp", None, "hid"),
            P("dp", None, "hid"),
            P("dp", None, "hid"),
            P("dp", "hid", None),
            P("dp", "hid", None),
            P("dp", "hid", None),
            P("dp", "hid", None),
        ),
        check_vma=False,
    )
```

```python
import functools

import jax
import jax.numpy as jnp
from jax import lax
from jax.experimental import pallas as pl
from jax.experimental.pallas import tpu as pltpu
from jax.sharding import PartitionSpec as P

D = 512
HEADS = 8
HS = 64
H = 2048
GROUP = 32
STEP = 10
BLK = 256
FS = 128
GB = 16

norm_epsilon = 1e-05
fill_value = -1e30
clip_limit = 1.0
beta_first = 0.9
beta_second = 0.95
adam_epsilon = 1e-08
weight_decay = 0.1

f32 = jnp.float32
bf16 = jnp.bfloat16
MESH = pl.DeviceIdType.MESH
EXACT = lax.Precision.HIGHEST
VM = pl.BlockSpec(memory_space=pltpu.VMEM)
HB = pl.BlockSpec(memory_space=pl.ANY)
SM = pl.BlockSpec(memory_space=pltpu.SMEM)
DMA = pltpu.SemaphoreType.DMA


def dot(a, b, precision=None):
    return lax.dot_general(
        a, b, (((1,), (0,)), ((), ())), precision=precision, preferred_element_type=f32
    )


def dot_last(a, b, precision=None):
    return lax.dot_general(
        a, b, (((1,), (1,)), ((), ())), precision=precision, preferred_element_type=f32
    )


def dot_first(a, b, precision=None):
    return lax.dot_general(
        a, b, (((0,), (0,)), ((), ())), precision=precision, preferred_element_type=f32
    )


def greet(peers):
    barrier = pltpu.get_barrier_semaphore()
    for peer in peers:
        pl.semaphore_signal(barrier, inc=1, device_id=peer, device_id_type=MESH)
    pl.semaphore_wait(barrier, len(peers))


def remote(src, dst, send, recv, peer):
    return pltpu.make_async_remote_copy(
        src_ref=src, dst_ref=dst, send_sem=send, recv_sem=recv, device_id=peer, device_id_type=MESH
    )


def lanes(ref_like, index):
    return pl.ds(pl.multiple_of(index * ref_like, ref_like), ref_like)


def features(ref, rows):
    return jnp.concatenate([ref[f, rows, :] for f in range(ref.shape[0])], axis=1)


def row_of(ref, row):
    return jnp.concatenate([ref[f, row : row + 1, :] for f in range(ref.shape[0])], axis=1)


def split(v):
    high = v.astype(bf16)
    return high, (v - high.astype(f32)).astype(bf16)


def split3(v):
    high, _ = split(v)
    rest = v - high.astype(f32)
    mid, low = split(rest)
    return high, mid, low


def iota(shape, dim):
    return lax.broadcasted_iota(jnp.int32, shape, dim)


def standardize(v):
    center = jnp.sum(v, -1, keepdims=True) / v.shape[-1]
    dev = v - center
    inv = lax.rsqrt(jnp.sum(dev * dev, -1, keepdims=True) / v.shape[-1] + norm_epsilon)
    return dev * inv, center, inv


def controller_rows(p, pad, experts):
    pad[...] = jnp.zeros_like(pad)
    for f in range(p.shape[0]):
        high, low = split(p[f, 8 : 8 + experts, :])
        pad[0, 0:experts, f * FS : (f + 1) * FS] = high.astype(f32)
        pad[1, 0:experts, f * FS : (f + 1) * FS] = low.astype(f32)


def both_heads(v):
    low = iota(v.shape, 1) < HS
    zero = jnp.zeros_like(v)
    return jnp.concatenate([jnp.where(low, v, zero), jnp.where(low, zero, v)], 0)


def forward_kernel(
    nd, nh, experts, tok, wblk, pblk,
    xo, wout, p, qkvo, kto, headso, recipo, h1o, h1f, stf, eouts,
    x, w, qkv, kt, heads, recip, h1, a1, vt, es, h1b, st, pad,
    tss, tsr, wss, wsr, dss, dsr, css, csr, pss, psr, hss, hsr, sss, ssr, loc, esem, mine_sem, save
):
    n = lax.axis_index("dp")
    h = lax.axis_index("hid")
    core = lax.rem(n, 2)
    chip = lax.div(n, 2)
    chips = nd // 2
    seq = tok.shape[1]
    blocks = seq // BLK
    zpeer = [{"hid": lax.rem(h + k, nh)} for k in range(1, nh)]
    cpeer = [{"dp": lax.rem(chip + k, chips) * 2 + core} for k in range(1, chips)]
    partner = {"dp": chip * 2 + 1 - core}
    greet(zpeer + cpeer + [partner])
    locals_ = [
        pltpu.make_async_copy(wblk, w.at[h, chip, core], loc.at[0]),
        pltpu.make_async_copy(pblk, p.at[h], loc.at[1]),
        pltpu.make_async_copy(tok.at[h], x.at[h], loc.at[2]),
    ]
    for c in locals_:
        c.start()
    wz = [
        remote(wblk, w.at[h, chip, core], wss.at[k], wsr.at[k], zpeer[k]) for k in range(nh - 1)
    ]
    pz = [remote(pblk, p.at[h], pss.at[k], psr.at[k], zpeer[k]) for k in range(nh - 1)]
    for c in wz + pz:
        c.start()
    tz = []
    for b in range(blocks):
        rows = pl.ds(b * BLK, BLK)
        for k in range(nh - 1):
            c = remote(
                tok.at[lax.rem(h + k + 1, nh), rows],
                x.at[h, rows],
                tss.at[b, k],
                tsr.at[b, k],
                zpeer[k],
            )
            c.start()
            tz.append(c)
    locals_[0].wait()
    wc = []
    for j in range(nh):
        piece = lax.rem(h - j + nh, nh)
        if j > 0:
            wz[j - 1].wait_recv()
        for k in range(chips - 1):
            c = remote(
                w.at[piece, chip, core], w.at[piece, chip, core],
                dss.at[j, k], dsr.at[j, k], cpeer[k]
            )
            c.start()
            wc.append(c)
    for c in pz + wc:
        c.wait_recv()
    wp = remote(w.at[:, :, core], w.at[:, :, core], css.at[0], csr.at[0], partner)
    wp.start()
    for c in locals_[1:]:
        c.wait()
    controller_rows(p, pad, experts)
    gain1 = row_of(p, 0)
    bias1 = row_of(p, 1)
    gain2 = row_of(p, 2)
    bias2 = row_of(p, 3)
    scale = jnp.where(iota((BLK, 3 * FS), 1) < FS, HS**-0.5, 1.0).astype(bf16)
    lane = iota((BLK, FS), 1)
    low_half = lane < HS
    causal = iota((BLK, 2 * BLK), 0) <= (iota((BLK, 2 * BLK), 1) & (BLK - 1))
    one = jnp.ones((FS, BLK), bf16)
    low_rows = iota((FS, BLK), 0) < HS
    sends = []
    for b in range(blocks):
        rows = pl.ds(b * BLK, BLK)
        past = b * BLK
        e_ref = es[b]
        for k in range(nh - 1):
            tz[b * (nh - 1) + k].wait_recv()
        normed, _, _ = standardize(features(x, rows).astype(f32))
        a1[...] = (normed * gain1 + bias1).astype(bf16)
        if b == 0:
            wp.wait_recv()
            c = pltpu.make_async_copy(w, wout, loc.at[3])
            c.start()
            sends.append(c)

        def pair(hp, carry):
            proj = dot(a1[...], w[hp].reshape(D, D)[:, : 3 * FS])
            low = proj.astype(bf16) * scale
            qkv[hp, rows, :] = low
            kt[hp, :, rows] = proj[:, FS : 2 * FS].T.astype(bf16)
            vt[hp, :, rows] = proj[:, 2 * FS :].T.astype(bf16)
            q = both_heads(low[:, :FS])
            s_now = dot_last(low[:, FS : 2 * FS], q)
            s_now = jnp.where(causal, s_now, fill_value)
            peak = jnp.max(s_now, 0, keepdims=True)
            if b > 0:
                s_past = dot_last(qkv[hp, 0:past, FS : 2 * FS], q)
                peak = jnp.maximum(peak, jnp.max(s_past, 0, keepdims=True))
                e_ref[hp, 0:past, :] = jnp.exp(s_past - peak).astype(bf16)
            e_ref[hp, past : past + BLK, :] = jnp.exp(s_now - peak).astype(bf16)
            outs = []
            for half in range(2):
                total = jnp.zeros((FS, BLK), f32)
                for j in range(b + 1):
                    keys = slice(j * BLK, (j + 1) * BLK)
                    v = vt[hp, :, keys]
                    v = jnp.where(low_rows, v, one) if half == 0 else jnp.where(low_rows, one, v)
                    total = total + dot(v, e_ref[hp, keys, half * BLK : (half + 1) * BLK])
                outs.append(total.T)
            value = jnp.where(low_half, outs[0], outs[1])
            total = jnp.where(low_half, pltpu.roll(outs[0], HS, 1), pltpu.roll(outs[1], HS, 1))
            inv = 1.0 / total
            recip[hp, rows, :] = inv
            heads[hp, rows, :] = (value * inv).astype(bf16)
            return carry

        lax.fori_loop(0, nh, pair, 0)
        saves = [
            (e_ref, eouts[b]),
            (x.at[:, rows], xo.at[:, rows]),
            (qkv.at[:, rows], qkvo.at[:, rows]),
            (kt.at[:, :, rows], kto.at[:, :, rows]),
            (heads.at[:, rows], headso.at[:, rows]),
            (recip.at[:, rows], recipo.at[:, rows]),
        ]
        for k, (src, dst) in enumerate(saves):
            c = pltpu.make_async_copy(src, dst, esem.at[b, k])
            c.start()
            sends.append(c)
        attn = jnp.zeros((BLK, D), f32)
        for hp in range(nh):
            attn = attn + dot_last(heads[hp, rows, :], w[hp].reshape(D, D)[:, 3 * FS :])
        hidden = features(x, rows).astype(f32) + attn
        h1[rows, :] = hidden
        c = pltpu.make_async_copy(h1.at[rows], h1o.at[rows], save.at[b])
        c.start()
        sends.append(c)
        normed, center, inv = standardize(hidden)
        u = normed * gain2 + bias2
        uh, ul = split(u)
        cols = dot_last(
            jnp.concatenate([uh, ul, uh], 1),
            jnp.concatenate([pad[0], pad[0], pad[1]], 1).astype(bf16),
        )
        cols = jnp.where(lane == experts, center, jnp.where(lane == experts + 1, inv, cols))
        st[:, rows] = cols.T[0 : experts + 8, :]
        for f in range(nh):
            h1b[f, rows, :] = hidden[:, f * FS : (f + 1) * FS].astype(bf16)
        mine = [
            pltpu.make_async_copy(h1b.at[h, rows], h1f.at[h, rows], mine_sem.at[b, 0]),
            pltpu.make_async_copy(st.at[:, rows], stf.at[h, :, rows], mine_sem.at[b, 1]),
        ]
        for c in mine:
            c.start()
        for k in range(nh - 1):
            c = remote(
                h1b.at[lax.rem(h + k + 1, nh), rows],
                h1f.at[h, rows],
                hss.at[b, k],
                hsr.at[b, k],
                zpeer[k],
            )
            s = remote(
                st.at[:, rows], stf.at[h, :, rows], sss.at[b, k], ssr.at[b, k], zpeer[k]
            )
            c.start()
            s.start()
            sends += [c, s]
        sends += mine
    for c in sends:
        c.wait()
    for c in wz + pz + tz + wc + [wp]:
        c.wait_send()


def expand(stb, experts, el, gates):
    height = stb.shape[1]
    width = (el if gates else 0) + 2 * FS
    rows = iota((3 * height, width), 0)
    cols = iota((3 * height, width), 1)
    rows = jnp.where(rows >= 2 * height, rows - 2 * height, rows)
    rows = jnp.where(rows >= height, rows - height, rows)
    base = el if gates else 0
    target = jnp.where(cols < base + FS, experts, experts + 1)
    if gates:
        target = jnp.where(cols < el, lax.shift_right_logical(cols, 4), target)
    pick = jnp.where(rows == target, 1.0, 0.0).astype(bf16)
    return [
        dot_first(jnp.concatenate(split3(stb[s]), 0), pick) for s in range(stb.shape[0])
    ]


def own_group(tokens, el):
    group = lax.shift_right_logical(iota((tokens, el), 0), 3) & (GB - 1)
    return (iota((tokens, el), 1) & (GB - 1)) == group


def block_values(h1f, og, gain, bias, live, rows, mean, inv):
    slots = h1f.shape[0]
    nhat, u, dy, hid = [], [], [], []
    for s in range(slots):
        hidden = h1f[s, rows, :].astype(f32)
        hat = (hidden - mean[s]) * inv[s]
        nhat.append(hat)
        u.append((hat * gain + bias).astype(bf16))
        hid.append(hidden)
        grad = og[s, rows, :]
        dy.append(jnp.where(s < live, grad, jnp.zeros_like(grad)))
    return nhat, u, dy, hid


def expert_kernel(
    nd, nh, experts, count, h1f, stf, og, npar, win, wout, gates, yin, g_in, g_out, sq,
    mout, xz, act, dpre, ps, inl, inr, yo, wf, wi, wo,
    dss, dsr, xsr, xsl, xrl, xrr, isr, isl, irl, irr, yss, ysr, loc
):
    n = lax.axis_index("dp")
    h = lax.axis_index("hid")
    seq = h1f.shape[1]
    slots = h1f.shape[0]
    el = experts * GB
    span = GB * GROUP // slots
    top = nh - 1
    right = {"hid": jnp.minimum(h + 1, top)}
    left = {"hid": jnp.maximum(h - 1, 0)}
    weights = [
        pltpu.make_async_copy(win, wf.at[0], loc.at[0]),
        pltpu.make_async_copy(wout, wf.at[1], loc.at[1]),
    ]
    for c in weights:
        c.start()
    greet([{"hid": lax.rem(h + k, nh)} for k in range(1, nh)] + [
        {"dp": lax.rem(n + k, nd)} for k in range(1, nd)
    ])
    live = count[0]
    gain = npar[2:3, :]
    bias = npar[3:4, :]
    mask = own_group(slots * span, el)

    def gate_block(b, carry):
        rows = pl.ds(pl.multiple_of(b * span, span), span)
        grows = pl.ds(pl.multiple_of(b * GB, GB), GB)
        spread = expand(stf[:, :, rows], experts, el, True)
        logits = jnp.stack(
            [jnp.where(s < live, spread[s][:, :el], fill_value) for s in range(slots)]
        ).reshape(slots, GB, span // GB, el)
        peak = jnp.max(logits, axis=(0, 2), keepdims=True)
        e = jnp.exp(logits - peak)
        gate = e / jnp.sum(e, axis=(0, 2), keepdims=True)
        gate = jnp.where(mask, gate.reshape(slots * span, el), 0.0).astype(bf16)
        gates[b] = gate
        mean = [v[:, el : el + FS] for v in spread]
        inv = [v[:, el + FS :] for v in spread]
        _, u, dy, _ = block_values(h1f, og, gain, bias, live, rows, mean, inv)
        both = jnp.concatenate([jnp.concatenate(u, 0), jnp.concatenate(dy, 0)], 1)
        mixed = dot_first(gate, both).astype(bf16)
        mout[:, 0, grows, :] = mixed[:, :FS].reshape(experts, GB, FS)
        mout[:, 1, grows, :] = mixed[:, FS:].reshape(experts, GB, FS)
        return carry

    lax.fori_loop(0, seq // span, gate_block, 0)

    def source(k):
        return lax.rem(n - k + nd, nd)

    def to_expert(k):
        e = lax.rem(n + k, nd)
        return remote(mout.at[e], xz.at[h, n], dss.at[k], dsr.at[k], {"dp": e})

    def go_right(k, j):
        piece = xz.at[jnp.maximum(h - j, 0), source(k)]
        return remote(piece, piece, xsr.at[k, j], xrl.at[k, j], right)

    def go_left(k, j):
        piece = xz.at[jnp.minimum(h + j, top), source(k)]
        return remote(piece, piece, xsl.at[k, j], xrr.at[k, j], left)

    def sum_right(k, d):
        piece = inl.at[k, jnp.minimum(h + d, top)]
        return remote(piece, piece, isr.at[k, d], irl.at[k, d - 1], right)

    def sum_left(k, d):
        piece = inr.at[k, jnp.maximum(h - d, 0)]
        return remote(piece, piece, isl.at[k, d], irr.at[k, d - 1], left)

    def from_left(k, d):
        piece = inl.at[k, jnp.minimum(h + d, top)]
        return remote(piece, piece, isr.at[k, d], irl.at[k, d], right)

    def from_right(k, d):
        piece = inr.at[k, jnp.maximum(h - d, 0)]
        return remote(piece, piece, isl.at[k, d], irr.at[k, d], left)

    def to_home(k):
        src = source(k)
        return remote(yo.at[k], yin.at[n], yss.at[k], ysr.at[k], {"dp": src})

    own = pltpu.make_async_copy(mout.at[n], xz.at[h, n], loc.at[2])
    own.start()

    def start_expert(k, carry):
        to_expert(k).start()
        return carry

    lax.fori_loop(1, nd, start_expert, 0)
    for c in weights:
        c.wait()
    wi[...] = wf[0].astype(bf16)
    wo[...] = wf[1].astype(bf16)
    own.wait()

    def expert(k):
        src = source(k)
        slot = lax.rem(k, nh)
        mixed = jnp.concatenate([xz[f, src, 0] for f in range(nh)], axis=1)
        drows = jnp.concatenate([xz[f, src, 1] for f in range(nh)], axis=1)
        pre = dot(mixed, wi[...])
        cube = 0.7978845608028654
        t = jnp.tanh(cube * (pre + 0.044715 * (pre * pre * pre)))
        a = (0.5 * pre * (1.0 + t)).astype(bf16)
        slope = 0.5 * (1.0 + t) + 0.5 * pre * (1.0 - t * t) * (
            cube * (1.0 + 3.0 * 0.044715 * (pre * pre))
        )
        rows = dot(a, wo[...])
        d = (dot_last(drows, wo[...]) * slope).astype(bf16)
        dmix = dot_last(d, wi[...])
        act[src] = a
        dpre[src] = d
        for f in range(nh):
            ps[slot, f, 0] = rows[:, f * FS : (f + 1) * FS].astype(bf16)
            ps[slot, f, 1] = dmix[:, f * FS : (f + 1) * FS].astype(bf16)

    def step(t, carry):
        @pl.when(t < nd)
        def _():
            @pl.when(t > 0)
            def _():
                to_expert(t).wait_recv()

            @pl.when(h < top)
            def _():
                go_right(t, 0).start()

            @pl.when(h > 0)
            def _():
                go_left(t, 0).start()

        for j in range(1, nh):
            k = t - j
            here = jnp.logical_and(k >= 0, k < nd)

            @pl.when(jnp.logical_and(here, h >= j))
            def _(k=k, j=j):
                go_right(k, j - 1).wait_recv()
                if j < top:

                    @pl.when(h < top)
                    def _():
                        go_right(k, j).start()

            @pl.when(jnp.logical_and(here, h + j <= top))
            def _(k=k, j=j):
                go_left(k, j - 1).wait_recv()
                if j < top:

                    @pl.when(h > 0)
                    def _():
                        go_left(k, j).start()

        ke = t - top

        @pl.when(jnp.logical_and(ke >= 0, ke < nd))
        def _():
            expert(ke)

        kr = t - top - h

        @pl.when(jnp.logical_and(kr >= 0, kr < nd))
        def _():
            slot = lax.rem(kr, nh)
            for d in range(nh):

                @pl.when(h + d <= top)
                def _(d=d):
                    dest = jnp.minimum(h + d, top)

                    @pl.when(h > 0)
                    def _():
                        from_left(kr, d).wait_recv()
                        if d > 0:
                            value = inl[kr, dest].astype(f32) + ps[slot, dest].astype(f32)
                            inl[kr, dest] = value.astype(bf16)

                    if d > 0:

                        @pl.when(h == 0)
                        def _():
                            inl[kr, dest] = ps[slot, dest]

                        sum_right(kr, d).start()

        kl = t - top - (top - h)

        @pl.when(jnp.logical_and(kl >= 0, kl < nd))
        def _():
            slot = lax.rem(kl, nh)
            for d in range(nh):

                @pl.when(h - d >= 0)
                def _(d=d):
                    dest = jnp.maximum(h - d, 0)

                    @pl.when(h < top)
                    def _():
                        from_right(kl, d).wait_recv()
                        if d > 0:
                            value = inr[kl, dest].astype(f32) + ps[slot, dest].astype(f32)
                            inr[kl, dest] = value.astype(bf16)

                    if d > 0:

                        @pl.when(h == top)
                        def _():
                            inr[kl, dest] = ps[slot, dest]

                        sum_left(kl, d).start()

        kf = t - 2 * top

        @pl.when(kf >= 0)
        def _():
            slot = lax.rem(kf, nh)

            @pl.when(h == 0)
            def _():
                yo[kf] = (ps[slot, h].astype(f32) + inr[kf, h].astype(f32)).astype(bf16)

            @pl.when(h == top)
            def _():
                yo[kf] = (ps[slot, h].astype(f32) + inl[kf, h].astype(f32)).astype(bf16)

            @pl.when(jnp.logical_and(h > 0, h < top))
            def _():
                value = ps[slot, h].astype(f32) + inl[kf, h].astype(f32)
                yo[kf] = (value + inr[kf, h].astype(f32)).astype(bf16)

            @pl.when(kf > 0)
            def _():
                to_home(kf).start()

        return carry

    lax.fori_loop(0, nd + 2 * top, step, 0)
    mine = pltpu.make_async_copy(yo.at[0], yin.at[n], loc.at[3])
    mine.start()
    total = nd * act.shape[1]
    squares = jnp.zeros((8, FS), f32)
    a_all = act[...].reshape(total, act.shape[2])
    d_all = dpre[...].reshape(total, dpre.shape[2])
    for f in range(nh):
        cols = pl.ds(f * FS, FS)
        gi = dot_first(xz[f, :, 0].reshape(total, FS), d_all)
        go = dot_first(a_all, xz[f, :, 1].reshape(total, FS))
        g_in[cols, :] = gi
        g_out[:, cols] = go
        for m in range(nh):
            part = gi[:, m * FS : (m + 1) * FS]
            squares = squares + jnp.sum((part * part).reshape(FS // 8, 8, FS), 0)
        squares = squares + jnp.sum((go * go).reshape(D // 8, 8, FS), 0)
    sq[...] = squares

    def finish(k, carry):
        @pl.when(k > 0)
        def _():
            to_expert(k).wait_send()
            to_home(k).wait()

        for j in range(top):

            @pl.when(jnp.logical_and(h < top, h >= j))
            def _(j=j):
                go_right(k, j).wait_send()

            @pl.when(jnp.logical_and(h > 0, h + j <= top))
            def _(j=j):
                go_left(k, j).wait_send()

        for d in range(1, nh):

            @pl.when(h + d <= top)
            def _(d=d):
                sum_right(k, d).wait_send()

            @pl.when(h - d >= 0)
            def _(d=d):
                sum_left(k, d).wait_send()

        return carry

    lax.fori_loop(0, nd, finish, 0)
    mine.wait()


def backward_kernel(
    nh, experts, count, h1f, stf, og, npar, gates, yin, p, xi, win, qkvi, kti, headsi, recipi, h1i,
    ein, block_out, fg, tgf, gw, sg,
    p1, py, p1s, pay, x, w, qkv, kt, heads, recip, h1, a1, dk, dv, dqkv, dattn, tgb, pad, small,
    es, pss, psr, sss, ssr, hss, hsr, loc, mloc, lsem, esem
):
    h = lax.axis_index("hid")
    seq = h1f.shape[1]
    slots = h1f.shape[0]
    blocks = seq // BLK
    el = experts * GB
    span = GB * GROUP // slots
    per = BLK // span
    zpeer = [{"hid": lax.rem(h + k, nh)} for k in range(1, nh)]
    held = [(xi, x), (win, w), (h1i, h1), (qkvi, qkv), (kti, kt), (headsi, heads), (recipi, recip)]
    held = [pltpu.make_async_copy(src, dst, lsem.at[i]) for i, (src, dst) in enumerate(held)]
    for c in held:
        c.start()
    loads = [pltpu.make_async_copy(ein[b], es[b], esem.at[b]) for b in range(blocks)]
    for c in reversed(loads):
        c.start()
    greet(zpeer)
    live = count[0]
    gain = npar[2:3, :]
    bias = npar[3:4, :]
    height = experts + 8
    srow = iota((height, el + 2 * FS), 0)
    scol = iota((height, el + 2 * FS), 1)
    target = jnp.where(scol < el, lax.shift_right_logical(scol, 4), experts)
    target = jnp.where(scol >= el + FS, experts + 1, target)
    fold = jnp.where(srow == target, 1.0, 0.0).astype(bf16)
    fold = jnp.concatenate([fold, fold], 1)
    fg[...] = jnp.zeros_like(fg)

    def back_block(b, carry):
        rows = pl.ds(pl.multiple_of(b * span, span), span)
        grows = pl.ds(pl.multiple_of(b * GB, GB), GB)
        spread = expand(stf[:, :, rows], experts, el, False)
        mean = [v[:, :FS] for v in spread]
        inv = [v[:, FS:] for v in spread]
        nhat, u, dy, hid = block_values(h1f, og, gain, bias, live, rows, mean, inv)
        y = jnp.concatenate(
            [yin[:, 0, grows, :].reshape(el, FS), yin[:, 1, grows, :].reshape(el, FS)], 1
        )
        gate = gates[b]
        bd = dot(gate, y)
        dgates = dot_last(
            jnp.concatenate([jnp.concatenate(dy, 0), jnp.concatenate(u, 0)], 1), y
        )
        gate = gate.astype(f32)
        gd = gate * dgates
        gd4 = gd.reshape(slots, GB, span // GB, el)
        inner = jnp.sum(gd4, axis=(0, 2), keepdims=True)
        dlog = gd4 - gate.reshape(slots, GB, span // GB, el) * inner
        dlog = dlog.reshape(slots * span, el)
        qs, qn = [], []
        acc_gain = jnp.zeros((1, FS), f32)
        acc_bias = jnp.zeros((1, FS), f32)
        for s in range(slots):
            part = slice(s * span, (s + 1) * span)
            back = bd[part, :FS]
            du = bd[part, FS:]
            block_out[s, rows, :] = jnp.where(s < live, hid[s] + back, 0.0).astype(bf16)
            q = du * gain
            p1[s, rows, :] = (dy[s].astype(f32) + inv[s] * q).astype(bf16)
            acc_gain = acc_gain + jnp.sum(du * nhat[s], 0, keepdims=True)
            acc_bias = acc_bias + jnp.sum(du, 0, keepdims=True)
            qs.append(q)
            qn.append(q * nhat[s])
        high, low = split(
            jnp.concatenate([dlog, jnp.concatenate(qs, 0), jnp.concatenate(qn, 0)], 1)
        )
        folded = dot_last(fold, jnp.concatenate([high, low], 1))
        for s in range(slots):
            py[s, :, rows] = folded[:, s * span : (s + 1) * span]
        fg[2:3, :] += acc_gain
        fg[3:4, :] += acc_bias
        return carry

    arrive = [None] * blocks
    sends = []
    for c in reversed(range(blocks)):
        lax.fori_loop(c * per, (c + 1) * per, back_block, 0)
        rows = pl.ds(c * BLK, BLK)
        mine = [
            pltpu.make_async_copy(p1.at[h, rows], p1s.at[h, rows], mloc.at[c, 0]),
            pltpu.make_async_copy(py.at[h, :, rows], pay.at[h, :, rows], mloc.at[c, 1]),
        ]
        for m in mine:
            m.start()
        far = []
        for k in range(nh - 1):
            peer = lax.rem(h + k + 1, nh)
            a = remote(p1.at[peer, rows], p1s.at[h, rows], pss.at[c, k], psr.at[c, k], zpeer[k])
            s = remote(
                py.at[peer, :, rows], pay.at[h, :, rows], sss.at[c, k], ssr.at[c, k], zpeer[k]
            )
            a.start()
            s.start()
            far += [a, s]
        arrive[c] = (mine, far)
    controller_rows(p, pad, experts)
    gain1 = row_of(p, 0)
    bias1 = row_of(p, 1)
    gain2 = row_of(p, 2)
    bias2 = row_of(p, 3)
    lane = iota((BLK, FS), 1)
    low_half = lane < HS
    er = iota((3 * height, FS), 0)
    er = jnp.where(er >= 2 * height, er - 2 * height, er)
    er = jnp.where(er >= height, er - height, er)
    eye = jnp.where(er == iota((3 * height, FS), 1), 1.0, 0.0).astype(bf16)
    pick = iota((8, 2 * FS), 1) & (FS - 1)
    row = iota((8, 2 * FS), 0)
    pick = ((row == 0) & (pick < HS)) | ((row == 1) & (pick >= HS))
    pick = jnp.where(pick, 1.0, 0.0).astype(bf16)
    small[...] = jnp.zeros_like(small)
    for c in held:
        c.wait()
    for b in reversed(range(blocks)):
        rows = pl.ds(b * BLK, BLK)
        last = b == blocks - 1
        e_ref = es[b]
        mine, far = arrive[b]
        for c in mine:
            c.wait()
        for c in far:
            c.wait_recv()
        total = pay[0, :, rows]
        for f in range(1, nh):
            total = total + pay[f, :, rows]
        cols = dot_first(jnp.concatenate(split3(total), 0), eye)
        s1 = cols[:, experts : experts + 1]
        s2 = cols[:, experts + 1 : experts + 2]
        hidden = h1[rows, :]
        nhat, _, inv = standardize(hidden)
        ch, cl = split(jnp.where(lane < experts, cols, 0.0))
        du = dot(
            jnp.concatenate([ch, cl, ch], 1),
            jnp.concatenate([pad[0], pad[0], pad[1]], 0).astype(bf16),
        )
        q = du * gain2
        mq = (s1 + jnp.sum(q, -1, keepdims=True)) / D
        mqn = (s2 + jnp.sum(q * nhat, -1, keepdims=True)) / D
        dh1 = features(p1s, rows).astype(f32) + inv * (q - mq - nhat * mqn)
        small[2:3, :] += jnp.sum(du * nhat, 0, keepdims=True)
        small[3:4, :] += jnp.sum(du, 0, keepdims=True)
        routed = dot_first(
            jnp.concatenate([ch, cl], 1), (nhat * gain2 + bias2).astype(bf16)
        )
        small[8 : 8 + experts, :] += routed[0:experts] + routed[FS : FS + experts]
        dattn[rows, :] = dh1.astype(bf16)
        loads[b].wait()

        def pair(hp, carry):
            dh = dot(dattn[rows, :], w[hp].reshape(D, D)[:, 3 * FS :]).astype(bf16).astype(f32)
            dh = dh * recip[hp, rows, :]
            high, rest = split(dh * heads[hp, rows, :].astype(f32))
            inner = dot_last(pick, jnp.concatenate([high, rest], 1))
            inner = jnp.concatenate([inner[0:1], inner[1:2]], 1)
            dhs = both_heads(dh.astype(bf16))
            qs = both_heads(qkv[hp, rows, 0:FS])
            dqt = jnp.zeros((FS, 2 * BLK), f32)
            for j in range(b + 1):
                keys = slice(j * BLK, (j + 1) * BLK)
                e = e_ref[hp, keys, :]
                dp = dot_last(qkv[hp, keys, 2 * FS :], dhs)
                ds = (e.astype(f32) * (dp - inner)).astype(bf16)
                dqt = dqt + dot(kt[hp, :, keys], ds)
                if last:
                    dk[hp, keys, :] = dot(ds, qs)
                    dv[hp, keys, :] = dot(e, dhs)
                else:
                    dk[hp, keys, :] += dot(ds, qs)
                    dv[hp, keys, :] += dot(e, dhs)
            dq = jnp.where(low_half, dqt[:, :BLK].T, dqt[:, BLK:].T)
            dqkv[hp, rows, 0:FS] = (dq * HS**-0.5).astype(bf16)
            dqkv[hp, rows, FS : 2 * FS] = dk[hp, rows, :].astype(bf16)
            dqkv[hp, rows, 2 * FS :] = dv[hp, rows, :].astype(bf16)
            return carry

        lax.fori_loop(0, nh, pair, 0)
        da1 = jnp.zeros((BLK, D), f32)
        for hp in range(nh):
            da1 = da1 + dot_last(dqkv[hp, rows, :], w[hp].reshape(D, D)[:, : 3 * FS])
        hat, _, inv1 = standardize(features(x, rows).astype(f32))
        a1[rows, :] = (hat * gain1 + bias1).astype(bf16)
        q1 = da1 * gain1
        m1 = jnp.sum(q1, -1, keepdims=True) / D
        m2 = jnp.sum(q1 * hat, -1, keepdims=True) / D
        tg = dh1 + inv1 * (q1 - m1 - hat * m2)
        small[0:1, :] += jnp.sum(da1 * hat, 0, keepdims=True)
        small[1:2, :] += jnp.sum(da1, 0, keepdims=True)
        for f in range(nh):
            tgb[f, rows, :] = tg[:, f * FS : (f + 1) * FS].astype(bf16)
        mine = pltpu.make_async_copy(tgb.at[h, rows], tgf.at[h, rows], loc.at[b])
        mine.start()
        sends.append(mine)
        for k in range(nh - 1):
            peer = lax.rem(h + k + 1, nh)
            c = remote(tgb.at[peer, rows], tgf.at[h, rows], hss.at[b, k], hsr.at[b, k], zpeer[k])
            c.start()
            sends.append(c)

    def weight_grads(hp, carry):
        gi = dot_first(a1[...], dqkv[hp]).astype(bf16)
        go = dot_first(dattn[...], heads[hp]).astype(bf16)
        gw[hp] = jnp.concatenate([gi, go], 1).reshape(gw.shape[1:])
        return carry

    lax.fori_loop(0, nh, weight_grads, 0)
    for f in range(nh):
        sg[f] = small[:, f * FS : (f + 1) * FS]
    for _, far in arrive:
        for c in far:
            c.wait_send()
    for c in sends:
        c.wait()


def block_kernel(
    nd, nh, experts, count, tok, attn_in, attn_out, npar, control, og_in, win, wout,
    block_out, tgf, g_in, g_out, gsum, ssum, norm,
    wblk, pblk, x, w, p, a1, qkv, kt, vt, heads, recip, h1, es, h1b, st, h1f, stf, og, gates, mout, xz,
    act, dpre, ps, inl, inr, yin, wi, wo, py, p1s, pay, dk, dv, pad, small,
    fg, sg, dacc, gwb, wc_in, ch, wr, zs, zr, szr, sdb, sdr, sqb, sqd, sqz,
    tss, tsr, wss, wsr, dss, dsr, css, csr, pss, psr, hss, hsr, sss, ssr,
    ess, esr, xsr, xsl, xrl, xrr, isr, isl, irl, irr, yss, ysr,
    bss, bsr, vss, vsr, gss, gsr, ass, asr, cts, ctr, zss, zsr, sms, smr, sns, snr,
    qss, qsr, rss, rsr, loc, hloc, ploc, gloc, wloc, oloc
):
    n = lax.axis_index("dp")
    h = lax.axis_index("hid")
    core = lax.rem(n, 2)
    chip = lax.div(n, 2)
    chips = nd // 2
    top = nh - 1
    slots, seq = h1f.shape[0], h1f.shape[1]
    blocks = seq // BLK
    el = experts * GB
    span = GB * GROUP // slots
    per = BLK // span
    right = {"hid": jnp.minimum(h + 1, top)}
    left = {"hid": jnp.maximum(h - 1, 0)}
    zid = [lax.rem(h + k, nh) for k in range(1, nh)]
    zpeer = [{"hid": z} for z in zid]
    did = [lax.rem(n + k, nd) for k in range(1, nd)]
    cid = [lax.rem(chip + k, chips) * 2 + core for k in range(1, chips)]
    partner = {"dp": chip * 2 + 1 - core}
    ends = []
    sent = []
    gathers = []
    scatters = []
    for m in range(3):
        wblk[:, m * FS : (m + 1) * FS] = attn_in[m].astype(bf16)
    wblk[:, 3 * FS :] = attn_out[...].astype(bf16)
    pblk[0:4, :] = npar[...]
    pblk[4:8, :] = jnp.zeros((4, FS), f32)
    pblk[8:, :] = control[...]

    def local(src, dst, sem):
        c = pltpu.make_async_copy(src, dst, sem)
        c.start()
        return c

    def far(src, dst, send, recv, peer):
        c = remote(src, dst, send, recv, peer)
        c.start()
        sent.append(c)
        return c

    og_load = local(og_in, og, loc.at[0])
    x_load = local(tok.at[h], x.at[h], loc.at[1])
    w_loads = []
    for f in range(nh):
        cols = pl.ds(f * FS, FS)
        w_loads.append(local(win.at[:, cols], dk.at[f, 0:D], wloc.at[f, 0]))
        w_loads.append(local(wout.at[:, cols], dk.at[f, D : 2 * D], wloc.at[f, 1]))
    greet(zpeer + [{"dp": d} for d in did])
    w_own = local(wblk, w.at[h, chip, core], loc.at[2])
    p_own = local(pblk, p.at[h], loc.at[3])
    wz = [
        far(wblk, w.at[h, chip, core], wss.at[k], wsr.at[k], zpeer[k]) for k in range(nh - 1)
    ]
    pz = [far(pblk, p.at[h], pss.at[k], psr.at[k], zpeer[k]) for k in range(nh - 1)]

    def rows_of(b):
        return pl.ds(b * BLK, BLK)

    def send_tokens(b):
        rows = rows_of(b)
        return [
            far(tok.at[zid[k], rows], x.at[h, rows], tss.at[b, k], tsr.at[b, k], zpeer[k])
            for k in range(nh - 1)
        ]

    tz = {b: send_tokens(b) for b in range(blocks)}
    w_own.wait()
    wc = []
    for j in range(nh):
        piece = lax.rem(h - j + nh, nh)
        if j > 0:
            wz[j - 1].wait_recv()
        part = w.at[piece, chip, core]
        wc.append(
            [far(part, part, dss.at[j, k], dsr.at[j, k], {"dp": cid[k]}) for k in range(chips - 1)]
        )
    p_own.wait()
    for c in pz:
        c.wait_recv()
    controller_rows(p, pad, experts)
    gain1 = row_of(p, 0)
    bias1 = row_of(p, 1)
    gain2 = row_of(p, 2)
    bias2 = row_of(p, 3)
    scale = jnp.where(iota((BLK, 3 * FS), 1) < FS, HS**-0.5, 1.0).astype(bf16)
    lane = iota((BLK, FS), 1)
    low_half = lane < HS
    causal = iota((BLK, 2 * BLK), 0) <= (iota((BLK, 2 * BLK), 1) & (BLK - 1))
    one = jnp.ones((FS, BLK), bf16)
    low_rows = iota((FS, BLK), 0) < HS
    wp = []

    def pass_weights(j):
        for c in wc[j]:
            c.wait_recv()
        part = w.at[lax.rem(h - j + nh, nh), :, core]
        wp.append(far(part, part, css.at[j], csr.at[j], partner))

    def begin(b):
        for c in tz[b]:
            c.wait_recv()
        normed, _, _ = standardize(features(x, rows_of(b)).astype(f32))
        a1[rows_of(b), :] = (normed * gain1 + bias1).astype(bf16)

    def attend(b, hp):
        rows = rows_of(b)
        past = b * BLK
        e_ref = es[b]
        proj = dot(a1[rows, :], w[hp].reshape(D, D)[:, : 3 * FS])
        low = proj.astype(bf16) * scale
        qkv[hp, rows, :] = low
        kt[hp, :, rows] = proj[:, FS : 2 * FS].T.astype(bf16)
        vt[hp, :, rows] = proj[:, 2 * FS :].T.astype(bf16)
        q = both_heads(low[:, :FS])
        s_now = dot_last(low[:, FS : 2 * FS], q)
        s_now = jnp.where(causal, s_now, fill_value)
        peak = jnp.max(s_now, 0, keepdims=True)
        if b > 0:
            s_past = dot_last(qkv[hp, 0:past, FS : 2 * FS], q)
            peak = jnp.maximum(peak, jnp.max(s_past, 0, keepdims=True))
            e_ref[hp, 0:past, :] = jnp.exp(s_past - peak).astype(bf16)
        e_ref[hp, past : past + BLK, :] = jnp.exp(s_now - peak).astype(bf16)
        outs = []
        for half in range(2):
            total = jnp.zeros((FS, BLK), f32)
            for j in range(b + 1):
                keys = slice(j * BLK, (j + 1) * BLK)
                v = vt[hp, :, keys]
                v = jnp.where(low_rows, v, one) if half == 0 else jnp.where(low_rows, one, v)
                total = total + dot(v, e_ref[hp, keys, half * BLK : (half + 1) * BLK])
            outs.append(total.T)
        value = jnp.where(low_half, outs[0], outs[1])
        total = jnp.where(low_half, pltpu.roll(outs[0], HS, 1), pltpu.roll(outs[1], HS, 1))
        inv = 1.0 / total
        recip[hp, rows, :] = inv
        heads[hp, rows, :] = (value * inv).astype(bf16)

    def attend_loop(b, first, last):
        def body(hp, carry):
            attend(b, hp)
            return carry

        lax.fori_loop(first, last, body, 0)

    hz = {}

    def finish(b):
        rows = rows_of(b)
        attn = jnp.zeros((BLK, D), f32)
        for hp in range(nh):
            attn = attn + dot_last(heads[hp, rows, :], w[hp].reshape(D, D)[:, 3 * FS :])
        hidden = features(x, rows).astype(f32) + attn
        h1[rows, :] = hidden
        normed, center, inv = standardize(hidden)
        u = normed * gain2 + bias2
        uh, ul = split(u)
        cols = dot_last(
            jnp.concatenate([uh, ul, uh], 1),
            jnp.concatenate([pad[0], pad[0], pad[1]], 1).astype(bf16),
        )
        cols = jnp.where(lane == experts, center, jnp.where(lane == experts + 1, inv, cols))
        st[:, rows] = cols.T[0 : experts + 8, :]
        for f in range(nh):
            h1b[f, rows, :] = hidden[:, f * FS : (f + 1) * FS].astype(bf16)
        mine = [
            local(h1b.at[h, rows], h1f.at[h, rows], hloc.at[b, 0]),
            local(st.at[:, rows], stf.at[h, :, rows], hloc.at[b, 1]),
        ]
        away = []
        for k in range(nh - 1):
            away.append(
                far(h1b.at[zid[k], rows], h1f.at[h, rows], hss.at[b, k], hsr.at[b, k], zpeer[k])
            )
            away.append(
                far(st.at[:, rows], stf.at[h, :, rows], sss.at[b, k], ssr.at[b, k], zpeer[k])
            )
        hz[b] = (mine, away)

    live = count[0]
    gain = npar[2:3, :]
    bias = npar[3:4, :]
    mask = own_group(slots * span, el)

    def gate(c):
        mine, away = hz[c]
        for v in mine:
            v.wait()
        for v in away:
            v.wait_recv()

        def body(i, carry):
            rows = pl.ds(pl.multiple_of(c * BLK + i * span, span), span)
            grows = pl.ds(pl.multiple_of(i * GB, GB), GB)
            spread = expand(stf[:, :, rows], experts, el, True)
            logits = jnp.stack(
                [jnp.where(s < live, spread[s][:, :el], fill_value) for s in range(slots)]
            ).reshape(slots, GB, span // GB, el)
            peak = jnp.max(logits, axis=(0, 2), keepdims=True)
            e = jnp.exp(logits - peak)
            g = e / jnp.sum(e, axis=(0, 2), keepdims=True)
            g = jnp.where(mask, g.reshape(slots * span, el), 0.0).astype(bf16)
            gates[c * per + i] = g
            mean = [v[:, el : el + FS] for v in spread]
            inv = [v[:, el + FS :] for v in spread]
            _, u, dy, _ = block_values(h1f, og, gain, bias, live, rows, mean, inv)
            both = jnp.concatenate([jnp.concatenate(u, 0), jnp.concatenate(dy, 0)], 1)
            mixed = dot_first(g, both).astype(bf16)
            mout[c, :, 0, grows, :] = mixed[:, :FS].reshape(experts, GB, FS)
            mout[c, :, 1, grows, :] = mixed[:, FS:].reshape(experts, GB, FS)
            return carry

        lax.fori_loop(0, per, body, 0)
        ez[c] = [
            far(mout.at[c, did[k]], xz.at[c, h, n], ess.at[c, k], esr.at[c, k], {"dp": did[k]})
            for k in range(nd - 1)
        ]
        xz[c, h, n] = mout[c, n]

    ez = {}

    def go_right(c, j):
        piece = xz.at[c, jnp.maximum(h - j, 0)]
        return remote(piece, piece, xsr.at[c, j], xrl.at[c, j], right)

    def go_left(c, j):
        piece = xz.at[c, jnp.minimum(h + j, top)]
        return remote(piece, piece, xsl.at[c, j], xrr.at[c, j], left)

    def gather(c, j):
        if j < top:
            gathers.append((c, j))
        if j == 0:
            for v in ez[c]:
                v.wait_recv()

            @pl.when(h < top)
            def _():
                go_right(c, 0).start()

            @pl.when(h > 0)
            def _():
                go_left(c, 0).start()

            return

        @pl.when(h >= j)
        def _():
            go_right(c, j - 1).wait_recv()
            if j < top:

                @pl.when(h < top)
                def _():
                    go_right(c, j).start()

        @pl.when(h + j <= top)
        def _():
            go_left(c, j - 1).wait_recv()
            if j < top:

                @pl.when(h > 0)
                def _():
                    go_left(c, j).start()

    count_rows = xz.shape[2] * xz.shape[4]

    def rows_at(c, f, kind):
        return xz[c, f, :, kind].reshape(count_rows, FS)

    def expert(c):
        mixed = jnp.concatenate([rows_at(c, f, 0) for f in range(nh)], axis=1)
        drows = jnp.concatenate([rows_at(c, f, 1) for f in range(nh)], axis=1)
        pre = dot(mixed, wi[...])
        cube = 0.7978845608028654
        t = jnp.tanh(cube * (pre + 0.044715 * (pre * pre * pre)))
        a = (0.5 * pre * (1.0 + t)).astype(bf16)
        slope = 0.5 * (1.0 + t) + 0.5 * pre * (1.0 - t * t) * (
            cube * (1.0 + 3.0 * 0.044715 * (pre * pre))
        )
        act[c] = a
        rows = dot(a, wo[...])
        d = (dot_last(drows, wo[...]) * slope).astype(bf16)
        dpre[c] = d
        dmix = dot_last(d, wi[...])
        shape = (xz.shape[2], xz.shape[4], FS)
        for f in range(nh):
            ps[c, f, :, 0] = rows[:, f * FS : (f + 1) * FS].astype(bf16).reshape(shape)
            ps[c, f, :, 1] = dmix[:, f * FS : (f + 1) * FS].astype(bf16).reshape(shape)

    def sum_right(c, d, mark):
        piece = inl.at[c, jnp.minimum(h + d, top)]
        return remote(piece, piece, isr.at[c, d], irl.at[c, mark], right)

    def sum_left(c, d, mark):
        piece = inr.at[c, jnp.maximum(h - d, 0)]
        return remote(piece, piece, isl.at[c, d], irr.at[c, mark], left)

    def scatter(c, stage):
        scatters.append((c, stage))

        @pl.when(h == stage)
        def _():
            for d in reversed(range(1, nh - stage)):
                dest = stage + d
                if stage > 0:
                    sum_right(c, d, d).wait_recv()
                    value = inl[c, dest].astype(f32) + ps[c, dest].astype(f32)
                    inl[c, dest] = value.astype(bf16)
                else:
                    inl[c, dest] = ps[c, dest]
                sum_right(c, d, d - 1).start()

        @pl.when(h == top - stage)
        def _():
            for d in reversed(range(1, nh - stage)):
                dest = top - stage - d
                if stage > 0:
                    sum_left(c, d, d).wait_recv()
                    value = inr[c, dest].astype(f32) + ps[c, dest].astype(f32)
                    inr[c, dest] = value.astype(bf16)
                else:
                    inr[c, dest] = ps[c, dest]
                sum_left(c, d, d - 1).start()

    yz = {}

    def home(c):
        for v in ez[c]:
            v.wait_send()
            sent[:] = [o for o in sent if o is not v]
        @pl.when(h > 0)
        def _():
            sum_right(c, 0, 0).wait_recv()

        @pl.when(h < top)
        def _():
            sum_left(c, 0, 0).wait_recv()

        @pl.when(h == 0)
        def _():
            mout[c] = (ps[c, 0].astype(f32) + inr[c, 0].astype(f32)).astype(bf16)

        @pl.when(h == top)
        def _():
            mout[c] = (ps[c, top].astype(f32) + inl[c, top].astype(f32)).astype(bf16)

        for m in range(1, top):

            @pl.when(h == m)
            def _(m=m):
                value = ps[c, m].astype(f32) + inl[c, m].astype(f32)
                mout[c] = (value + inr[c, m].astype(f32)).astype(bf16)

        yz[c] = []
        for k in range(1, nd):
            src = lax.rem(n - k + nd, nd)
            yz[c].append(
                far(mout.at[c, src], yin.at[c, n], yss.at[c, k], ysr.at[c, k], {"dp": src})
            )
        yin[c, n] = mout[c, n]

    height = experts + 8
    srow = iota((height, el + 2 * FS), 0)
    scol = iota((height, el + 2 * FS), 1)
    target = jnp.where(scol < el, lax.shift_right_logical(scol, 4), experts)
    target = jnp.where(scol >= el + FS, experts + 1, target)
    fold = jnp.where(srow == target, 1.0, 0.0).astype(bf16)
    fold = jnp.concatenate([fold, fold], 1)
    fg[...] = jnp.zeros_like(fg)

    def back(c):
        for v in yz[c]:
            v.wait_recv()

        def body(i, carry):
            rows = pl.ds(pl.multiple_of(c * BLK + i * span, span), span)
            grows = pl.ds(pl.multiple_of(i * GB, GB), GB)
            spread = expand(stf[:, :, rows], experts, el, False)
            mean = [v[:, :FS] for v in spread]
            inv = [v[:, FS:] for v in spread]
            nhat, u, dy, hid = block_values(h1f, og, gain, bias, live, rows, mean, inv)
            y = jnp.concatenate(
                [yin[c, :, 0, grows, :].reshape(el, FS), yin[c, :, 1, grows, :].reshape(el, FS)], 1
            )
            g = gates[c * per + i]
            bd = dot(g, y)
            dgates = dot_last(
                jnp.concatenate([jnp.concatenate(dy, 0), jnp.concatenate(u, 0)], 1), y
            )
            g = g.astype(f32)
            gd = (g * dgates).reshape(slots, GB, span // GB, el)
            inner = jnp.sum(gd, axis=(0, 2), keepdims=True)
            dlog = gd - g.reshape(slots, GB, span // GB, el) * inner
            dlog = dlog.reshape(slots * span, el)
            qs, qn = [], []
            acc_gain = jnp.zeros((1, FS), f32)
            acc_bias = jnp.zeros((1, FS), f32)
            for s in range(slots):
                part = slice(s * span, (s + 1) * span)
                du = bd[part, FS:]
                h1f[s, rows, :] = jnp.where(s < live, hid[s] + bd[part, :FS], 0.0).astype(bf16)
                q = du * gain
                og[s, rows, :] = (dy[s].astype(f32) + inv[s] * q).astype(bf16)
                acc_gain = acc_gain + jnp.sum(du * nhat[s], 0, keepdims=True)
                acc_bias = acc_bias + jnp.sum(du, 0, keepdims=True)
                qs.append(q)
                qn.append(q * nhat[s])
            high, low = split(
                jnp.concatenate([dlog, jnp.concatenate(qs, 0), jnp.concatenate(qn, 0)], 1)
            )
            folded = dot_last(fold, jnp.concatenate([high, low], 1))
            for s in range(slots):
                py[s, :, rows] = folded[:, s * span : (s + 1) * span].astype(bf16)
            fg[2:3, :] += acc_gain
            fg[3:4, :] += acc_bias
            return carry

        lax.fori_loop(0, per, body, 0)
        rows = rows_of(c)
        ends.append(local(h1f.at[:, rows], block_out.at[:, rows], oloc.at[c]))

    dz = {}

    def send_back(c):
        rows = rows_of(c)
        mine = [
            local(og.at[h, rows], p1s.at[h, rows], ploc.at[c, 0]),
            local(py.at[h, :, rows], pay.at[h, :, rows], ploc.at[c, 1]),
        ]
        away = []
        for k in range(nh - 1):
            away.append(
                far(og.at[zid[k], rows], p1s.at[h, rows], bss.at[c, k], bsr.at[c, k], zpeer[k])
            )
            away.append(
                far(py.at[zid[k], :, rows], pay.at[h, :, rows], vss.at[c, k], vsr.at[c, k], zpeer[k])
            )
        dz[c] = (mine, away)

    def expert_grads():
        total = blocks * count_rows
        squares = jnp.zeros((8, FS), f32)
        a_all = act[...].reshape(total, act.shape[2])
        d_all = dpre[...].reshape(total, dpre.shape[2])
        for f in range(nh):
            gi = dot_first(xz[:, f, :, 0].reshape(total, FS), d_all)
            go = dot_first(a_all, xz[:, f, :, 1].reshape(total, FS))
            dv[f, 0:D, :] = go
            for m in range(nh):
                part = gi[:, m * FS : (m + 1) * FS]
                dv[m, D + f * FS : D + (f + 1) * FS, :] = part
                squares = squares + jnp.sum((part * part).reshape(FS // 8, 8, FS), 0)
            squares = squares + jnp.sum((go * go).reshape(D // 8, 8, FS), 0)
        sqb[0] = squares
        for f in range(nh):
            cols = pl.ds(f * FS, FS)
            grads.append(local(dv.at[f, 0:D], g_out.at[:, cols], wloc.at[f, 0]))
            grads.append(local(dv.at[f, D : 2 * D], g_in.at[:, cols], wloc.at[f, 1]))

    grads = []

    x_load.wait()
    og_load.wait()
    for v in w_loads:
        v.wait()
    for f in range(nh):
        cols = pl.ds(f * FS, FS)
        wi[:, cols] = dk[f, 0:D].astype(bf16)
        wo[:, cols] = dk[f, D : 2 * D].astype(bf16)
    pass_weights(0)
    begin(0)
    for j in range(nh):
        if j + 1 < nh:
            pass_weights(j + 1)
        wp[j].wait_recv()
        attend(0, lax.rem(h - j + nh, nh))
    finish(0)
    begin(1)
    attend_loop(1, 0, nh)
    finish(1)
    gate(0)
    begin(2)
    attend_loop(2, 0, 2)
    gather(0, 0)
    attend_loop(2, 2, nh)
    finish(2)
    gate(1)
    gather(0, 1)
    begin(3)
    attend_loop(3, 0, 2)
    gather(1, 0)
    attend_loop(3, 2, 3)
    gather(0, 2)
    attend_loop(3, 3, nh)
    gather(1, 1)
    finish(3)
    gather(0, 3)
    expert(0)
    scatter(0, 0)
    gate(2)
    gather(1, 2)
    gather(2, 0)
    scatter(0, 1)
    gather(1, 3)
    expert(1)
    scatter(1, 0)
    gather(2, 1)
    gate(3)
    scatter(0, 2)
    scatter(1, 1)
    gather(2, 2)
    gather(3, 0)
    home(0)
    scatter(1, 2)
    gather(2, 3)
    expert(2)
    scatter(2, 0)
    gather(3, 1)
    scatter(2, 1)
    home(1)
    back(0)
    gather(3, 2)
    scatter(2, 2)
    gather(3, 3)
    expert(3)
    scatter(3, 0)
    home(2)
    scatter(3, 1)
    back(1)
    scatter(3, 2)
    back(2)
    home(3)
    back(3)
    for c in reversed(range(blocks)):
        send_back(c)
    expert_grads()
    er = iota((3 * height, FS), 0)
    er = jnp.where(er >= 2 * height, er - 2 * height, er)
    er = jnp.where(er >= height, er - height, er)
    eye = jnp.where(er == iota((3 * height, FS), 1), 1.0, 0.0).astype(bf16)
    pick = iota((8, 2 * FS), 1) & (FS - 1)
    row = iota((8, 2 * FS), 0)
    pick = ((row == 0) & (pick < HS)) | ((row == 1) & (pick >= HS))
    pick = jnp.where(pick, 1.0, 0.0).astype(bf16)
    small[...] = jnp.zeros_like(small)
    for b in range(blocks):
        for v in hz[b][1]:
            v.wait_send()
            sent[:] = [c for c in sent if c is not v]
    tgb = h1b

    def arrive(b):
        rows = rows_of(b)
        mine, away = dz[b]
        for v in mine:
            v.wait()
        for v in away:
            v.wait_recv()
        total = pay[0, :, rows].astype(f32)
        for f in range(1, nh):
            total = total + pay[f, :, rows].astype(f32)
        cols = dot_first(jnp.concatenate(split3(total), 0), eye)
        s1 = cols[:, experts : experts + 1]
        s2 = cols[:, experts + 1 : experts + 2]
        nhat, _, inv = standardize(h1[rows, :])
        ch, cl = split(jnp.where(lane < experts, cols, 0.0))
        du = dot(
            jnp.concatenate([ch, cl, ch], 1),
            jnp.concatenate([pad[0], pad[0], pad[1]], 0).astype(bf16),
        )
        q = du * gain2
        mq = (s1 + jnp.sum(q, -1, keepdims=True)) / D
        mqn = (s2 + jnp.sum(q * nhat, -1, keepdims=True)) / D
        dh1 = features(p1s, rows).astype(f32) + inv * (q - mq - nhat * mqn)
        small[2:3, :] += jnp.sum(du * nhat, 0, keepdims=True)
        small[3:4, :] += jnp.sum(du, 0, keepdims=True)
        routed = dot_first(jnp.concatenate([ch, cl], 1), (nhat * gain2 + bias2).astype(bf16))
        small[8 : 8 + experts, :] += routed[0:experts] + routed[FS : FS + experts]
        act[b] = dh1.astype(bf16)
        h1[rows, :] = dh1

    def pair(b, hp):
        rows = rows_of(b)
        e_ref = es[b]
        dh = dot(act[b], w[hp].reshape(D, D)[:, 3 * FS :]).astype(bf16).astype(f32)
        dh = dh * recip[hp, rows, :]
        high, rest = split(dh * heads[hp, rows, :].astype(f32))
        inner = dot_last(pick, jnp.concatenate([high, rest], 1))
        inner = jnp.concatenate([inner[0:1], inner[1:2]], 1)
        dhs = both_heads(dh.astype(bf16))
        qs = both_heads(qkv[hp, rows, 0:FS])
        stop = (b + 1) * BLK
        e = e_ref[hp]
        dp = dot_last(qkv[hp, 0:stop, 2 * FS :], dhs)
        ds = (e.astype(f32) * (dp - inner)).astype(bf16)
        dqt = dot(kt[hp, :, 0:stop], ds)
        if b == blocks - 1:
            dk[hp] = dot(ds, qs)
            dv[hp] = dot(e, dhs)
        else:
            dk[hp, 0:stop, :] += dot(ds, qs)
            dv[hp, 0:stop, :] += dot(e, dhs)
        dq = jnp.where(low_half, dqt[:, :BLK].T, dqt[:, BLK:].T)
        qkv[hp, rows, 0:FS] = (dq * HS**-0.5).astype(bf16)
        qkv[hp, rows, FS : 2 * FS] = dk[hp, rows, :].astype(bf16)
        qkv[hp, rows, 2 * FS :] = dv[hp, rows, :].astype(bf16)

    def pairs(b, first, last):
        def body(hp, carry):
            pair(b, hp)
            return carry

        lax.fori_loop(first, last, body, 0)
        total = jnp.zeros((BLK, D), f32)
        for hp in range(first, last):
            total = total + dot_last(qkv[hp, rows_of(b), :], w[hp].reshape(D, D)[:, : 3 * FS])
        return total

    def settle(b, da1):
        rows = rows_of(b)
        hat, _, inv1 = standardize(features(x, rows).astype(f32))
        q1 = da1 * gain1
        m1 = jnp.sum(q1, -1, keepdims=True) / D
        m2 = jnp.sum(q1 * hat, -1, keepdims=True) / D
        tg = h1[rows, :] + inv1 * (q1 - m1 - hat * m2)
        small[0:1, :] += jnp.sum(da1 * hat, 0, keepdims=True)
        small[1:2, :] += jnp.sum(da1, 0, keepdims=True)
        for f in range(nh):
            tgb[f, rows, :] = tg[:, f * FS : (f + 1) * FS].astype(bf16)
        ends.append(local(tgb.at[h, rows], tgf.at[h, rows], gloc.at[b]))
        for k in range(nh - 1):
            c = remote(
                tgb.at[zid[k], rows], tgf.at[h, rows], gss.at[b, k], gsr.at[b, k], zpeer[k]
            )
            c.start()
            ends.append(c)

    ring = {}

    def weight_grads(hp):
        gi = dot_first(a1[...], qkv[hp]).astype(bf16)
        go = dot_first(act[...].reshape(seq, D), heads[hp]).astype(bf16)
        gwb[hp] = jnp.concatenate([gi, go], 1).reshape(gwb.shape[1:])
        ring[hp] = far(gwb.at[hp, :, 1 - core], wc_in.at[hp], ass.at[hp], asr.at[hp], partner)

    cnum = [lax.rem(chip + k, chips) for k in range(1, chips)]

    def over_chips(hp):
        ring[hp].wait_recv()
        ch[hp] = (gwb[hp, :, core].astype(f32) + wc_in[hp].astype(f32)).astype(bf16)
        ring[hp] = [
            far(ch.at[hp, cnum[k]], wr.at[hp, k], cts.at[hp, k], ctr.at[hp, k], {"dp": cid[k]})
            for k in range(chips - 1)
        ]

    def to_owner(hp):
        return remote(zs.at[hp], zr.at[h], zss.at[hp], zsr.at[h], {"hid": hp})

    def over_z(hp):
        for v in ring[hp]:
            v.wait_recv()
        total = ch[hp, chip].astype(f32)
        for k in range(chips - 1):
            total = total + wr[hp, k].astype(f32)
        zs[hp] = total.astype(bf16)

        @pl.when(h != hp)
        def _():
            to_owner(hp).start()

        @pl.when(h == hp)
        def _():
            zr[hp] = zs[hp]

    half = nh // 2
    for b in reversed(range(blocks)):
        arrive(b)
        if b == blocks - 1:
            for v in grads:
                v.wait()
        if b >= 2:
            settle(b, pairs(b, 0, nh))
        else:
            dacc[rows_of(b), :] = pairs(b, 0, half)
    for hp in range(half):
        weight_grads(hp)
    settle(1, dacc[rows_of(1), :] + pairs(1, half, nh))
    for hp in range(half):
        over_chips(hp)
    settle(0, dacc[rows_of(0), :] + pairs(0, half, nh))
    for hp in range(half, nh):
        weight_grads(hp)
    for hp in range(half, nh):
        over_chips(hp)
    for hp in range(half):
        over_z(hp)
    for f in range(nh):
        sg[f] = small[:, f * FS : (f + 1) * FS]
    sz = [far(sg.at[zid[k]], szr.at[k], sms.at[k], smr.at[k], zpeer[k]) for k in range(nh - 1)]
    for c in sz:
        c.wait_recv()
    part = sg[h]
    for k in range(nh - 1):
        part = part + szr[k]
    part = jnp.concatenate([part[0:8] + fg[...], part[8:]], 0)
    sdb[...] = part
    sd = [
        far(sdb, sdr.at[k], sns.at[k], snr.at[k], {"dp": did[k]}) for k in range(nd - 1)
    ]
    for hp in range(half, nh):
        over_z(hp)
    for c in sd:
        c.wait_recv()
    for k in range(nd - 1):
        part = part + sdr[k]
    ssum[...] = part
    squares = sqb[0] + jnp.where(
        n == 0, jnp.sum((part * part).reshape(part.shape[0] // 8, 8, FS), 0), 0.0
    )
    for src in range(nh):

        @pl.when(h != src)
        def _(src=src):
            remote(zs.at[src], zr.at[src], zss.at[src], zsr.at[src], {"hid": src}).wait_recv()

    block = zr[0].astype(f32)
    for src in range(1, nh):
        block = block + zr[src].astype(f32)
    gsum[...] = block
    for f in range(nh):
        part = block[:, f * FS : (f + 1) * FS]
        squares = squares + jnp.sum((part * part).reshape(part.shape[0] // 8, 8, FS), 0)
    sqb[1] = squares
    qd = [
        far(sqb.at[1], sqd.at[k], qss.at[k], qsr.at[k], {"dp": did[k]}) for k in range(nd - 1)
    ]
    for c in qd:
        c.wait_recv()
    for k in range(nd - 1):
        squares = squares + sqd[k]
    sqb[2] = squares
    qz = [far(sqb.at[2], sqz.at[k], rss.at[k], rsr.at[k], zpeer[k]) for k in range(nh - 1)]
    for c in qz:
        c.wait_recv()
    for k in range(nh - 1):
        squares = squares + sqz[k]
    everything = jnp.sum(jnp.sum(squares, 1, keepdims=True), 0, keepdims=True)
    norm[0, 0] = jnp.sqrt(everything)[0, 0]
    for c in sent:
        c.wait_send()
    for hp in range(nh):

        @pl.when(h != hp)
        def _(hp=hp):
            to_owner(hp).wait_send()

    for c, j in gathers:

        @pl.when(jnp.logical_and(h < top, h >= j))
        def _(c=c, j=j):
            go_right(c, j).wait_send()

        @pl.when(jnp.logical_and(h > 0, h + j <= top))
        def _(c=c, j=j):
            go_left(c, j).wait_send()

    for c, stage in scatters:

        @pl.when(h == stage)
        def _(c=c, stage=stage):
            for d in range(1, nh - stage):
                sum_right(c, d, d - 1).wait_send()

        @pl.when(h == top - stage)
        def _(c=c, stage=stage):
            for d in range(1, nh - stage):
                sum_left(c, d, d - 1).wait_send()

    for c in ends:
        c.wait()


def reduce_kernel(
    nd, nh, experts, gw, sg, fg, sqe, gsum, ssum, norm,
    wc, ch, own, wr, zr, zs, szr, sdr, sqd, sqz, sdb, sqb,
    css, csr, dss, dsr, zss, zsr, ass, asr, bss, bsr, qss, qsr, rss, rsr
):
    n = lax.axis_index("dp")
    h = lax.axis_index("hid")
    core = lax.rem(n, 2)
    chip = lax.div(n, 2)
    chips = nd // 2
    zid = [lax.rem(h + k, nh) for k in range(1, nh)]
    zpeer = [{"hid": z} for z in zid]
    did = [lax.rem(n + k, nd) for k in range(1, nd)]
    dpeer = [{"dp": d} for d in did]
    greet(zpeer + dpeer)
    partner = {"dp": chip * 2 + 1 - core}
    first = remote(gw.at[:, :, 1 - core], wc, css.at[0], csr.at[0], partner)
    first.start()
    sz = [remote(sg.at[zid[k]], szr.at[k], ass.at[k], asr.at[k], zpeer[k]) for k in range(nh - 1)]
    for c in sz:
        c.start()
    for c in sz:
        c.wait_recv()
    small = sg[h]
    for k in range(nh - 1):
        small = small + szr[k]
    small = jnp.concatenate([small[0:8] + fg[...], small[8:]], 0)
    sdb[...] = small
    sd = [remote(sdb, sdr.at[k], bss.at[k], bsr.at[k], dpeer[k]) for k in range(nd - 1)]
    for c in sd:
        c.start()
    first.wait_recv()
    for hp in range(nh):
        ch[hp] = (gw[hp, :, core].astype(f32) + wc[hp].astype(f32)).astype(bf16)
    cid = [lax.rem(chip + k, chips) for k in range(1, chips)]
    second = [
        remote(ch.at[:, cid[k]], wr.at[k], dss.at[k], dsr.at[k], {"dp": cid[k] * 2 + core})
        for k in range(chips - 1)
    ]
    for c in second:
        c.start()
    for c in sd:
        c.wait_recv()
    for k in range(nd - 1):
        small = small + sdr[k]
    ssum[...] = small
    for c in second:
        c.wait_recv()
    total = ch[:, chip].astype(f32)
    for k in range(chips - 1):
        total = total + wr[k].astype(f32)
    zs[...] = total.astype(bf16)
    third = [
        remote(zs.at[zid[k]], zr.at[k], zss.at[k], zsr.at[k], zpeer[k]) for k in range(nh - 1)
    ]
    for c in third:
        c.start()
    for c in third:
        c.wait_recv()
    block = zs[h].astype(f32)
    for k in range(nh - 1):
        block = block + zr[k].astype(f32)
    gsum[...] = block
    squares = sqe[...]
    for f in range(nh):
        part = block[:, f * FS : (f + 1) * FS]
        squares = squares + jnp.sum((part * part).reshape(part.shape[0] // 8, 8, FS), 0)
    both = jnp.sum((small * small).reshape(small.shape[0] // 8, 8, FS), 0)
    squares = squares + jnp.where(n == 0, both, 0.0)
    sqb[0] = squares
    qd = [remote(sqb.at[0], sqd.at[k], qss.at[k], qsr.at[k], dpeer[k]) for k in range(nd - 1)]
    for c in qd:
        c.start()
    for c in qd:
        c.wait_recv()
    for k in range(nd - 1):
        squares = squares + sqd[k]
    sqb[1] = squares
    qz = [remote(sqb.at[1], sqz.at[k], rss.at[k], rsr.at[k], zpeer[k]) for k in range(nh - 1)]
    for c in qz:
        c.start()
    for c in qz:
        c.wait_recv()
    for k in range(nh - 1):
        squares = squares + sqz[k]
    everything = jnp.sum(jnp.sum(squares, 1, keepdims=True), 0, keepdims=True)
    norm[...] = jnp.broadcast_to(jnp.sqrt(everything), norm.shape)
    for c in [first] + sz + sd + second + third + qd + qz:
        c.wait_send()


def call(kernel, cid, outs, scratch, ins, out_specs=None, limit=60, pack=None):
    shapes = [jax.ShapeDtypeStruct(s, t) for s, t in outs]
    specs = out_specs or [VM] * len(outs)
    if pack is not None:
        shapes = shapes[: pack[0]] + [shapes[pack[0] :]]
        specs = specs[: pack[0]] + [specs[pack[0] :]]
    result = pl.pallas_call(
        kernel,
        out_shape=shapes,
        in_specs=[spec for spec, _ in ins],
        out_specs=specs,
        scratch_shapes=scratch,
        compiler_params=pltpu.CompilerParams(
            collective_id=cid, has_side_effects=True, vmem_limit_bytes=limit * 2**20
        ),
    )(*[value for _, value in ins])
    if pack is not None:
        result = list(result[: pack[0]]) + list(result[pack[0]])
    return result


def adam_update(weight, grad, first, second, rate, factor):
    clipped = grad * factor
    first_new = beta_first * first + (1.0 - beta_first) * clipped
    second_new = beta_second * second + (1.0 - beta_second) * clipped * clipped
    first_hat = first_new / (1.0 - beta_first**STEP)
    second_hat = second_new / (1.0 - beta_second**STEP)
    weight_new = weight - rate * (
        first_hat / (jnp.sqrt(second_hat) + adam_epsilon) + weight_decay * weight
    )
    return (first_new, second_new, weight_new)


def update_kernel(ema_keep, experts, norm, tgf, *refs):
    big, refs = refs[:10], refs[10:]
    gsum, ssum, norms, router, proj, out = (
        refs[0], refs[1], refs[2:5], refs[5:8], refs[8:12], refs[12:16]
    )
    tokens_grad, refs = refs[16], refs[17:]
    big_out, refs = refs[:8], refs[8:]
    norms_out, router_out, proj_out, out_out = refs[0:3], refs[3:6], refs[6:10], refs[10:14]
    value = jnp.full((1, 1), norm[0, 0], f32)
    factor = jnp.minimum(1.0, clip_limit / value)
    rates = (2.5 * (D // GROUP) ** (-0.5), 0.5 * H ** (-0.5))
    tokens_grad[...] = tgf[...].astype(f32)

    def store(outs, new, average):
        outs[0][...] = new[0]
        outs[1][...] = new[1]
        outs[2][...] = new[2]
        if average is not None:
            outs[3][...] = ema_keep * average + (1.0 - ema_keep) * new[2]

    for k in range(2):
        g, w, m, v, average = big[5 * k : 5 * k + 5]
        new = adam_update(w[...], g[...], m[...], v[...], rates[k], factor)
        store(big_out[4 * k : 4 * k + 4], new, average[...])

    @pl.when(pl.program_id(0) == 0)
    def _():
        new = adam_update(norms[0][...], ssum[0:4, :], norms[1][...], norms[2][...], 0.6, factor)
        store(norms_out, new, None)
        new = adam_update(
            router[0][...],
            ssum[8 : 8 + experts, :],
            router[1][...],
            router[2][...],
            (4 * D) ** (-0.5),
            factor,
        )
        store(router_out, new, None)
        for c in range(3):
            new = adam_update(
                proj[0][c],
                gsum[:, c * FS : (c + 1) * FS],
                proj[1][c],
                proj[2][c],
                0.5 * D ** (-0.5),
                factor,
            )
            store([o.at[c] for o in proj_out], new, proj[3][c])
        new = adam_update(
            out[0][...],
            gsum[:, 3 * FS :],
            out[1][...],
            out[2][...],
            0.5 * (HEADS * HS // 16) ** (-0.5),
            factor,
        )
        store(out_out, new, out[3][...])


def shards(
    tokens,
    seq_count,
    out_grad,
    norm_params,
    norm_first,
    norm_second,
    controller_weight,
    router_first,
    router_second,
    attn_in,
    attn_in_first,
    attn_in_second,
    attn_in_average,
    attn_out,
    attn_out_first,
    attn_out_second,
    attn_out_average,
    expert_in,
    expert_in_first,
    expert_in_second,
    expert_in_average,
    expert_out,
    expert_out_first,
    expert_out_second,
    expert_out_average,
):
    ema_keep = (1.0 + STEP) / (10.0 + STEP)
    nd = lax.axis_size("dp")
    nh = lax.axis_size("hid")
    chips = nd // 2
    slots, seq, _ = tokens.shape
    experts = controller_weight.shape[1]
    r = attn_in.shape[0]
    el = experts * GB
    groups = seq * slots // GROUP
    blocks = seq // BLK
    hidden = expert_in.shape[2]
    er = 8 + experts
    z3 = nh - 1

    etypes = [((nh, (b + 1) * BLK, 2 * BLK), bf16) for b in range(blocks)]
    slices = ((nh, seq, FS), bf16)
    wtype = ((nh, chips, 2, r, D), bf16)
    qtype = ((nh, seq, 3 * FS), bf16)
    ttype = ((nh, FS, seq), bf16)
    rtype = ((nh, seq, FS), f32)
    htype = ((seq, D), f32)
    stype = ((nh, er, seq), f32)
    ptype = ((nh, er, FS), f32)
    ytype = ((nd, 2, groups, FS), bf16)
    gtype = ((groups // GB, GB * GROUP, el), bf16)

    def vmem(*types):
        return [pltpu.VMEM(*t) for t in types]

    share = groups // blocks
    xtype = ((blocks, nh, nd, 2, share, FS), bf16)
    if nd * share == BLK and blocks == 4 and slots == nh and hidden == D:
        block_out, tgf, g_in, g_out, gsum, ssum, norm = call(
            functools.partial(block_kernel, nd, nh, experts),
            5,
            [
                slices,
                slices,
                ((D, hidden), f32),
                ((hidden, D), f32),
                ((r, D), f32),
                ((er, FS), f32),
                ((1, 1), f32),
            ],
            vmem(((r, D), bf16), ((er, FS), f32))
            + vmem(slices, wtype, ptype, ((seq, D), bf16), qtype, ttype, ttype, slices, rtype, htype)
            + [vmem(*etypes)]
            + vmem(
                slices,
                ((er, seq), f32),
                slices,
                stype,
                slices,
                gtype,
                ((blocks, experts, 2, share, FS), bf16),
                xtype,
                ((blocks, nd * share, hidden), bf16),
                ((blocks, nd * share, hidden), bf16),
                xtype,
                xtype,
                xtype,
                ((blocks, nd, 2, share, FS), bf16),
                ((D, hidden), bf16),
                ((hidden, D), bf16),
                ((nh, er, seq), bf16),
                slices,
                ((nh, er, seq), bf16),
                rtype,
                rtype,
                ((2, FS, D), f32),
                ((er, D), f32),
                ((8, FS), f32),
                ptype,
                htype,
                wtype,
                ((nh, chips, r, D), bf16),
                ((nh, chips, r, D), bf16),
                ((nh, chips - 1, r, D), bf16),
                ((nh, r, D), bf16),
                ((nh, r, D), bf16),
                ((z3, er, FS), f32),
                ((er, FS), f32),
                ((nd - 1, er, FS), f32),
                ((3, 8, FS), f32),
                ((nd - 1, 8, FS), f32),
                ((z3, 8, FS), f32),
            )
            + [DMA((blocks, z3))] * 2
            + [DMA((z3,))] * 2
            + [DMA((nh, chips - 1))] * 2
            + [DMA((nh,))] * 2
            + [DMA((z3,))] * 2
            + [DMA((blocks, z3))] * 4
            + [DMA((blocks, nd - 1))] * 2
            + [DMA((blocks, z3))] * 4
            + [DMA((blocks, nh))] * 4
            + [DMA((blocks, nd))] * 2
            + [DMA((blocks, z3))] * 6
            + [DMA((nh,))] * 2
            + [DMA((nh, chips - 1))] * 2
            + [DMA((nh,))] * 2
            + [DMA((z3,))] * 2
            + [DMA((nd - 1,))] * 4
            + [DMA((z3,))] * 2
            + [DMA((4,)), DMA((blocks, 2)), DMA((blocks, 2)), DMA((blocks,))]
            + [DMA((nh, 2)), DMA((blocks,))],
            [
                (SM, seq_count),
                (HB, tokens),
                (VM, attn_in.transpose(1, 0, 2)),
                (VM, attn_out),
                (VM, norm_params),
                (VM, controller_weight.T),
                (HB, out_grad),
                (HB, expert_in[0]),
                (HB, expert_out[0]),
            ],
            [HB, VM, HB, HB, VM, VM, SM],
        )
    else:
        wblk = jnp.concatenate([attn_in.reshape(r, 3 * FS), attn_out], 1).astype(bf16)
        pblk = jnp.concatenate([norm_params, jnp.zeros((4, FS), f32), controller_weight.T], 0)
        x, w, p, qkv, kt, heads, recip, h1, h1f, stf, *es = call(
            functools.partial(forward_kernel, nd, nh, experts),
            1,
            [slices, wtype, ptype, qtype, ttype, slices, rtype, htype, slices, stype] + etypes,
            vmem(slices, wtype, qtype, ttype, slices, rtype, htype)
            + vmem(((BLK, D), bf16), ttype)
            + [vmem(*etypes)]
            + vmem(slices, ((er, seq), f32), ((2, FS, D), f32))
            + [DMA((blocks, z3))] * 2
            + [DMA((z3,))] * 2
            + [DMA((nh, chips - 1))] * 2
            + [DMA((1,))] * 2
            + [DMA((z3,))] * 2
            + [DMA((blocks, z3))] * 4
            + [DMA((4,)), DMA((blocks, 6)), DMA((blocks, 2)), DMA((blocks,))],
            [(VM, tokens), (VM, wblk), (VM, pblk)],
            [HB, HB, VM, HB, HB, HB, HB, HB, VM, VM] + [HB] * blocks,
            pack=(10, blocks),
        )
        gates, yin, g_in, g_out, sqe = call(
            functools.partial(expert_kernel, nd, nh, experts),
            2,
            [gtype, ytype, ((D, hidden), f32), ((hidden, D), f32), ((8, FS), f32)],
            vmem(
                ytype,
                ((nh, nd, 2, groups, FS), bf16),
                ((nd, groups, hidden), bf16),
                ((nd, groups, hidden), bf16),
                ((nh, nh, 2, groups, FS), bf16),
                ((nd, nh, 2, groups, FS), bf16),
                ((nd, nh, 2, groups, FS), bf16),
                ytype,
                ((2, D, D), f32),
                ((D, hidden), bf16),
                ((hidden, D), bf16),
            )
            + [DMA((nd,))] * 2
            + [DMA((nd, z3))] * 4
            + [DMA((nd, nh))] * 4
            + [DMA((nd,))] * 2
            + [DMA((4,))],
            [
                (SM, seq_count),
                (VM, h1f),
                (VM, stf),
                (VM, out_grad),
                (VM, norm_params),
                (HB, expert_in[0]),
                (HB, expert_out[0]),
            ],
        )
        block_out, fg, tgf, gw, sg = call(
            functools.partial(backward_kernel, nh, experts),
            3,
            [slices, ((8, FS), f32), slices, wtype, ptype],
            vmem(slices, stype, slices, stype)
            + vmem(slices, wtype, qtype, ttype, slices, rtype, htype)
            + vmem(
                ((seq, D), bf16),
                rtype,
                rtype,
                qtype,
                ((seq, D), bf16),
                slices,
                ((2, FS, D), f32),
                ((er, D), f32),
            )
            + [vmem(*etypes)]
            + [DMA((blocks, z3))] * 6
            + [DMA((blocks,)), DMA((blocks, 2)), DMA((7,)), DMA((blocks,))],
            [(SM, seq_count)]
            + [(VM, v) for v in (h1f, stf, out_grad, norm_params, gates, yin, p)]
            + [(HB, v) for v in (x, w, qkv, kt, heads, recip, h1)]
            + [([HB] * blocks, list(es))],
        )
        gsum, ssum, norm = call(
            functools.partial(reduce_kernel, nd, nh, experts),
            4,
            [((r, D), f32), ((er, FS), f32), ((8, FS), f32)],
            [
                pltpu.VMEM((nh, chips, r, D), bf16),
                pltpu.VMEM((nh, chips, r, D), bf16),
                pltpu.VMEM((8, FS), f32),
                pltpu.VMEM((chips - 1, nh, r, D), bf16),
                pltpu.VMEM((z3, r, D), bf16),
                pltpu.VMEM((nh, r, D), bf16),
                pltpu.VMEM((z3, er, FS), f32),
                pltpu.VMEM((nd - 1, er, FS), f32),
                pltpu.VMEM((nd - 1, 8, FS), f32),
                pltpu.VMEM((z3, 8, FS), f32),
                pltpu.VMEM((er, FS), f32),
                pltpu.VMEM((2, 8, FS), f32),
            ]
            + [DMA((1,))] * 2
            + [DMA((chips - 1,))] * 2
            + [DMA((z3,))] * 4
            + [DMA((nd - 1,))] * 4
            + [DMA((z3,))] * 2,
            [(VM, gw), (VM, sg), (VM, fg), (VM, sqe)],
        )
    grad_norm = norm[0:1, 0:1].reshape(())
    steps = 4
    rowsz = D // steps
    wide = pl.BlockSpec((rowsz, hidden), lambda i: (i, 0))
    tall = pl.BlockSpec((hidden // steps, D), lambda i: (i, 0))
    tspec = pl.BlockSpec((slots, seq // steps, FS), lambda i: (0, i, 0))

    def whole(value):
        return pl.BlockSpec(value.shape, lambda i, rank=value.ndim: (0,) * rank)

    flip = (1, 0, 2)
    smalls = [gsum, ssum, norm_params, norm_first, norm_second]
    smalls += [controller_weight.T, router_first.T, router_second.T]
    smalls += [
        v.transpose(flip) for v in (attn_in, attn_in_first, attn_in_second, attn_in_average)
    ]
    smalls += [attn_out, attn_out_first, attn_out_second, attn_out_average]
    like = [norm_params] * 3 + [smalls[5]] * 3 + [smalls[8]] * 4 + [attn_out] * 4
    news = pl.pallas_call(
        functools.partial(update_kernel, ema_keep, experts),
        grid=(steps,),
        out_shape=[jax.ShapeDtypeStruct((slots, seq, FS), f32)]
        + [jax.ShapeDtypeStruct((D, hidden), f32)] * 4
        + [jax.ShapeDtypeStruct((hidden, D), f32)] * 4
        + [jax.ShapeDtypeStruct(v.shape, f32) for v in like],
        in_specs=[SM, tspec] + [wide] * 5 + [tall] * 5 + [whole(v) for v in smalls],
        out_specs=[tspec] + [wide] * 4 + [tall] * 4 + [whole(v) for v in like],
        compiler_params=pltpu.CompilerParams(vmem_limit_bytes=60 * 2**20),
    )(
        norm[0:1, 0:1],
        tgf,
        g_in,
        expert_in[0],
        expert_in_first[0],
        expert_in_second[0],
        expert_in_average[0],
        g_out,
        expert_out[0],
        expert_out_first[0],
        expert_out_second[0],
        expert_out_average[0],
        *smalls,
    )
    return (
        block_out,
        news[0],
        grad_norm,
        *news[9:12],
        *[v.T for v in news[12:15]],
        *[v.transpose(flip) for v in news[15:19]],
        *news[19:23],
        *[v[None] for v in news[1:9]],
    )


def solution(mesh):
    return jax.shard_map(
        shards,
        mesh=mesh,
        in_specs=(
            P("dp", None, "hid"),
            P("dp"),
            P("dp", None, "hid"),
            P(None, "hid"),
            P(None, "hid"),
            P(None, "hid"),
            P("hid", None),
            P("hid", None),
            P("hid", None),
            P("dp", None, "hid"),
            P("dp", None, "hid"),
            P("dp", None, "hid"),
            P("dp", None, "hid"),
            P("dp", "hid"),
            P("dp", "hid"),
            P("dp", "hid"),
            P("dp", "hid"),
            P("dp", None, "hid"),
            P("dp", None, "hid"),
            P("dp", None, "hid"),
            P("dp", None, "hid"),
            P("dp", "hid", None),
            P("dp", "hid", None),
            P("dp", "hid", None),
            P("dp", "hid", None),
        ),
        out_specs=(
            P("dp", None, "hid"),
            P("dp", None, "hid"),
            P(),
            P(None, "hid"),
            P(None, "hid"),
            P(None, "hid"),
            P("hid", None),
            P("hid", None),
            P("hid", None),
            P("dp", None, "hid"),
            P("dp", None, "hid"),
            P("dp", None, "hid"),
            P("dp", None, "hid"),
            P("dp", "hid"),
            P("dp", "hid"),
            P("dp", "hid"),
            P("dp", "hid"),
            P("dp", None, "hid"),
            P("dp", None, "hid"),
            P("dp", None, "hid"),
            P("dp", None, "hid"),
            P("dp", "hid", None),
            P("dp", "hid", None),
            P("dp", "hid", None),
            P("dp", "hid", None),
        ),
        check_vma=False,
    )
```
